128 devices in a mesh: dp: 16 (over y_lo, z, core), tensor: 8 (over y_hi, x).
Axes of the slice: x: 4, y: 4 (y_hi: 2, y_lo: 2; y = y_hi * 2 + y_lo), z: 4, core: 2. Of those that a mesh axis runs over, the one named last changes fastest.
Arguments:
- resid: bfloat16 [2048, 4096], P('dp'), may hold values from -22 to 22
- teacher_mixed: bfloat16 [2048, 4096], P('dp'), may hold values from -6 to 6
- gain_mix: float32 [4096], replicated, may hold values from 0.5 to 1.5
- gain_mlp: float32 [4096], replicated, may hold values from 0.5 to 1.5
- w_c: bfloat16 [4096, 4096], P(None, 'tensor'), may hold values from -0.09375 to 0.09375
- w_b: bfloat16 [4096, 1024], P(None, 'tensor'), may hold values from -0.0078125 to 0.0078125
- w_x: bfloat16 [4096, 1024], P(None, 'tensor'), may hold values from -0.09375 to 0.09375
- w_dt: bfloat16 [4096, 32], P(None, 'tensor'), may hold values from -0.09375 to 0.09375
- dt_bias: float32 [32], P('tensor'), may hold values from -2 to 1
- decay_rate: float32 [32], P('tensor'), may hold values from 9.765625e-05 to 0.05
- skip: float32 [32], P('tensor'), may hold values from 0.5 to 1.5
- w_out: bfloat16 [4096, 4096], P('tensor'), may hold values from -0.0234375 to 0.0234375
- w_gate: bfloat16 [4096, 14336], P('dp', 'tensor'), may hold values from -0.09375 to 0.09375
- w_up: bfloat16 [4096, 14336], P('dp', 'tensor'), may hold values from -0.09375 to 0.09375
Outputs:
- grad_c: float32 [4096, 4096], P('dp', 'tensor')
- grad_b: float32 [4096, 1024], P('dp', 'tensor')
- grad_x: float32 [4096, 1024], P('dp', 'tensor')
- grad_dt: float32 [4096, 32], P('dp', 'tensor')
The draws below stay inside these ranges and needn't reach their ends.
All inputs are finite; a program needn't handle non-finite values.
Results may differ from the reference program's by a relative error of at most 0.035.
Values may be sent and summed in bfloat16 or wider, within the bound.
A program may use at most 128 MiB of HBM per device.

```python
import math
import jax
import jax.numpy as jnp
from jax import lax

D = 4096
FF = 14336
HEADS = 32
GROUPS = 8
HEAD = 128
STATE = 128
TOK_DEV = 128
LENGTH = 2048


def draw_resid(key, part):
    key = jax.random.fold_in(key, 11)
    base_key, rough_key = jax.random.split(key)
    position = jnp.arange(D, dtype=jnp.float32) / (D - 1)
    lowest = 0.5
    highest = 2.5
    base = jnp.clip(jax.random.normal(base_key, (LENGTH, D), jnp.float32), -6.0, 6.0)
    rough = jnp.exp(jax.random.uniform(rough_key, (D,), jnp.float32, -0.35, 0.35))
    scale = lowest * jnp.exp(position * jnp.log(highest / lowest)) * rough
    return (base * scale[None, :]).astype(jnp.bfloat16)


def level_of(own_key, dims, cuts, smallest, high):
    level, own = 1.0, jax.random.fold_in(own_key, 6)
    for dim, shards_of in cuts:
        draws = jnp.exp(jax.random.uniform(jax.random.fold_in(own, dim), (shards_of,), jnp.float32, smallest / len(cuts), high / len(cuts)))
        level = level * jnp.repeat(draws, dims[dim] // shards_of).reshape([-1 if axis == dim else 1 for axis in range(len(dims))])
    return level


def normal_values(stream_key, extent, deviation, limit, cuts=(), kind=jnp.bfloat16):
    array = jax.random.normal(stream_key, extent, jnp.float32) * deviation
    if len(cuts) > 0:
        array = level_of(stream_key, extent, cuts, -0.22, 0.18) * array
    return jnp.clip(array, min=-limit, max=limit).astype(kind)


def setup_inputs(seed: int = 0) -> dict:
    arg_keys = jax.random.split(jax.random.key(seed), 15)
    resid = draw_resid(jax.random.fold_in(arg_keys[14], 71), 0)
    teacher_mixed = normal_values(arg_keys[1], (LENGTH, D), 1.0, 6.0, ((0, 16),))
    gain_mix = jnp.clip(1.0 + 0.1 * jax.random.normal(arg_keys[2], (D,), jnp.float32), 0.5, 1.5)
    gain_mlp = jnp.clip(1.0 + 0.1 * jax.random.normal(arg_keys[3], (D,), jnp.float32), 0.5, 1.5)
    w_c = normal_values(arg_keys[4], (D, HEADS * STATE), D ** -0.5, 0.09375, ((1, 8),))
    w_b = normal_values(arg_keys[5], (D, GROUPS * STATE), (D * STATE) ** -0.5, 0.0078125, ((1, 8),))
    w_x = normal_values(arg_keys[6], (D, GROUPS * HEAD), D ** -0.5, 0.09375, ((1, 8),))
    w_dt = normal_values(arg_keys[7], (D, HEADS), D ** -0.5, 0.09375, ((1, 8),))
    dt_bias = jnp.clip(-2.0 + 3.0 * jax.random.uniform(arg_keys[8], (HEADS,), jnp.float32) ** level_of(arg_keys[8], (HEADS,), ((0, 8),), -0.2, 0.2), -2.0, 1.0)
    decay_rate = jnp.clip(jnp.exp(math.log(0.05) - 6.2383246 * jax.random.uniform(arg_keys[9], (HEADS,), jnp.float32) ** level_of(arg_keys[9], (HEADS,), ((0, 8),), -0.2, 0.2)), 9.765625145519152e-05, 0.05)
    skip = jnp.clip(0.5 + 1.0 * jax.random.uniform(arg_keys[10], (HEADS,), jnp.float32) ** level_of(arg_keys[10], (HEADS,), ((0, 8),), -0.2, 0.2), 0.5, 1.5)
    w_out = normal_values(arg_keys[11], (HEADS * HEAD, D), (HEADS * HEAD * 16) ** -0.5, 0.0234375, ((0, 8),))
    w_gate = normal_values(arg_keys[12], (D, FF), D ** -0.5, 0.09375, ((0, 16), (1, 8)))
    w_up = normal_values(arg_keys[13], (D, FF), D ** -0.5, 0.09375, ((0, 16), (1, 8)))
    return dict(resid=resid, teacher_mixed=teacher_mixed, gain_mix=gain_mix, gain_mlp=gain_mlp, w_c=w_c, w_b=w_b, w_x=w_x, w_dt=w_dt, dt_bias=dt_bias, decay_rate=decay_rate, skip=skip, w_out=w_out, w_gate=w_gate, w_up=w_up)


EPS = 1e-05
HIGH_ACCURACY = lax.Precision.HIGHEST

def norm_rows(rows, gain):
    scale = lax.rsqrt(lax.optimization_barrier(jnp.mean(rows * rows, axis=-1, keepdims=True)) + EPS)
    return (rows * scale * gain, scale)

def local_scan(state_readout, input_injection, value_rows, raw_step, bias, rate, retained_mask):
    step_size = jax.nn.softplus(raw_step + bias)
    log_decay = jnp.cumsum(-step_size * rate, axis=0)
    score_matrix = jnp.einsum('mkfb,wkb->kfmw', state_readout, input_injection, precision=HIGH_ACCURACY)
    ordered = jnp.transpose(log_decay, (1, 2, 0))
    spread = ordered[:, :, :, None] - ordered[:, :, None, :]
    length = state_readout.shape[0]
    causal = jnp.arange(length)[:, None] >= jnp.arange(length)[None, :]
    weight_table = jnp.exp(jnp.where(causal, spread, -jnp.inf)) * score_matrix * jnp.transpose(step_size, (1, 2, 0))[:, :, None, :]
    mixer_result = jnp.einsum('djeh,hda->edja', weight_table, value_rows, precision=HIGH_ACCURACY) + retained_mask[None, :, :, None] * value_rows[:, :, None, :]
    tail_weight = jnp.exp(log_decay[-1][None] - log_decay) * step_size
    carried = jnp.einsum('tgr,tgn,tgp->grnp', tail_weight, input_injection, value_rows, precision=HIGH_ACCURACY)
    return (mixer_result, carried, log_decay)

def enter_state(state_readout, log_decay, state):
    return jnp.exp(log_decay)[..., None] * jnp.einsum('tgrn,grnp->tgrp', state_readout, state, precision=HIGH_ACCURACY)

def sequence_mixer(state_readout, input_injection, value_rows, raw_step, bias, rate, retained_mask):
    length, groups, ratio, state_size = state_readout.shape
    head_size = value_rows.shape[2]
    blocks = length // TOK_DEV

    def advance(state, pieces):
        read_block, inject_block, value_block, raw_block = pieces
        mixer_result, carried, log_decay = local_scan(read_block, inject_block, value_block, raw_block, bias, rate, retained_mask)
        mixer_result = mixer_result + enter_state(read_block, log_decay, state)
        state = jnp.exp(log_decay[-1])[:, :, None, None] * state + carried
        return (state, mixer_result)
    start = jnp.zeros((groups, ratio, state_size, head_size), jnp.float32)
    pieces = (state_readout.reshape(blocks, TOK_DEV, groups, ratio, state_size), input_injection.reshape(blocks, TOK_DEV, groups, state_size), value_rows.reshape(blocks, TOK_DEV, groups, head_size), raw_step.reshape(blocks, TOK_DEV, groups, ratio))
    _, mixer_result = lax.scan(advance, start, pieces)
    return mixer_result.reshape(length, groups, ratio, head_size)

def block_grads(normed_in, deltas):
    length, width = normed_in.shape
    blocks = length // TOK_DEV
    rows = normed_in.reshape(blocks, TOK_DEV, width)
    pieces = tuple((delta.reshape(blocks, TOK_DEV, delta.shape[1]) for delta in deltas))

    def accumulate(totals, items):
        block_rows, block_deltas = items
        fresh = []
        for total, delta in zip(totals, block_deltas):
            term = jnp.dot(block_rows.T, delta, preferred_element_type=jnp.float32).astype(jnp.bfloat16)
            fresh.append(total + lax.optimization_barrier(term).astype(jnp.float32))
        return (tuple(fresh), None)
    start = tuple((jnp.zeros((width, delta.shape[1]), jnp.float32) for delta in deltas))
    totals, _ = lax.scan(accumulate, start, (rows, pieces))
    return totals

def reference(resid, teacher_mixed, gain_mix, gain_mlp, w_c, w_b, w_x, w_dt, dt_bias, decay_rate, skip, w_out, w_gate, w_up):
    length = resid.shape[0]
    groups = GROUPS
    ratio = HEADS // GROUPS
    normed, _ = norm_rows(resid.astype(jnp.float32), gain_mix)
    normed_in = normed.astype(jnp.bfloat16)
    state_readout = jnp.dot(normed_in, w_c, preferred_element_type=jnp.float32).reshape(length, groups, ratio, STATE)
    input_injection = jnp.dot(normed_in, w_b, preferred_element_type=jnp.float32).reshape(length, groups, STATE)
    value_rows = jnp.dot(normed_in, w_x, preferred_element_type=jnp.float32).reshape(length, groups, HEAD)
    raw_step = jnp.dot(normed_in, w_dt, preferred_element_type=jnp.float32).reshape(length, groups, ratio)
    bias = dt_bias.reshape(groups, ratio)
    rate = decay_rate.reshape(groups, ratio)
    retained_mask = skip.reshape(groups, ratio)

    def mixer_of(read_part, inject_part, value_part, raw_part):
        return sequence_mixer(read_part, inject_part, value_part, raw_part, bias, rate, retained_mask)
    mixer_result, pullback = jax.vjp(mixer_of, state_readout, input_injection, value_rows, raw_step)
    mixer_out = mixer_result.reshape(length, HEADS * HEAD).astype(jnp.bfloat16)
    stream = resid.astype(jnp.float32) + jnp.dot(mixer_out, w_out, preferred_element_type=jnp.float32)
    normed_mid, scale_mid = norm_rows(stream, gain_mlp)
    normed_mid = normed_mid.astype(jnp.bfloat16)
    gate = jnp.dot(normed_mid, w_gate, preferred_element_type=jnp.float32)
    up = jnp.dot(normed_mid, w_up, preferred_element_type=jnp.float32)
    student = jax.nn.silu(gate) * up
    teacher_normed, _ = norm_rows(teacher_mixed.astype(jnp.float32), gain_mlp)
    teacher_in = teacher_normed.astype(jnp.bfloat16)
    target = jax.nn.silu(jnp.dot(teacher_in, w_gate, preferred_element_type=jnp.float32)) * jnp.dot(teacher_in, w_up, preferred_element_type=jnp.float32)
    hidden_grad = 2.0 / math.sqrt(FF) * (student - target)
    sigma = jax.nn.sigmoid(gate)
    gate_grad = (hidden_grad * up * sigma * (1.0 + gate * (1.0 - sigma))).astype(jnp.bfloat16)
    up_grad = (hidden_grad * gate * sigma).astype(jnp.bfloat16)
    mid_grad = jnp.dot(gate_grad, w_gate.T, preferred_element_type=jnp.float32) + jnp.dot(up_grad, w_up.T, preferred_element_type=jnp.float32)
    gained = mid_grad * gain_mlp
    stream_grad = scale_mid * gained - stream * scale_mid ** 3 * lax.optimization_barrier(jnp.mean(gained * stream, axis=-1, keepdims=True))
    stream_grad = stream_grad.astype(jnp.bfloat16)
    out_grad = jnp.dot(stream_grad, w_out.T, preferred_element_type=jnp.float32).reshape(length, groups, ratio, HEAD)
    read_grad, inject_grad, value_grad, step_grad = pullback(out_grad)
    deltas = (read_grad.reshape(length, HEADS * STATE).astype(jnp.bfloat16), inject_grad.reshape(length, GROUPS * STATE).astype(jnp.bfloat16), value_grad.reshape(length, GROUPS * HEAD).astype(jnp.bfloat16), step_grad.reshape(length, HEADS).astype(jnp.bfloat16))
    grad_c, grad_b, grad_x, grad_dt = block_grads(normed_in, deltas)
    return (grad_c, grad_b, grad_x, grad_dt)
```

```python
import functools
import math

import jax
import jax.numpy as jnp
from jax import lax
from jax.experimental import pallas as pl
from jax.experimental.pallas import tpu as pltpu
from jax.sharding import PartitionSpec as P

D = 4096
FF = 14336
EPS = 1e-05
T = 128
HEADS = 4
DP = 16
TP = 8
HID = 1792
ROWS = 256
WIDTH = 512
PACK = 896
F32 = jnp.float32
BF16 = jnp.bfloat16
MESH = pl.DeviceIdType.MESH
MIB = 1024 * 1024

LEGS = {
    "RO": ("R", 0, 0, "full", 0, -1),
    "LO": ("L", 0, 0, "full", 0, 1),
    "YO": ("Y", 0, 0, "full", 1, 0),
    "RQ": ("R", 1, 0, "Q", 1, -1),
    "LQ": ("L", 1, 0, "Q", 1, 1),
    "RA": ("R", 0, -1, "A", 0, 2),
    "LB": ("L", 0, 1, "B", 0, 2),
    "YL": ("Y", 0, -1, "P", 1, -1),
    "YR": ("Y", 0, 1, "P", 1, 1),
    "RQA": ("R", 1, -1, "QA", 1, 2),
    "LQB": ("L", 1, 1, "QB", 1, 2),
    "YO2": ("Y", 0, 2, "P", 1, 2),
}
ORDER = list(LEGS)
NSEM = 2 * len(ORDER) + 1


def place():
    me = lax.axis_index("dp")
    return me, me // 8, (me % 8) // 2, me % 2


def barrier_all(axis, size):
    me = lax.axis_index(axis)
    sem = pltpu.get_barrier_semaphore()
    for k in range(1, size):
        pl.semaphore_signal(
            sem, inc=1, device_id={axis: (me + k) % size}, device_id_type=MESH
        )
    pl.semaphore_wait(sem, size - 1)


class Gather:
    def __init__(self, piece, rows, p, qa, send, recv):
        self.piece, self.send, self.recv = piece, send, recv
        self.me, self.y, self.z, self.c = place()
        half = rows // 2
        self.rows = {
            "full": (0, rows),
            "P": (0, p),
            "Q": (p, rows - p),
            "A": (0, half),
            "B": (half, rows - half),
            "QA": (p, qa),
            "QB": (p + qa, rows - p - qa),
        }

    def block(self, flip, dz, core):
        y = (1 - self.y) if flip else self.y
        return y * 8 + ((self.z + dz + 4) % 4) * 2 + core

    def target(self, name):
        if name == "R":
            return self.block(0, 1, self.c)
        if name == "L":
            return self.block(0, -1, self.c)
        if name == "Y":
            return self.block(1, 0, self.c)
        return self.block(0, 0, 1 - self.c)

    def copy(self, ref, sem, to):
        return pltpu.make_async_remote_copy(
            src_ref=ref,
            dst_ref=ref,
            send_sem=self.send.at[sem],
            recv_sem=self.recv.at[sem],
            device_id={"dp": to},
            device_id_type=MESH,
        )

    def leg(self, name):
        to, flip, dz, rows, _, _ = LEGS[name]
        ref = self.piece(self.block(flip, dz, self.c), *self.rows[rows])
        return self.copy(ref, ORDER.index(name), self.target(to))

    def landed(self, name):
        to, _, _, rows, flip, dz = LEGS[name]
        ref = self.piece(self.block(flip, dz, self.c), *self.rows[rows])
        return self.copy(ref, ORDER.index(name), self.target(to))

    def side(self, name, core):
        if name == "own":
            flip, dz, rows, sem = 0, 0, "full", len(ORDER)
        else:
            _, _, _, rows, flip, dz = LEGS[name]
            sem = len(ORDER) + 1 + ORDER.index(name)
        ref = self.piece(self.block(flip, dz, core), *self.rows[rows])
        return self.copy(ref, sem, self.target("S"))

    def begin(self):
        for name in ("RO", "LO", "YO"):
            self.leg(name).start()
        self.side("own", self.c).start()

    def arrive(self, name, *then):
        self.landed(name).wait_recv()
        for other in then:
            self.leg(other).start()
        self.side(name, self.c).start()

    def side_arrive(self, *names):
        for name in names:
            self.side(name, 1 - self.c).wait_recv()

    def finish(self):
        for name in ORDER:
            self.leg(name).wait_send()
        for name in ["own"] + ORDER:
            self.side(name, self.c).wait_send()


def run_gather(g, use):
    g.arrive("YO", "RQ", "LQ")
    g.arrive("RO", "RA", "YL")
    g.arrive("LO", "LB", "YR")
    g.side_arrive("own")
    use(0, 0)
    g.side_arrive("YO")
    use(1, 0)
    g.arrive("RQ", "RQA")
    g.arrive("LQ", "LQB")
    g.arrive("RA", "YO2")
    g.arrive("LB")
    g.side_arrive("RO")
    use(0, -1)
    g.arrive("YL")
    g.arrive("YR")
    g.side_arrive("LO")
    use(0, 1)
    g.arrive("RQA")
    g.arrive("LQB")
    g.arrive("YO2")
    g.side_arrive("RA", "LB")
    use(0, 2)
    g.side_arrive("RQ", "YL")
    use(1, -1)
    g.side_arrive("LQ", "YR")
    use(1, 1)
    g.side_arrive("RQA", "LQB", "YO2")
    use(1, 2)


def iota(axis):
    return lax.broadcasted_iota(jnp.int32, (T, T), axis)


def mm(a, b):
    return jnp.dot(a.astype(BF16), b.astype(BF16), preferred_element_type=F32)


def mm_t(a, b):
    return lax.dot_general(
        a.astype(BF16), b.astype(BF16), (((1,), (1,)), ((), ())), preferred_element_type=F32
    )


def softplus(v):
    return jnp.maximum(v, 0.0) + jnp.log1p(jnp.exp(-jnp.abs(v)))


def steps_of(raw, params):
    step = softplus(raw + params[0:1, :])
    lower = (iota(0) >= iota(1)).astype(F32)
    decay = jnp.dot(
        lower, -step * params[1:2, :], preferred_element_type=F32, precision=lax.Precision.HIGHEST
    )
    return step, decay, jnp.transpose(step), jnp.transpose(decay)


def head(k):
    return slice(k * 128, (k + 1) * 128)


class States:
    def __init__(self, slots, sums, send, recv):
        self.slots, self.sums, self.send, self.recv = slots, sums, send, recv
        self.me, self.y, self.z, self.c = place()
        self.m = self.me % 8

    def peer(self, k):
        at = (self.m + k) % 8
        return pltpu.make_async_remote_copy(
            src_ref=self.slots.at[self.m],
            dst_ref=self.slots.at[self.m],
            send_sem=self.send.at[k - 1],
            recv_sem=self.recv.at[k - 1],
            device_id={"dp": self.y * 8 + at},
            device_id_type=MESH,
        )

    def from_peer(self, k):
        at = (self.m - k + 8) % 8
        return pltpu.make_async_remote_copy(
            src_ref=self.slots.at[at],
            dst_ref=self.slots.at[at],
            send_sem=self.send.at[k - 1],
            recv_sem=self.recv.at[k - 1],
            device_id={"dp": self.y * 8 + at},
            device_id_type=MESH,
        )

    def across(self):
        return pltpu.make_async_remote_copy(
            src_ref=self.sums.at[0],
            dst_ref=self.sums.at[1],
            send_sem=self.send.at[7],
            recv_sem=self.recv.at[7],
            device_id={"dp": (1 - self.y) * 8 + self.m},
            device_id_type=MESH,
        )

    def begin(self):
        for k in range(1, 8):
            self.peer(k).start()

    def gathered(self):
        for k in range(1, 8):
            self.from_peer(k).wait_recv()

    def finish(self):
        for k in range(1, 8):
            self.peer(k).wait_send()
        self.across().wait_send()


def front_kernel(
    resid, teacher, gain_mix, gain_mlp, w_c, w_b, w_x, w_dt, params, w_gate, w_up,
    w_all, cols, mixer_out, target, read_out, inject_out, value_out, raw_out, enter_out, decays,
    held, v_resid, v_teacher, v_wc, v_wb, v_wx, v_wdt, nin, tin, acc, proj, state, sums, through,
    in_sem, out_sem, g_send, g_recv, s_send, s_recv, d_send, d_recv, c_send, c_recv,
):
    me, y, z, c = place()
    m = me % 8
    own = [
        pltpu.make_async_copy(w_gate, held.at[me, 0], in_sem.at[0]),
        pltpu.make_async_copy(w_up, held.at[me, 1], in_sem.at[1]),
    ]
    loads = [
        pltpu.make_async_copy(src, dst, in_sem.at[2 + k])
        for k, (src, dst) in enumerate(
            ((resid, v_resid), (w_c, v_wc), (w_b, v_wb), (w_x, v_wx), (w_dt, v_wdt), (teacher, v_teacher))
        )
    ]
    for copy in own + loads:
        copy.start()
    barrier_all("dp", DP)
    for copy in own:
        copy.wait()
    gather = Gather(
        lambda j, start, size: held.at[j, :, pl.ds(start, size), :], ROWS, 112, 64, g_send, g_recv
    )
    gather.begin()

    def norm(source, gain, put):
        def square(k, total):
            part = source[:, pl.ds(pl.multiple_of(k * 256, 256), 256)].astype(F32)
            return total + jnp.sum(part * part, axis=1, keepdims=True)

        scale = lax.rsqrt(lax.fori_loop(0, 16, square, jnp.zeros((T, 1), F32)) / D + EPS)

        def write(k, _):
            at = pl.ds(pl.multiple_of(k * 256, 256), 256)
            put(k, (source[:, at].astype(F32) * scale * gain[:, at]).astype(BF16))
            return 0

        lax.fori_loop(0, 16, write, 0)

    def put_nin(k, value):
        nin[k] = value

    def put_tin(k, value):
        tin[k] = value

    loads[0].wait()
    norm(v_resid, gain_mix, put_nin)

    def column_copy(k):
        to = (me + k) % DP
        return pltpu.make_async_remote_copy(
            src_ref=nin.at[to],
            dst_ref=cols.at[me],
            send_sem=c_send.at[k - 1],
            recv_sem=c_recv.at[k - 1],
            device_id={"dp": to},
            device_id_type=MESH,
        )

    def column_landed(k):
        at = (me - k + DP) % DP
        return pltpu.make_async_remote_copy(
            src_ref=nin.at[at],
            dst_ref=cols.at[at],
            send_sem=c_send.at[k - 1],
            recv_sem=c_recv.at[k - 1],
            device_id={"dp": at},
            device_id_type=MESH,
        )

    for k in range(1, DP):
        column_copy(k).start()
    cols[me] = nin[me]

    for copy in loads[1:5]:
        copy.wait()
    proj[...] = jnp.zeros_like(proj)

    def project(k, _):
        at = pl.ds(pl.multiple_of(k * 256, 256), 256)
        rows = nin[k]
        proj[:, 0:512] += jnp.dot(rows, v_wc[at, :], preferred_element_type=F32)
        proj[:, 512:640] += jnp.dot(rows, v_wb[at, :], preferred_element_type=F32)
        proj[:, 640:768] += jnp.dot(rows, v_wx[at, :], preferred_element_type=F32)
        proj[:, 768:896] += jnp.dot(rows, v_wdt[at, :], preferred_element_type=F32)
        return 0

    lax.fori_loop(0, 16, project, 0)
    read_out[...] = proj[:, 0:512].astype(BF16)
    inject = proj[:, 512:640]
    values = proj[:, 640:768]
    inject_out[...] = inject.astype(BF16)
    value_out[...] = values.astype(BF16)
    raw_out[...] = proj[:, 768:896]
    step, decay, step_t, decay_t = steps_of(proj[:, 768:896], params)
    causal = iota(0) >= iota(1)
    inject_t = jnp.transpose(inject)
    for h in range(HEADS):
        row, col, step_row = decay_t[h : h + 1, :], decay[:, h : h + 1], step_t[h : h + 1, :]
        last = row[:, T - 1 : T]
        weight = jnp.exp(jnp.where(causal, col - row, -1e30)) * step_row
        weight = weight * mm_t(read_out[:, head(h)], inject)
        through[:, head(h)] = mm(weight, values) + params[2:3, h : h + 1] * values
        state[m, :, head(h)] = mm(inject_t * (jnp.exp(last - row) * step_row), values).astype(BF16)
    decays[m] = jnp.broadcast_to(decay[T - 1 : T, :], (8, 128))

    states = States(state, sums, s_send, s_recv)
    ends = States(decays, None, d_send, d_recv)
    states.begin()
    ends.begin()

    loads[5].wait()
    norm(v_teacher, gain_mlp, put_tin)
    acc[...] = jnp.zeros_like(acc)
    ends.gathered()
    states.gathered()

    def weights():
        run_in, run_all = jnp.zeros((1, 128), F32), jnp.zeros((1, 128), F32)
        inside, whole = [None] * 8, [None] * 8
        for j in reversed(range(8)):
            reached = (j < m).astype(F32)
            inside[j] = reached * jnp.exp(run_in)
            whole[j] = jnp.exp(run_all)
            end = decays[j, 0:1, :]
            run_in = run_in + reached * end
            run_all = run_all + end
        return inside, whole, jnp.exp(run_in)

    inside, whole, lead = weights()
    for h in range(HEADS):
        total = jnp.zeros((128, 128), F32)
        for j in range(8):
            total = total + whole[j][:, h : h + 1] * state[j, :, head(h)].astype(F32)
        sums[0, :, head(h)] = total.astype(BF16)
    states.across().start()
    states.across().wait_recv()
    after = (y == 1).astype(F32)
    for h in range(HEADS):
        total = (after * lead[:, h : h + 1]) * sums[1, :, head(h)].astype(F32)
        for j in range(8):
            total = total + inside[j][:, h : h + 1] * state[j, :, head(h)].astype(F32)
        entering = total.astype(BF16)
        enter_out[:, head(h)] = entering
        grown = jnp.exp(decay[:, h : h + 1]) * mm(read_out[:, head(h)], entering)
        mixer_out[:, head(h)] = (through[:, head(h)] + grown).astype(BF16)

    def out_copy(j):
        return pltpu.make_async_copy(held.at[j], w_all.at[j], out_sem.at[j])

    def use(flip, dz):
        base = gather.block(flip, dz, 0)

        def one(i, _):
            j = base + i
            out_copy(j).start()
            rows = tin[j]
            acc[0] += jnp.dot(rows, held[j, 0], preferred_element_type=F32)
            acc[1] += jnp.dot(rows, held[j, 1], preferred_element_type=F32)
            return 0

        lax.fori_loop(0, 2, one, 0)

    run_gather(gather, use)

    def aim(k, _):
        at = pl.ds(pl.multiple_of(k * 256, 256), 256)
        gate = acc[0, :, at]
        target[:, at] = gate * jax.nn.sigmoid(gate) * acc[1, :, at]
        return 0

    lax.fori_loop(0, HID // 256, aim, 0)
    gather.finish()
    states.finish()
    for k in range(1, 8):
        ends.peer(k).wait_send()
    for k in range(1, DP):
        column_copy(k).wait_send()
        column_landed(k).wait_recv()
    for j in range(DP):
        out_copy(j).wait()


def middle_kernel(
    mixer_out, w_out, gain_mlp, resid, target, w_all,
    out_grad,
    held, v_out, v_resid, v_target, p_send, p_recv, strm, xs, g_up, g_gate, q_send, q_recv, gained_all, delta,
    in_sem, w_sem, send, recv,
):
    t = lax.axis_index("tensor")
    copies = [
        pltpu.make_async_copy(w_out, v_out, in_sem.at[0]),
        pltpu.make_async_copy(
            resid.at[:, pl.ds(pl.multiple_of(t * WIDTH, WIDTH), WIDTH)], v_resid, in_sem.at[1]
        ),
        pltpu.make_async_copy(target, v_target, in_sem.at[2]),
    ]
    w_copies = [pltpu.make_async_copy(w_all.at[j], held.at[j], w_sem.at[j]) for j in range(DP)]
    for copy in copies:
        copy.start()
    for copy in w_copies:
        copy.start()
    barrier_all("tensor", TP)

    def move(phase, k, src, dst):
        return pltpu.make_async_remote_copy(
            src_ref=src,
            dst_ref=dst,
            send_sem=send.at[phase, k - 1],
            recv_sem=recv.at[phase, k - 1],
            device_id={"tensor": (t + k) % TP},
            device_id_type=MESH,
        )

    def columns(p):
        return pl.ds(pl.multiple_of(p * WIDTH, WIDTH), WIDTH)

    def out_part(p):
        return jnp.dot(mixer_out[...], v_out[:, columns(p)], preferred_element_type=F32)

    copies[0].wait()
    for k in range(1, TP):
        p_send[k - 1] = out_part((t + k) % TP).astype(BF16)
        move(0, k, p_send.at[k - 1], p_recv.at[k - 1]).start()
    copies[1].wait()
    stream = out_part(t) + v_resid[...].astype(F32)
    for k in range(1, TP):
        move(0, k, p_send.at[k - 1], p_recv.at[k - 1]).wait_recv()
        stream = stream + p_recv[k - 1].astype(F32)
    strm[t] = stream.astype(BF16)
    for k in range(1, TP):
        move(1, k, strm.at[t], strm.at[t]).start()
    for k in range(1, TP):
        at = (t - k + TP) % TP
        move(1, k, strm.at[at], strm.at[at]).wait_recv()

    def square(p, total):
        part = strm[p].astype(F32)
        return total + jnp.sum(part * part, axis=1, keepdims=True)

    scale = lax.rsqrt(lax.fori_loop(0, TP, square, jnp.zeros((T, 1), F32)) / D + EPS)

    def write(p, _):
        part = (strm[p].astype(F32) * scale * gain_mlp[:, columns(p)]).astype(BF16)
        xs[2 * p] = part[:, 0:256]
        xs[2 * p + 1] = part[:, 256:512]
        return 0

    lax.fori_loop(0, TP, write, 0)
    copies[2].wait()
    for copy in w_copies:
        copy.wait()

    def hidden(n, _):
        at = pl.ds(pl.multiple_of(n * 256, 256), 256)
        gate = jnp.zeros((T, 256), F32)
        up = jnp.zeros((T, 256), F32)
        for k in range(DP):
            gate = gate + jnp.dot(xs[k], held[k, 0, :, at], preferred_element_type=F32)
            up = up + jnp.dot(xs[k], held[k, 1, :, at], preferred_element_type=F32)
        sigma = jax.nn.sigmoid(gate)
        silu = gate * sigma
        grad = (2.0 / math.sqrt(FF)) * (silu * up - v_target[:, at])
        g_gate[:, at] = (grad * up * sigma * (1.0 + gate * (1.0 - sigma))).astype(BF16)
        g_up[:, at] = (grad * silu).astype(BF16)
        return 0

    lax.fori_loop(0, HID // 256, hidden, 0)

    def back(p):
        return jnp.concatenate(
            [
                mm_t(g_gate[...], held[2 * p + i, 0]) + mm_t(g_up[...], held[2 * p + i, 1])
                for i in range(2)
            ],
            axis=1,
        )

    def back_send(k, _):
        q_send[k - 1] = back((t + k) % TP).astype(BF16)
        move(2, k, q_send.at[k - 1], q_recv.at[k - 1]).start()
        return 0

    lax.fori_loop(1, TP, back_send, 0)
    mid = back(t)
    for k in range(1, TP):
        move(2, k, q_send.at[k - 1], q_recv.at[k - 1]).wait_recv()
        mid = mid + q_recv[k - 1].astype(F32)
    gained_all[t] = (mid * gain_mlp[:, columns(t)]).astype(BF16)
    for k in range(1, TP):
        move(3, k, gained_all.at[t], gained_all.at[t]).start()
    for k in range(1, TP):
        at = (t - k + TP) % TP
        move(3, k, gained_all.at[at], gained_all.at[at]).wait_recv()

    def product(p, total):
        return total + jnp.sum(
            gained_all[p].astype(F32) * strm[p].astype(F32), axis=1, keepdims=True
        )

    inner = lax.fori_loop(0, TP, product, jnp.zeros((T, 1), F32))
    pull = scale * scale * scale * (inner / D)
    out_grad[...] = jnp.zeros_like(out_grad)

    def project(p, _):
        delta[...] = (gained_all[p].astype(F32) * scale - strm[p].astype(F32) * pull).astype(BF16)
        out_grad[...] += mm_t(delta[...], v_out[:, columns(p)])
        return 0

    lax.fori_loop(0, TP, project, 0)
    for k in range(1, TP):
        move(0, k, p_send.at[k - 1], p_recv.at[k - 1]).wait_send()
        move(1, k, strm.at[t], strm.at[t]).wait_send()
        move(2, k, q_send.at[k - 1], q_recv.at[k - 1]).wait_send()
        move(3, k, gained_all.at[t], gained_all.at[t]).wait_send()


def back_kernel(
    out_grad, read, inject_in, value_in, raw, params, enter, decays, cols,
    grad_c, grad_b, grad_x, grad_dt,
    packed, state, sums, acc, cols_t, dread, dinject, dvalue,
    g_send, g_recv, s_send, s_recv,
):
    me, y, z, c = place()
    m = me % 8
    inject, values = inject_in[...].astype(F32), value_in[...].astype(F32)
    step, decay, step_t, decay_t = steps_of(raw[...], params)
    growth, growth_t = jnp.exp(decay), jnp.exp(decay_t)
    for h in range(HEADS):
        read_t = jnp.transpose(read[:, head(h)].astype(F32))
        state[m, :, head(h)] = mm(read_t * growth_t[h : h + 1, :], out_grad[:, head(h)]).astype(BF16)
    barrier_all("dp", DP)
    states = States(state, sums, s_send, s_recv)
    states.begin()

    causal = iota(0) >= iota(1)
    lanes = lax.broadcasted_iota(jnp.int32, (1, 128), 1)
    dinject[...] = jnp.zeros_like(dinject)
    dvalue[...] = jnp.zeros_like(dvalue)
    step_rows, decay_rows, decay_cols = [], [], []
    for h in range(HEADS):
        row, col, step_row = decay_t[h : h + 1, :], decay[:, h : h + 1], step_t[h : h + 1, :]
        read_h, grad_h = read[:, head(h)], out_grad[:, head(h)]
        enter_h = enter[:, head(h)]
        fade = jnp.exp(jnp.where(causal, col - row, -1e30))
        score = mm_t(read_h, inject)
        plain = fade * score
        dweight = mm_t(grad_h, values)
        direct = dweight * plain
        dscore = dweight * fade * step_row
        weight = plain * step_row
        through = mm_t(grad_h, enter_h)
        dread[:, head(h)] = mm(dscore, inject) + growth[:, h : h + 1] * through
        dinject[...] += mm(jnp.transpose(dscore), read_h)
        dvalue[...] += mm(jnp.transpose(weight), grad_h) + params[2:3, h : h + 1] * grad_h
        column = jnp.sum(direct, axis=0, keepdims=True)
        step_rows.append(column)
        decay_rows.append(-column * step_row)
        along = growth[:, h : h + 1] * jnp.sum(
            through * read_h.astype(F32), axis=1, keepdims=True
        )
        decay_cols.append(jnp.sum(direct * step_row, axis=1, keepdims=True) + along)

    def turn(k, _):
        cols_t[k] = jnp.transpose(cols[k].astype(F32)).astype(BF16)
        return 0

    lax.fori_loop(0, DP, turn, 0)
    states.gathered()
    run_in, run_all = jnp.zeros((1, 128), F32), jnp.zeros((1, 128), F32)
    inside, whole = [None] * 8, [None] * 8
    for j in range(8):
        reached = (j > m).astype(F32)
        inside[j] = reached * jnp.exp(run_in)
        whole[j] = jnp.exp(run_all)
        end = decays[j, 0:1, :]
        run_in = run_in + reached * end
        run_all = run_all + end
    lead = jnp.exp(run_in)
    for h in range(HEADS):
        total = jnp.zeros((128, 128), F32)
        for j in range(8):
            total = total + whole[j][:, h : h + 1] * state[j, :, head(h)].astype(F32)
        sums[0, :, head(h)] = total.astype(BF16)
    states.across().start()
    states.across().wait_recv()
    before = (y == 0).astype(F32)
    dstep = jnp.zeros((T, 128), F32)
    ddecay = jnp.zeros((T, 128), F32)
    step_parts, decay_parts = [], []
    for h in range(HEADS):
        row, step_row = decay_t[h : h + 1, :], step_t[h : h + 1, :]
        last = row[:, T - 1 : T]
        behind = (before * lead[:, h : h + 1]) * sums[1, :, head(h)].astype(F32)
        for j in range(8):
            behind = behind + inside[j][:, h : h + 1] * state[j, :, head(h)].astype(F32)
        tail_col = jnp.exp(decay[T - 1 : T, h : h + 1] - decay[:, h : h + 1])
        scaled_col = tail_col * step[:, h : h + 1]
        pulled = mm_t(values, behind)
        dinject[...] += scaled_col * pulled
        dvalue[...] += scaled_col * mm(inject, behind)
        drawn = tail_col * jnp.sum(inject * pulled, axis=1, keepdims=True)
        moved = drawn * step[:, h : h + 1]
        kept = jnp.exp(last) * jnp.sum(
            jnp.sum(behind * enter[:, head(h)].astype(F32), axis=1, keepdims=True),
            axis=0,
            keepdims=True,
        )
        end = kept + jnp.sum(moved, axis=0, keepdims=True)
        onehot = (lanes == h).astype(F32)
        final = (lax.broadcasted_iota(jnp.int32, (T, 1), 0) == T - 1).astype(F32)
        dstep = dstep + drawn * onehot
        ddecay = ddecay + (decay_cols[h] - moved + final * end) * onehot
    zero = jnp.zeros((128 - HEADS, 128), F32)
    dstep = dstep + jnp.transpose(jnp.concatenate(step_rows + [zero], axis=0))
    ddecay = ddecay + jnp.transpose(jnp.concatenate(decay_rows + [zero], axis=0))
    upper = (iota(0) <= iota(1)).astype(F32)
    later = jnp.dot(
        upper, ddecay, preferred_element_type=F32, precision=lax.Precision.HIGHEST
    )
    dstep = dstep - params[1:2, :] * later
    draw = dstep * jax.nn.sigmoid(raw[...] + params[0:1, :])
    packed[me, :, 0:512] = dread[...].astype(BF16)
    packed[me, :, 512:640] = dinject[...].astype(BF16)
    packed[me, :, 640:768] = dvalue[...].astype(BF16)
    packed[me, :, 768:896] = draw.astype(BF16)

    gather = Gather(lambda j, start, size: packed.at[j, pl.ds(start, size), :], T, 48, 48, g_send, g_recv)
    gather.begin()
    acc[...] = jnp.zeros_like(acc)

    def use(flip, dz):
        base = gather.block(flip, dz, 0)

        def one(i, _):
            acc[...] += jnp.dot(cols_t[base + i], packed[base + i], preferred_element_type=F32)
            return 0

        lax.fori_loop(0, 2, one, 0)

    run_gather(gather, use)
    grad_c[...] = acc[:, 0:512]
    grad_b[...] = acc[:, 512:640]
    grad_x[...] = acc[:, 640:768]
    grad_dt[...] = acc[:, 768:896]
    gather.finish()
    states.finish()


VM = pl.BlockSpec(memory_space=pltpu.VMEM)
ANY = pl.BlockSpec(memory_space=pl.ANY)
DMA = pltpu.SemaphoreType.DMA


def struct(shape, dtype):
    return jax.ShapeDtypeStruct(shape, dtype)


def params_of(number):
    return pltpu.CompilerParams(
        collective_id=number, has_side_effects=True, vmem_limit_bytes=60 * MIB
    )


def local(
    resid, teacher_mixed, gain_mix, gain_mlp, w_c, w_b, w_x, w_dt, dt_bias, decay_rate, skip, w_out,
    w_gate, w_up,
):
    w_dt_wide = jnp.pad(w_dt, ((0, 0), (0, 128 - HEADS)))
    scalars = jnp.pad(jnp.stack([dt_bias, decay_rate, skip]), ((0, 5), (0, 128 - HEADS)))
    gain_mix, gain_mlp = gain_mix.reshape(1, D), gain_mlp.reshape(1, D)
    w_all, cols, mixer_out, target, read, inject, values, raw, enter, decays = pl.pallas_call(
        front_kernel,
        out_shape=(
            struct((DP, 2, ROWS, HID), BF16),
            struct((DP, T, 256), BF16),
            struct((T, WIDTH), BF16),
            struct((T, HID), F32),
            struct((T, WIDTH), BF16),
            struct((T, 128), BF16),
            struct((T, 128), BF16),
            struct((T, 128), F32),
            struct((128, WIDTH), BF16),
            struct((8, 8, 128), F32),
        ),
        in_specs=[ANY, ANY, VM, VM, ANY, ANY, ANY, ANY, VM, ANY, ANY],
        out_specs=(ANY,) + (VM,) * 9,
        scratch_shapes=[
            pltpu.VMEM((DP, 2, ROWS, HID), BF16),
            pltpu.VMEM((T, D), BF16),
            pltpu.VMEM((T, D), BF16),
            pltpu.VMEM((D, 512), BF16),
            pltpu.VMEM((D, 128), BF16),
            pltpu.VMEM((D, 128), BF16),
            pltpu.VMEM((D, 128), BF16),
            pltpu.VMEM((16, T, 256), BF16),
            pltpu.VMEM((16, T, 256), BF16),
            pltpu.VMEM((2, T, HID), F32),
            pltpu.VMEM((T, PACK), F32),
            pltpu.VMEM((8, 128, WIDTH), BF16),
            pltpu.VMEM((2, 128, WIDTH), BF16),
            pltpu.VMEM((T, WIDTH), F32),
            DMA((8,)),
            DMA((DP,)),
            DMA((NSEM,)),
            DMA((NSEM,)),
            DMA((8,)),
            DMA((8,)),
            DMA((8,)),
            DMA((8,)),
            DMA((DP,)),
            DMA((DP,)),
        ],
        compiler_params=params_of(0),
        name="front",
    )(resid, teacher_mixed, gain_mix, gain_mlp, w_c, w_b, w_x, w_dt_wide, scalars, w_gate, w_up)
    out_grad = pl.pallas_call(
        middle_kernel,
        out_shape=struct((T, WIDTH), F32),
        in_specs=[VM, ANY, VM, ANY, ANY, ANY],
        out_specs=VM,
        scratch_shapes=[
            pltpu.VMEM((DP, 2, ROWS, HID), BF16),
            pltpu.VMEM((512, D), BF16),
            pltpu.VMEM((T, WIDTH), BF16),
            pltpu.VMEM((T, HID), F32),
            pltpu.VMEM((TP - 1, T, WIDTH), BF16),
            pltpu.VMEM((TP - 1, T, WIDTH), BF16),
            pltpu.VMEM((TP, T, WIDTH), BF16),
            pltpu.VMEM((16, T, 256), BF16),
            pltpu.VMEM((T, HID), BF16),
            pltpu.VMEM((T, HID), BF16),
            pltpu.VMEM((TP - 1, T, WIDTH), BF16),
            pltpu.VMEM((TP - 1, T, WIDTH), BF16),
            pltpu.VMEM((TP, T, WIDTH), BF16),
            pltpu.VMEM((T, WIDTH), BF16),
            DMA((4,)),
            DMA((DP,)),
            DMA((4, TP - 1)),
            DMA((4, TP - 1)),
        ],
        compiler_params=params_of(1),
        name="middle",
    )(mixer_out, w_out, gain_mlp, resid, target, w_all)
    grad_c, grad_b, grad_x, grad_dt = pl.pallas_call(
        back_kernel,
        out_shape=(
            struct((ROWS, 512), F32),
            struct((ROWS, 128), F32),
            struct((ROWS, 128), F32),
            struct((ROWS, 128), F32),
        ),
        in_specs=[VM] * 9,
        out_specs=(VM,) * 4,
        scratch_shapes=[
            pltpu.VMEM((DP, T, PACK), BF16),
            pltpu.VMEM((8, 128, WIDTH), BF16),
            pltpu.VMEM((2, 128, WIDTH), BF16),
            pltpu.VMEM((ROWS, PACK), F32),
            pltpu.VMEM((DP, 256, T), BF16),
            pltpu.VMEM((T, WIDTH), F32),
            pltpu.VMEM((T, 128), F32),
            pltpu.VMEM((T, 128), F32),
            DMA((NSEM,)),
            DMA((NSEM,)),
            DMA((8,)),
            DMA((8,)),
        ],
        compiler_params=params_of(2),
        name="back",
    )(out_grad, read, inject, values, raw, scalars, enter, decays, cols)
    return grad_c, grad_b, grad_x, grad_dt[:, 0:HEADS]


def solution(mesh):
    in_specs = (
        P("dp", None),
        P("dp", None),
        P(),
        P(),
        P(None, "tensor"),
        P(None, "tensor"),
        P(None, "tensor"),
        P(None, "tensor"),
        P("tensor"),
        P("tensor"),
        P("tensor"),
        P("tensor", None),
        P("dp", "tensor"),
        P("dp", "tensor"),
    )
    out_specs = (P("dp", "tensor"), P("dp", "tensor"), P("dp", "tensor"), P("dp", "tensor"))
    return jax.shard_map(local, mesh=mesh, in_specs=in_specs, out_specs=out_specs, check_vma=False)
```

```python
import math
from types import SimpleNamespace

import jax
import jax.numpy as jnp
from jax import lax
from jax.experimental import pallas as pl
from jax.experimental.pallas import tpu as pltpu
from jax.sharding import PartitionSpec as P

D = 4096
FF = 14336
EPS = 1e-05
T = 128
HEADS = 4
DP = 16
TP = 8
HID = 1792
ROWS = 256
WIDTH = 512
PACK = 896
F32 = jnp.float32
BF16 = jnp.bfloat16
MESH = pl.DeviceIdType.MESH
MIB = 1024 * 1024

LEGS = {
    "RO": ("R", 0, 0, "full", 0, -1),
    "LO": ("L", 0, 0, "full", 0, 1),
    "YO": ("Y", 0, 0, "full", 1, 0),
    "RQ": ("R", 1, 0, "Q", 1, -1),
    "LQ": ("L", 1, 0, "Q", 1, 1),
    "RA": ("R", 0, -1, "A", 0, 2),
    "LB": ("L", 0, 1, "B", 0, 2),
    "YL": ("Y", 0, -1, "P", 1, -1),
    "YR": ("Y", 0, 1, "P", 1, 1),
    "RQA": ("R", 1, -1, "QA", 1, 2),
    "LQB": ("L", 1, 1, "QB", 1, 2),
    "YO2": ("Y", 0, 2, "P", 1, 2),
}
ORDER = list(LEGS)
NSEM = 2 * len(ORDER) + 1


def place():
    me = lax.axis_index("dp")
    return me, me // 8, (me % 8) // 2, me % 2


class Gather:
    def __init__(self, piece, rows, p, qa, send, recv):
        self.piece, self.send, self.recv = piece, send, recv
        self.me, self.y, self.z, self.c = place()
        half = rows // 2
        self.rows = {
            "full": (0, rows),
            "P": (0, p),
            "Q": (p, rows - p),
            "A": (0, half),
            "B": (half, rows - half),
            "QA": (p, qa),
            "QB": (p + qa, rows - p - qa),
        }

    def block(self, flip, dz, core):
        y = (1 - self.y) if flip else self.y
        return y * 8 + ((self.z + dz + 4) % 4) * 2 + core

    def target(self, name):
        if name == "R":
            return self.block(0, 1, self.c)
        if name == "L":
            return self.block(0, -1, self.c)
        if name == "Y":
            return self.block(1, 0, self.c)
        return self.block(0, 0, 1 - self.c)

    def copy(self, ref, sem, to):
        return pltpu.make_async_remote_copy(
            src_ref=ref,
            dst_ref=ref,
            send_sem=self.send.at[sem],
            recv_sem=self.recv.at[sem],
            device_id={"dp": to},
            device_id_type=MESH,
        )

    def leg(self, name):
        to, flip, dz, rows, _, _ = LEGS[name]
        ref = self.piece(self.block(flip, dz, self.c), *self.rows[rows])
        return self.copy(ref, ORDER.index(name), self.target(to))

    def landed(self, name):
        to, _, _, rows, flip, dz = LEGS[name]
        ref = self.piece(self.block(flip, dz, self.c), *self.rows[rows])
        return self.copy(ref, ORDER.index(name), self.target(to))

    def side(self, name, core):
        if name == "own":
            flip, dz, rows, sem = 0, 0, "full", len(ORDER)
        else:
            _, _, _, rows, flip, dz = LEGS[name]
            sem = len(ORDER) + 1 + ORDER.index(name)
        ref = self.piece(self.block(flip, dz, core), *self.rows[rows])
        return self.copy(ref, sem, self.target("S"))

    def begin(self):
        for name in ("RO", "LO", "YO"):
            self.leg(name).start()
        self.side("own", self.c).start()

    def arrive(self, name, *then):
        self.landed(name).wait_recv()
        for other in then:
            self.leg(other).start()
        self.side(name, self.c).start()

    def side_arrive(self, *names):
        for name in names:
            self.side(name, 1 - self.c).wait_recv()

    def finish(self):
        for name in ORDER:
            self.leg(name).wait_send()
        for name in ["own"] + ORDER:
            self.side(name, self.c).wait_send()


def iota(axis):
    return lax.broadcasted_iota(jnp.int32, (T, T), axis)


def mm(a, b):
    return jnp.dot(a.astype(BF16), b.astype(BF16), preferred_element_type=F32)


def mm_t(a, b):
    return lax.dot_general(
        a.astype(BF16), b.astype(BF16), (((1,), (1,)), ((), ())), preferred_element_type=F32
    )


def softplus(v):
    return jnp.maximum(v, 0.0) + jnp.log1p(jnp.exp(-jnp.abs(v)))


def steps_of(raw, params):
    step = softplus(raw + params[0:1, :])
    lower = (iota(0) >= iota(1)).astype(F32)
    decay = jnp.dot(
        lower, -step * params[1:2, :], preferred_element_type=F32, precision=lax.Precision.HIGHEST
    )
    return step, decay, jnp.transpose(step), jnp.transpose(decay)


def head(k):
    return slice(k * 128, (k + 1) * 128)


class States:
    def __init__(self, slots, sums, send, recv):
        self.slots, self.sums, self.send, self.recv = slots, sums, send, recv
        self.me, self.y, self.z, self.c = place()
        self.m = self.me % 8

    def peer(self, k):
        at = (self.m + k) % 8
        return pltpu.make_async_remote_copy(
            src_ref=self.slots.at[self.m],
            dst_ref=self.slots.at[self.m],
            send_sem=self.send.at[k - 1],
            recv_sem=self.recv.at[k - 1],
            device_id={"dp": self.y * 8 + at},
            device_id_type=MESH,
        )

    def from_peer(self, k):
        at = (self.m - k + 8) % 8
        return pltpu.make_async_remote_copy(
            src_ref=self.slots.at[at],
            dst_ref=self.slots.at[at],
            send_sem=self.send.at[k - 1],
            recv_sem=self.recv.at[k - 1],
            device_id={"dp": self.y * 8 + at},
            device_id_type=MESH,
        )

    def across(self):
        return pltpu.make_async_remote_copy(
            src_ref=self.sums.at[0],
            dst_ref=self.sums.at[1],
            send_sem=self.send.at[7],
            recv_sem=self.recv.at[7],
            device_id={"dp": (1 - self.y) * 8 + self.m},
            device_id_type=MESH,
        )

    def begin(self):
        for k in range(1, 8):
            self.peer(k).start()

    def gathered(self):
        for k in range(1, 8):
            self.from_peer(k).wait_recv()

    def finish(self):
        for k in range(1, 8):
            self.peer(k).wait_send()
        self.across().wait_send()


def spread(scalars):
    lane = lax.broadcasted_iota(jnp.int32, (1, 128), 1)
    row = jnp.zeros((1, 128), F32)
    for h in range(HEADS):
        row = jnp.where(lane == h, scalars[h], row)
    return row


SCRATCH = {
    "held": pltpu.VMEM((DP, 2, ROWS, HID), BF16),
    "v_wc": pltpu.VMEM((D, 512), BF16),
    "v_wb": pltpu.VMEM((D, 128), BF16),
    "v_wx": pltpu.VMEM((D, 128), BF16),
    "v_wdt": pltpu.VMEM((HEADS, D), BF16),
    "v_out": pltpu.VMEM((512, D), BF16),
    "v_resid": pltpu.VMEM((T, WIDTH), BF16),
    "nin": pltpu.VMEM((T, D), BF16),
    "nin_t": pltpu.VMEM((DP, 256, T), BF16),
    "cols": pltpu.VMEM((DP, 256, T), BF16),
    "lhs": pltpu.VMEM((2 * T, D), BF16),
    "acc": pltpu.VMEM((2, 2 * T, HID), F32),
    "proj": pltpu.VMEM((T, PACK), F32),
    "read": pltpu.VMEM((T, WIDTH), BF16),
    "state": pltpu.VMEM((8, 128, WIDTH), BF16),
    "sums": pltpu.VMEM((2, 128, WIDTH), BF16),
    "decays": pltpu.VMEM((8, 8, 128), F32),
    "enter": pltpu.VMEM((128, WIDTH), BF16),
    "through": pltpu.VMEM((T, WIDTH), F32),
    "mixer_out": pltpu.VMEM((T, WIDTH), BF16),
    "fade": pltpu.VMEM((HEADS, T, T), F32),
    "plain": pltpu.VMEM((HEADS, T, T), F32),
    "p_send": pltpu.VMEM((TP - 1, T, WIDTH), BF16),
    "p_recv": pltpu.VMEM((TP - 1, T, WIDTH), BF16),
    "strm": pltpu.VMEM((TP, T, WIDTH), BF16),
    "gained": pltpu.VMEM((TP, T, WIDTH), BF16),
    "g_gate": pltpu.VMEM((T, HID), BF16),
    "g_up": pltpu.VMEM((T, HID), BF16),
    "out_grad": pltpu.VMEM((T, WIDTH), F32),
    "b_state": pltpu.VMEM((8, 128, WIDTH), BF16),
    "b_sums": pltpu.VMEM((2, 128, WIDTH), BF16),
    "packed": pltpu.VMEM((DP, T, PACK), BF16),
    "dread": pltpu.VMEM((T, WIDTH), F32),
    "dinject": pltpu.VMEM((T, 128), F32),
    "dvalue": pltpu.VMEM((T, 128), F32),
    "in_sem": pltpu.SemaphoreType.DMA((10,)),
    "g_send": pltpu.SemaphoreType.DMA((NSEM,)),
    "g_recv": pltpu.SemaphoreType.DMA((NSEM,)),
    "h_send": pltpu.SemaphoreType.DMA((NSEM,)),
    "h_recv": pltpu.SemaphoreType.DMA((NSEM,)),
    "s_send": pltpu.SemaphoreType.DMA((8,)),
    "s_recv": pltpu.SemaphoreType.DMA((8,)),
    "d_send": pltpu.SemaphoreType.DMA((8,)),
    "d_recv": pltpu.SemaphoreType.DMA((8,)),
    "b_send": pltpu.SemaphoreType.DMA((8,)),
    "b_recv": pltpu.SemaphoreType.DMA((8,)),
    "c_send": pltpu.SemaphoreType.DMA((DP - 1,)),
    "c_recv": pltpu.SemaphoreType.DMA((DP - 1,)),
    "t_send": pltpu.SemaphoreType.DMA((4, TP - 1)),
    "t_recv": pltpu.SemaphoreType.DMA((4, TP - 1)),
}


def chunk(k, size=256):
    return pl.ds(pl.multiple_of(k * size, size), size)


def columns(p):
    return chunk(p, WIDTH)


def normalise(ref, rows, gain):
    def square(k, total):
        part = ref[rows, chunk(k)].astype(F32)
        return total + jnp.sum(part * part, axis=1, keepdims=True)

    scale = lax.rsqrt(lax.fori_loop(0, 16, square, jnp.zeros((T, 1), F32)) / D + EPS)

    def write(k, _):
        ref[rows, chunk(k)] = (ref[rows, chunk(k)].astype(F32) * scale * gain[:, chunk(k)]).astype(BF16)
        return 0

    lax.fori_loop(0, 16, write, 0)


def state_weights(decays, m, forward):
    run_in, run_all = jnp.zeros((1, 128), F32), jnp.zeros((1, 128), F32)
    inside, whole = [None] * 8, [None] * 8
    for j in reversed(range(8)) if forward else range(8):
        reached = ((j < m) if forward else (j > m)).astype(F32)
        inside[j] = reached * jnp.exp(run_in)
        whole[j] = jnp.exp(run_all)
        end = decays[j, 0:1, :]
        run_in = run_in + reached * end
        run_all = run_all + end
    return inside, whole, jnp.exp(run_in)


def combine(state, weights, h):
    total = jnp.zeros((128, 128), F32)
    for j in range(8):
        total = total + weights[j][:, h : h + 1] * state[j, :, head(h)].astype(F32)
    return total


def whole_kernel(
    resid, teacher, gain_mix, gain_mlp, w_c, w_b, w_x, w_dt, bias, rate, skip, w_out, w_gate, w_up, out, *scratch
):
    s = SimpleNamespace(**dict(zip(SCRATCH, scratch)))
    me, y, z, c = place()
    m = me % 8
    t = lax.axis_index("tensor")
    top, low = pl.ds(0, T), pl.ds(T, T)
    pairs = (
        (w_gate, s.held.at[me, 0]),
        (w_up, s.held.at[me, 1]),
        (resid, s.nin),
        (w_c, s.v_wc),
        (w_b, s.v_wb),
        (w_x, s.v_wx),
        (w_dt, s.v_wdt),
        (teacher, s.lhs.at[top, :]),
        (w_out, s.v_out),
        (resid.at[:, columns(t)], s.v_resid),
    )
    loads = [pltpu.make_async_copy(a, b, s.in_sem.at[k]) for k, (a, b) in enumerate(pairs)]
    for copy in loads:
        copy.start()
    sem = pltpu.get_barrier_semaphore()
    for k in range(1, DP):
        pl.semaphore_signal(sem, inc=1, device_id={"dp": (me + k) % DP}, device_id_type=MESH)
    for k in range(1, TP):
        pl.semaphore_signal(sem, inc=1, device_id={"tensor": (t + k) % TP}, device_id_type=MESH)
    pl.semaphore_wait(sem, DP + TP - 2)
    loads[0].wait()
    loads[1].wait()
    gather = Gather(
        lambda j, start, size: s.held.at[j, :, pl.ds(start, size), :], ROWS, 112, 64, s.g_send, s.g_recv
    )
    gather.begin()

    bias_row, rate_row, skip_row = spread(bias), spread(rate), spread(skip)
    params = jnp.concatenate([bias_row, rate_row, skip_row, jnp.zeros((5, 128), F32)], axis=0)
    loads[2].wait()
    normalise(s.nin, slice(None), gain_mix)
    for copy in loads[3:7]:
        copy.wait()
    s.proj[...] = jnp.zeros_like(s.proj)

    def project(k, _):
        rows = s.nin[:, chunk(k)]
        s.proj[:, 0:512] += jnp.dot(rows, s.v_wc[chunk(k), :], preferred_element_type=F32)
        s.proj[:, 512:640] += jnp.dot(rows, s.v_wb[chunk(k), :], preferred_element_type=F32)
        s.proj[:, 640:768] += jnp.dot(rows, s.v_wx[chunk(k), :], preferred_element_type=F32)
        s.proj[:, 768 : 768 + HEADS] += mm_t(rows, s.v_wdt[:, chunk(k)])
        return 0

    lax.fori_loop(0, 16, project, 0)
    s.read[...] = s.proj[:, 0:512].astype(BF16)
    inject, values = s.proj[:, 512:640], s.proj[:, 640:768]
    raw = s.proj[:, 768:896]
    step, decay, step_t, decay_t = steps_of(raw, params)
    causal = iota(0) >= iota(1)
    inject_t = jnp.transpose(inject)
    for h in range(HEADS):
        row, col, step_row = decay_t[h : h + 1, :], decay[:, h : h + 1], step_t[h : h + 1, :]
        last = row[:, T - 1 : T]
        s.fade[h] = jnp.exp(jnp.where(causal, col - row, -1e30))
        s.plain[h] = s.fade[h] * mm_t(s.read[:, head(h)], inject)
        s.through[:, head(h)] = mm(s.plain[h] * step_row, values) + skip_row[:, h : h + 1] * values
        s.state[m, :, head(h)] = mm(inject_t * (jnp.exp(last - row) * step_row), values).astype(BF16)
    s.decays[m] = jnp.broadcast_to(decay[T - 1 : T, :], (8, 128))
    states = States(s.state, s.sums, s.s_send, s.s_recv)
    ends = States(s.decays, None, s.d_send, s.d_recv)
    ends.begin()
    states.begin()

    loads[7].wait()
    normalise(s.lhs, top, gain_mlp)

    def turn(k, _):
        s.nin_t[k] = jnp.transpose(s.nin[:, chunk(k)].astype(F32)).astype(BF16)
        return 0

    lax.fori_loop(0, DP, turn, 0)
    s.acc[...] = jnp.zeros_like(s.acc)
    ends.gathered()
    states.gathered()
    inside, whole, lead = state_weights(s.decays, m, True)
    for h in range(HEADS):
        s.sums[0, :, head(h)] = combine(s.state, whole, h).astype(BF16)
    states.across().start()
    states.across().wait_recv()
    after = (y == 1).astype(F32)
    for h in range(HEADS):
        total = combine(s.state, inside, h)
        total = total + (after * lead[:, h : h + 1]) * s.sums[1, :, head(h)].astype(F32)
        entering = total.astype(BF16)
        s.enter[:, head(h)] = entering
        grown = jnp.exp(decay[:, h : h + 1]) * mm(s.read[:, head(h)], entering)
        s.mixer_out[:, head(h)] = (s.through[:, head(h)] + grown).astype(BF16)

    def move(phase, k, src, dst):
        return pltpu.make_async_remote_copy(
            src_ref=src,
            dst_ref=dst,
            send_sem=s.t_send.at[phase, k - 1],
            recv_sem=s.t_recv.at[phase, k - 1],
            device_id={"tensor": (t + k) % TP},
            device_id_type=MESH,
        )

    def part_move(phase, k):
        return move(phase, k, s.p_send.at[k - 1], s.p_recv.at[k - 1])

    def out_part(p):
        return jnp.dot(s.mixer_out[...], s.v_out[:, columns(p)], preferred_element_type=F32)

    loads[8].wait()
    loads[9].wait()

    def out_send(k, _):
        s.p_send[k - 1] = out_part((t + k) % TP).astype(BF16)
        part_move(0, k).start()
        return 0

    lax.fori_loop(1, TP, out_send, 0)
    stream = out_part(t) + s.v_resid[...].astype(F32)
    gather.arrive("YO", "RQ", "LQ")
    gather.arrive("RO", "RA", "YL")
    gather.arrive("LO", "LB", "YR")
    for k in range(1, TP):
        part_move(0, k).wait_recv()
        stream = stream + s.p_recv[k - 1].astype(F32)
    s.strm[t] = stream.astype(BF16)
    for k in range(1, TP):
        move(1, k, s.strm.at[t], s.strm.at[t]).start()
    for k in range(1, TP):
        at = (t - k + TP) % TP
        move(1, k, s.strm.at[at], s.strm.at[at]).wait_recv()

    def square(p, total):
        part = s.strm[p].astype(F32)
        return total + jnp.sum(part * part, axis=1, keepdims=True)

    scale = lax.rsqrt(lax.fori_loop(0, TP, square, jnp.zeros((T, 1), F32)) / D + EPS)

    def write(p, _):
        s.lhs[low, columns(p)] = (s.strm[p].astype(F32) * scale * gain_mlp[:, columns(p)]).astype(BF16)
        return 0

    lax.fori_loop(0, TP, write, 0)

    def use(flip, dz):
        base = gather.block(flip, dz, 0)

        def one(n, _):
            at = chunk(n)
            first, second = s.lhs[:, chunk(base)], s.lhs[:, chunk(base + 1)]
            for g in range(2):
                s.acc[g, :, at] += jnp.dot(
                    first, s.held[base, g, :, at], preferred_element_type=F32
                ) + jnp.dot(second, s.held[base + 1, g, :, at], preferred_element_type=F32)
            return 0

        lax.fori_loop(0, HID // 256, one, 0)

    gather.side_arrive("own")
    use(0, 0)
    gather.side_arrive("YO")
    use(1, 0)
    gather.arrive("RQ", "RQA")
    gather.arrive("LQ", "LQB")
    gather.arrive("RA", "YO2")
    gather.arrive("LB")
    gather.side_arrive("RO")
    use(0, -1)
    gather.arrive("YL")
    gather.arrive("YR")
    gather.side_arrive("LO")
    use(0, 1)
    gather.side_arrive("RA", "LB")
    use(0, 2)
    gather.arrive("RQA")
    gather.arrive("LQB")
    gather.arrive("YO2")
    gather.side_arrive("RQ", "YL")
    use(1, -1)
    gather.side_arrive("LQ", "YR")
    use(1, 1)
    gather.side_arrive("RQA", "LQB", "YO2")
    use(1, 2)

    def column_copy(k):
        to = (me + k) % DP
        return pltpu.make_async_remote_copy(
            src_ref=s.nin_t.at[to],
            dst_ref=s.cols.at[me],
            send_sem=s.c_send.at[k - 1],
            recv_sem=s.c_recv.at[k - 1],
            device_id={"dp": to},
            device_id_type=MESH,
        )

    def column_landed(k):
        at = (me - k + DP) % DP
        return pltpu.make_async_remote_copy(
            src_ref=s.nin_t.at[at],
            dst_ref=s.cols.at[at],
            send_sem=s.c_send.at[k - 1],
            recv_sem=s.c_recv.at[k - 1],
            device_id={"dp": at},
            device_id_type=MESH,
        )

    for k in range(1, DP):
        column_copy(k).start()
    s.cols[me] = s.nin_t[me]

    def hidden(n, _):
        at = chunk(n)
        aim_gate = s.acc[0, top, at]
        aim = aim_gate * jax.nn.sigmoid(aim_gate) * s.acc[1, top, at]
        gate, up = s.acc[0, low, at], s.acc[1, low, at]
        sigma = jax.nn.sigmoid(gate)
        silu = gate * sigma
        grad = (2.0 / math.sqrt(FF)) * (silu * up - aim)
        s.g_gate[:, at] = (grad * up * sigma * (1.0 + gate * (1.0 - sigma))).astype(BF16)
        s.g_up[:, at] = (grad * silu).astype(BF16)
        return 0

    lax.fori_loop(0, HID // 256, hidden, 0)

    def back(p):
        return jnp.concatenate(
            [
                mm_t(s.g_gate[...], s.held[2 * p + i, 0]) + mm_t(s.g_up[...], s.held[2 * p + i, 1])
                for i in range(2)
            ],
            axis=1,
        )

    for k in range(1, TP):
        part_move(0, k).wait_send()

    def back_send(k, _):
        s.p_send[k - 1] = back((t + k) % TP).astype(BF16)
        part_move(2, k).start()
        return 0

    lax.fori_loop(1, TP, back_send, 0)
    mid = back(t)
    for k in range(1, TP):
        part_move(2, k).wait_recv()
        mid = mid + s.p_recv[k - 1].astype(F32)
    s.gained[t] = (mid * gain_mlp[:, columns(t)]).astype(BF16)
    for k in range(1, TP):
        move(3, k, s.gained.at[t], s.gained.at[t]).start()
    for k in range(1, TP):
        at = (t - k + TP) % TP
        move(3, k, s.gained.at[at], s.gained.at[at]).wait_recv()

    def product(p, total):
        return total + jnp.sum(s.gained[p].astype(F32) * s.strm[p].astype(F32), axis=1, keepdims=True)

    inner = lax.fori_loop(0, TP, product, jnp.zeros((T, 1), F32))
    pull = scale * scale * scale * (inner / D)
    s.out_grad[...] = jnp.zeros_like(s.out_grad)

    def unproject(p, _):
        delta = (s.gained[p].astype(F32) * scale - s.strm[p].astype(F32) * pull).astype(BF16)
        s.out_grad[...] += mm_t(delta, s.v_out[:, columns(p)])
        return 0

    lax.fori_loop(0, TP, unproject, 0)

    inject, values = s.proj[:, 512:640], s.proj[:, 640:768]
    raw = s.proj[:, 768:896]
    step, decay, step_t, decay_t = steps_of(raw, params)
    growth, growth_t = jnp.exp(decay), jnp.exp(decay_t)
    for h in range(HEADS):
        read_t = jnp.transpose(s.read[:, head(h)].astype(F32))
        s.b_state[m, :, head(h)] = mm(read_t * growth_t[h : h + 1, :], s.out_grad[:, head(h)]).astype(BF16)
    states_back = States(s.b_state, s.b_sums, s.b_send, s.b_recv)
    states_back.begin()
    lanes = lax.broadcasted_iota(jnp.int32, (1, 128), 1)
    s.dinject[...] = jnp.zeros_like(s.dinject)
    s.dvalue[...] = jnp.zeros_like(s.dvalue)
    step_rows, decay_rows, decay_cols = [], [], []
    for h in range(HEADS):
        step_row = step_t[h : h + 1, :]
        read_h, grad_h = s.read[:, head(h)], s.out_grad[:, head(h)]
        dweight = mm_t(grad_h, values)
        direct = dweight * s.plain[h]
        dscore = dweight * s.fade[h] * step_row
        weight = s.plain[h] * step_row
        through = mm_t(grad_h, s.enter[:, head(h)])
        s.dread[:, head(h)] = mm(dscore, inject) + growth[:, h : h + 1] * through
        s.dinject[...] += mm(jnp.transpose(dscore), read_h)
        s.dvalue[...] += mm(jnp.transpose(weight), grad_h) + skip_row[:, h : h + 1] * grad_h
        column = jnp.sum(direct, axis=0, keepdims=True)
        step_rows.append(column)
        decay_rows.append(-column * step_row)
        along = growth[:, h : h + 1] * jnp.sum(through * read_h.astype(F32), axis=1, keepdims=True)
        decay_cols.append(jnp.sum(direct * step_row, axis=1, keepdims=True) + along)
    states_back.gathered()
    inside, whole, lead = state_weights(s.decays, m, False)
    for h in range(HEADS):
        s.b_sums[0, :, head(h)] = combine(s.b_state, whole, h).astype(BF16)
    states_back.across().start()
    states_back.across().wait_recv()
    before = (y == 0).astype(F32)
    dstep = jnp.zeros((T, 128), F32)
    ddecay = jnp.zeros((T, 128), F32)
    for h in range(HEADS):
        behind = combine(s.b_state, inside, h)
        behind = behind + (before * lead[:, h : h + 1]) * s.b_sums[1, :, head(h)].astype(F32)
        tail_col = jnp.exp(decay[T - 1 : T, h : h + 1] - decay[:, h : h + 1])
        scaled_col = tail_col * step[:, h : h + 1]
        pulled = mm_t(values, behind)
        s.dinject[...] += scaled_col * pulled
        s.dvalue[...] += scaled_col * mm(inject, behind)
        drawn = tail_col * jnp.sum(inject * pulled, axis=1, keepdims=True)
        moved = drawn * step[:, h : h + 1]
        kept = jnp.exp(decay[T - 1 : T, h : h + 1]) * jnp.sum(
            jnp.sum(behind * s.enter[:, head(h)].astype(F32), axis=1, keepdims=True), axis=0, keepdims=True
        )
        end = kept + jnp.sum(moved, axis=0, keepdims=True)
        onehot = (lanes == h).astype(F32)
        final = (lax.broadcasted_iota(jnp.int32, (T, 1), 0) == T - 1).astype(F32)
        dstep = dstep + drawn * onehot
        ddecay = ddecay + (decay_cols[h] - moved + final * end) * onehot
    zero = jnp.zeros((128 - HEADS, 128), F32)
    dstep = dstep + jnp.transpose(jnp.concatenate(step_rows + [zero], axis=0))
    ddecay = ddecay + jnp.transpose(jnp.concatenate(decay_rows + [zero], axis=0))
    upper = (iota(0) <= iota(1)).astype(F32)
    later = jnp.dot(upper, ddecay, preferred_element_type=F32, precision=lax.Precision.HIGHEST)
    draw = (dstep - rate_row * later) * jax.nn.sigmoid(raw + bias_row)
    s.packed[me, :, 0:512] = s.dread[...].astype(BF16)
    s.packed[me, :, 512:640] = s.dinject[...].astype(BF16)
    s.packed[me, :, 640:768] = s.dvalue[...].astype(BF16)
    s.packed[me, :, 768:896] = draw.astype(BF16)

    last = Gather(lambda j, start, size: s.packed.at[j, pl.ds(start, size), :], T, 48, 48, s.h_send, s.h_recv)
    last.begin()
    out[...] = jnp.zeros_like(out)
    for k in range(1, DP):
        column_landed(k).wait_recv()

    def add(flip, dz):
        base = last.block(flip, dz, 0)
        out[...] += jnp.dot(s.cols[base], s.packed[base], preferred_element_type=F32) + jnp.dot(
            s.cols[base + 1], s.packed[base + 1], preferred_element_type=F32
        )

    last.arrive("YO", "RQ", "LQ")
    last.arrive("RO", "RA", "YL")
    last.arrive("LO", "LB", "YR")
    last.side_arrive("own")
    add(0, 0)
    last.side_arrive("YO")
    add(1, 0)
    last.arrive("RQ", "RQA")
    last.arrive("LQ", "LQB")
    last.arrive("RA", "YO2")
    last.arrive("LB")
    last.arrive("YL")
    last.arrive("YR")
    last.side_arrive("RO")
    add(0, -1)
    last.side_arrive("LO")
    add(0, 1)
    last.arrive("RQA")
    last.arrive("LQB")
    last.arrive("YO2")
    last.side_arrive("RA", "LB")
    add(0, 2)
    last.side_arrive("RQ", "YL")
    add(1, -1)
    last.side_arrive("LQ", "YR")
    add(1, 1)
    last.side_arrive("RQA", "LQB", "YO2")
    add(1, 2)

    gather.finish()
    last.finish()
    states.finish()
    states_back.finish()
    for k in range(1, 8):
        ends.peer(k).wait_send()
    for k in range(1, DP):
        column_copy(k).wait_send()
    for k in range(1, TP):
        move(1, k, s.strm.at[t], s.strm.at[t]).wait_send()
        part_move(2, k).wait_send()
        move(3, k, s.gained.at[t], s.gained.at[t]).wait_send()


def split_kernel(packed, grad_c, grad_b, grad_x, grad_dt):
    grad_c[...] = packed[:, 0:512]
    grad_b[...] = packed[:, 512:640]
    grad_x[...] = packed[:, 640:768]
    grad_dt[...] = packed[:, 768 : 768 + HEADS]


VM = pl.BlockSpec(memory_space=pltpu.VMEM)
SM = pl.BlockSpec(memory_space=pltpu.SMEM)
ANY = pl.BlockSpec(memory_space=pl.ANY)


def struct(shape, dtype):
    return jax.ShapeDtypeStruct(shape, dtype)


def local(
    resid, teacher_mixed, gain_mix, gain_mlp, w_c, w_b, w_x, w_dt, dt_bias, decay_rate, skip, w_out,
    w_gate, w_up,
):
    gain_mix, gain_mlp = gain_mix.reshape(1, D), gain_mlp.reshape(1, D)
    packed = pl.pallas_call(
        whole_kernel,
        out_shape=struct((ROWS, PACK), F32),
        in_specs=[ANY, ANY, VM, VM, ANY, ANY, ANY, ANY, SM, SM, SM, ANY, ANY, ANY],
        out_specs=VM,
        scratch_shapes=list(SCRATCH.values()),
        compiler_params=pltpu.CompilerParams(
            collective_id=0, has_side_effects=True, vmem_limit_bytes=63 * MIB
        ),
        name="whole",
    )(
        resid, teacher_mixed, gain_mix, gain_mlp, w_c, w_b, w_x, w_dt.T, dt_bias, decay_rate, skip, w_out,
        w_gate, w_up,
    )
    return pl.pallas_call(
        split_kernel,
        out_shape=(
            struct((ROWS, 512), F32),
            struct((ROWS, 128), F32),
            struct((ROWS, 128), F32),
            struct((ROWS, HEADS), F32),
        ),
        in_specs=[VM],
        out_specs=(VM,) * 4,
        name="split",
    )(packed)


def solution(mesh):
    in_specs = (
        P("dp", None),
        P("dp", None),
        P(),
        P(),
        P(None, "tensor"),
        P(None, "tensor"),
        P(None, "tensor"),
        P(None, "tensor"),
        P("tensor"),
        P("tensor"),
        P("tensor"),
        P("tensor", None),
        P("dp", "tensor"),
        P("dp", "tensor"),
    )
    out_specs = (P("dp", "tensor"), P("dp", "tensor"), P("dp", "tensor"), P("dp", "tensor"))
    return jax.shard_map(local, mesh=mesh, in_specs=in_specs, out_specs=out_specs, check_vma=False)
```

```python
import math
from types import SimpleNamespace

import jax
import jax.numpy as jnp
from jax import lax
from jax.experimental import pallas as pl
from jax.experimental.pallas import tpu as pltpu
from jax.sharding import PartitionSpec as P

D = 4096
FF = 14336
EPS = 1e-05
T = 128
HEADS = 4
DP = 16
TP = 8
HID = 1792
ROWS = 256
WIDTH = 512
PACK = 896
F32 = jnp.float32
BF16 = jnp.bfloat16
MESH = pl.DeviceIdType.MESH
MIB = 1024 * 1024

LEGS = {
    "RO": ("R", 0, 0, "full", 0, -1),
    "LO": ("L", 0, 0, "full", 0, 1),
    "YO": ("Y", 0, 0, "full", 1, 0),
    "RQ": ("R", 1, 0, "Q", 1, -1),
    "LQ": ("L", 1, 0, "Q", 1, 1),
    "RA": ("R", 0, -1, "A", 0, 2),
    "LB": ("L", 0, 1, "B", 0, 2),
    "YL": ("Y", 0, -1, "P", 1, -1),
    "YR": ("Y", 0, 1, "P", 1, 1),
    "RQA": ("R", 1, -1, "QA", 1, 2),
    "LQB": ("L", 1, 1, "QB", 1, 2),
    "YO2": ("Y", 0, 2, "P", 1, 2),
}
HALVES = {
    "RO1": ("R", 0, 0, "A", 0, -1),
    "RO2": ("R", 0, 0, "B", 0, -1),
    "LO1": ("L", 0, 0, "A", 0, 1),
    "LO2": ("L", 0, 0, "B", 0, 1),
    "YO1": ("Y", 0, 0, "A", 1, 0),
    "YO2": ("Y", 0, 0, "B", 1, 0),
    "RX1": ("R", 1, 0, "A", 1, -1),
    "RX2": ("R", 1, 0, "B", 1, -1),
    "LX1": ("L", 1, 0, "A", 1, 1),
    "LX2": ("L", 1, 0, "B", 1, 1),
    "RA": ("R", 0, -1, "A", 0, 2),
    "LB": ("L", 0, 1, "B", 0, 2),
    "RXA": ("R", 1, -1, "A", 1, 2),
    "LXB": ("L", 1, 1, "B", 1, 2),
}
NSEM = 2 * len(LEGS) + 1
NSEM_HALF = 2 * len(HALVES) + 1


def place():
    me = lax.axis_index("dp")
    return me, me // 8, (me % 8) // 2, me % 2


class Gather:
    def __init__(self, legs, piece, rows, p, qa, send, recv, give=None):
        self.legs, self.order = legs, list(legs)
        self.piece, self.send, self.recv, self.give = piece, send, recv, give
        self.me, self.y, self.z, self.c = place()
        half = rows // 2
        self.rows = {
            "full": (0, rows),
            "P": (0, p),
            "Q": (p, rows - p),
            "A": (0, half),
            "B": (half, rows - half),
            "QA": (p, qa),
            "QB": (p + qa, rows - p - qa),
        }

    def block(self, flip, dz, core):
        y = (1 - self.y) if flip else self.y
        return y * 8 + ((self.z + dz + 4) % 4) * 2 + core

    def target(self, name):
        if name == "R":
            return self.block(0, 1, self.c)
        if name == "L":
            return self.block(0, -1, self.c)
        if name == "Y":
            return self.block(1, 0, self.c)
        return self.block(0, 0, 1 - self.c)

    def copy(self, src, ref, sem, to):
        return pltpu.make_async_remote_copy(
            src_ref=src,
            dst_ref=ref,
            send_sem=self.send.at[sem],
            recv_sem=self.recv.at[sem],
            device_id={"dp": to},
            device_id_type=MESH,
        )

    def leg(self, name):
        to, flip, dz, rows, _, _ = self.legs[name]
        ref = self.piece(self.block(flip, dz, self.c), *self.rows[rows])
        src = ref
        if to == "Y" and self.give is not None:
            src = self.give(*self.rows[rows])
        return self.copy(src, ref, self.order.index(name), self.target(to))

    def landed(self, name):
        to, _, _, rows, flip, dz = self.legs[name]
        ref = self.piece(self.block(flip, dz, self.c), *self.rows[rows])
        return self.copy(ref, ref, self.order.index(name), self.target(to))

    def side(self, name, core):
        if name == "own":
            flip, dz, rows, sem = 0, 0, "full", len(self.order)
        else:
            _, _, _, rows, flip, dz = self.legs[name]
            sem = len(self.order) + 1 + self.order.index(name)
        ref = self.piece(self.block(flip, dz, core), *self.rows[rows])
        return self.copy(ref, ref, sem, self.target("S"))

    def begin(self, *names):
        for name in names:
            self.leg(name).start()
        self.side("own", self.c).start()

    def arrive(self, name, *then):
        self.landed(name).wait_recv()
        for other in then:
            self.leg(other).start()
        self.side(name, self.c).start()

    def side_arrive(self, *names):
        for name in names:
            self.side(name, 1 - self.c).wait_recv()

    def finish(self):
        for name in self.order:
            self.leg(name).wait_send()
        for name in ["own"] + self.order:
            self.side(name, self.c).wait_send()


def iota(axis):
    return lax.broadcasted_iota(jnp.int32, (T, T), axis)


def mm(a, b):
    return jnp.dot(a.astype(BF16), b.astype(BF16), preferred_element_type=F32)


def mm_t(a, b):
    return lax.dot_general(
        a.astype(BF16), b.astype(BF16), (((1,), (1,)), ((), ())), preferred_element_type=F32
    )


def softplus(v):
    return jnp.maximum(v, 0.0) + jnp.log1p(jnp.exp(-jnp.abs(v)))


def steps_of(raw, params):
    step = softplus(raw + params[0:1, :])
    lower = (iota(0) >= iota(1)).astype(F32)
    decay = jnp.dot(
        lower, -step * params[1:2, :], preferred_element_type=F32, precision=lax.Precision.HIGHEST
    )
    return step, decay, jnp.transpose(step), jnp.transpose(decay)


def head(k):
    return slice(k * 128, (k + 1) * 128)


class States:
    def __init__(self, slots, sums, send, recv):
        self.slots, self.sums, self.send, self.recv = slots, sums, send, recv
        self.me, self.y, self.z, self.c = place()
        self.m = self.me % 8

    def peer(self, k):
        at = (self.m + k) % 8
        return pltpu.make_async_remote_copy(
            src_ref=self.slots.at[self.m],
            dst_ref=self.slots.at[self.m],
            send_sem=self.send.at[k - 1],
            recv_sem=self.recv.at[k - 1],
            device_id={"dp": self.y * 8 + at},
            device_id_type=MESH,
        )

    def from_peer(self, k):
        at = (self.m - k + 8) % 8
        return pltpu.make_async_remote_copy(
            src_ref=self.slots.at[at],
            dst_ref=self.slots.at[at],
            send_sem=self.send.at[k - 1],
            recv_sem=self.recv.at[k - 1],
            device_id={"dp": self.y * 8 + at},
            device_id_type=MESH,
        )

    def across(self):
        return pltpu.make_async_remote_copy(
            src_ref=self.sums.at[0],
            dst_ref=self.sums.at[1],
            send_sem=self.send.at[7],
            recv_sem=self.recv.at[7],
            device_id={"dp": (1 - self.y) * 8 + self.m},
            device_id_type=MESH,
        )

    def begin(self):
        for k in range(1, 8):
            self.peer(k).start()

    def gathered(self):
        for k in range(1, 8):
            self.from_peer(k).wait_recv()

    def finish(self):
        for k in range(1, 8):
            self.peer(k).wait_send()
        self.across().wait_send()


def spread(scalars):
    lane = lax.broadcasted_iota(jnp.int32, (1, 128), 1)
    row = jnp.zeros((1, 128), F32)
    for h in range(HEADS):
        row = jnp.where(lane == h, scalars[h], row)
    return row


SCRATCH = {
    "held": pltpu.VMEM((DP, ROWS, HID), BF16),
    "give": pltpu.VMEM((ROWS, HID), BF16),
    "v_wc": pltpu.VMEM((D, 512), BF16),
    "v_wb": pltpu.VMEM((D, 128), BF16),
    "v_wx": pltpu.VMEM((D, 128), BF16),
    "v_wdt": pltpu.VMEM((HEADS, D), BF16),
    "v_out": pltpu.VMEM((512, D), BF16),
    "v_resid": pltpu.VMEM((T, WIDTH), BF16),
    "nin": pltpu.VMEM((T, D), BF16),
    "nin_t": pltpu.VMEM((DP, 256, T), BF16),
    "cols": pltpu.VMEM((DP, 256, T), BF16),
    "lhs": pltpu.VMEM((4 * T, D), BF16),
    "acc": pltpu.VMEM((4 * T, HID), F32),
    "proj": pltpu.VMEM((T, PACK), F32),
    "read": pltpu.VMEM((T, WIDTH), BF16),
    "state": pltpu.VMEM((8, 128, WIDTH), BF16),
    "sums": pltpu.VMEM((2, 128, WIDTH), BF16),
    "decays": pltpu.VMEM((8, 8, 128), F32),
    "enter": pltpu.VMEM((128, WIDTH), BF16),
    "through": pltpu.VMEM((T, WIDTH), F32),
    "mixer_out": pltpu.VMEM((T, WIDTH), BF16),
    "fade": pltpu.VMEM((HEADS, T, T), F32),
    "plain": pltpu.VMEM((HEADS, T, T), F32),
    "p_send": pltpu.VMEM((2, TP, T, WIDTH), BF16),
    "p_recv": pltpu.VMEM((2, TP, T, WIDTH), BF16),
    "strm": pltpu.VMEM((2, TP, T, WIDTH), BF16),
    "gained": pltpu.VMEM((TP, T, WIDTH), BF16),
    "grads": pltpu.VMEM((2 * T, HID), BF16),
    "out_grad": pltpu.VMEM((T, WIDTH), F32),
    "b_state": pltpu.VMEM((8, 128, WIDTH), BF16),
    "b_sums": pltpu.VMEM((2, 128, WIDTH), BF16),
    "packed": pltpu.VMEM((DP, T, PACK), BF16),
    "dread": pltpu.VMEM((T, WIDTH), F32),
    "dinject": pltpu.VMEM((T, 128), F32),
    "dvalue": pltpu.VMEM((T, 128), F32),
    "in_sem": pltpu.SemaphoreType.DMA((12,)),
    "g_send": pltpu.SemaphoreType.DMA((NSEM_HALF,)),
    "g_recv": pltpu.SemaphoreType.DMA((NSEM_HALF,)),
    "a_send": pltpu.SemaphoreType.DMA((2,)),
    "a_recv": pltpu.SemaphoreType.DMA((2,)),
    "h_send": pltpu.SemaphoreType.DMA((NSEM,)),
    "h_recv": pltpu.SemaphoreType.DMA((NSEM,)),
    "s_send": pltpu.SemaphoreType.DMA((8,)),
    "s_recv": pltpu.SemaphoreType.DMA((8,)),
    "d_send": pltpu.SemaphoreType.DMA((8,)),
    "d_recv": pltpu.SemaphoreType.DMA((8,)),
    "b_send": pltpu.SemaphoreType.DMA((8,)),
    "b_recv": pltpu.SemaphoreType.DMA((8,)),
    "c_send": pltpu.SemaphoreType.DMA((DP - 1,)),
    "c_recv": pltpu.SemaphoreType.DMA((DP - 1,)),
    "t_send": pltpu.SemaphoreType.DMA((4, DP)),
    "t_recv": pltpu.SemaphoreType.DMA((4, DP)),
}


def chunk(k, size=256):
    return pl.ds(pl.multiple_of(k * size, size), size)


def columns(p):
    return chunk(p, WIDTH)


def normalise(ref, rows, gain):
    def square(k, total):
        part = ref[rows, chunk(k)].astype(F32)
        return total + jnp.sum(part * part, axis=1, keepdims=True)

    scale = lax.rsqrt(lax.fori_loop(0, 16, square, jnp.zeros((T, 1), F32)) / D + EPS)

    def write(k, _):
        ref[rows, chunk(k)] = (ref[rows, chunk(k)].astype(F32) * scale * gain[:, chunk(k)]).astype(BF16)
        return 0

    lax.fori_loop(0, 16, write, 0)


def state_weights(decays, m, forward):
    run_in, run_all = jnp.zeros((1, 128), F32), jnp.zeros((1, 128), F32)
    inside, whole = [None] * 8, [None] * 8
    for j in reversed(range(8)) if forward else range(8):
        reached = ((j < m) if forward else (j > m)).astype(F32)
        inside[j] = reached * jnp.exp(run_in)
        whole[j] = jnp.exp(run_all)
        end = decays[j, 0:1, :]
        run_in = run_in + reached * end
        run_all = run_all + end
    return inside, whole, jnp.exp(run_in)


def combine(state, weights, h):
    total = jnp.zeros((128, 128), F32)
    for j in range(8):
        total = total + weights[j][:, h : h + 1] * state[j, :, head(h)].astype(F32)
    return total


def whole_kernel(
    resid, teacher, gain_mix, gain_mlp, w_c, w_b, w_x, w_dt, bias, rate, skip, w_out, w_gate, w_up, out, *scratch
):
    s = SimpleNamespace(**dict(zip(SCRATCH, scratch)))
    me, y, z, c = place()
    m = me % 8
    t = lax.axis_index("tensor")
    other = (1 - y) * 8 + m
    half = HID // 2
    keep = pl.ds(pl.multiple_of(y * half, 128), half)
    rest = pl.ds(pl.multiple_of((1 - y) * half, 128), half)
    mine = pl.ds(pl.multiple_of(y * T, T), T)
    pairs = (
        (w_gate.at[:, keep], s.held.at[me, :, 0:half]),
        (w_up.at[:, keep], s.held.at[me, :, half:HID]),
        (w_gate.at[:, rest], s.give.at[:, 0:half]),
        (w_up.at[:, rest], s.give.at[:, half:HID]),
        (resid, s.nin),
        (w_c, s.v_wc),
        (w_b, s.v_wb),
        (w_x, s.v_wx),
        (w_dt, s.v_wdt),
        (teacher, s.lhs.at[mine, :]),
        (w_out, s.v_out),
        (resid.at[:, columns(t)], s.v_resid),
    )
    loads = [pltpu.make_async_copy(a, b, s.in_sem.at[k]) for k, (a, b) in enumerate(pairs)]
    for copy in loads:
        copy.start()
    sem = pltpu.get_barrier_semaphore()
    for k in range(1, DP):
        pl.semaphore_signal(sem, inc=1, device_id={"dp": (me + k) % DP}, device_id_type=MESH)
    for k in range(1, TP):
        for dp in (me, other):
            pl.semaphore_signal(
                sem, inc=1, device_id={"dp": dp, "tensor": (t + k) % TP}, device_id_type=MESH
            )
    pl.semaphore_wait(sem, DP - 1 + 2 * (TP - 1))
    for copy in loads[0:4]:
        copy.wait()
    gather = Gather(
        HALVES,
        lambda j, start, size: s.held.at[j, pl.ds(start, size), :],
        ROWS,
        112,
        64,
        s.g_send,
        s.g_recv,
        lambda start, size: s.give.at[pl.ds(start, size), :],
    )
    gather.begin("RO1", "LO2", "YO1", "YO2")

    bias_row, rate_row, skip_row = spread(bias), spread(rate), spread(skip)
    params = jnp.concatenate([bias_row, rate_row, skip_row, jnp.zeros((5, 128), F32)], axis=0)
    loads[4].wait()
    normalise(s.nin, slice(None), gain_mix)
    for copy in loads[5:9]:
        copy.wait()
    s.proj[...] = jnp.zeros_like(s.proj)

    def project(k, _):
        rows = s.nin[:, chunk(k)]
        s.proj[:, 0:512] += jnp.dot(rows, s.v_wc[chunk(k), :], preferred_element_type=F32)
        s.proj[:, 512:640] += jnp.dot(rows, s.v_wb[chunk(k), :], preferred_element_type=F32)
        s.proj[:, 640:768] += jnp.dot(rows, s.v_wx[chunk(k), :], preferred_element_type=F32)
        s.proj[:, 768 : 768 + HEADS] += mm_t(rows, s.v_wdt[:, chunk(k)])
        return 0

    lax.fori_loop(0, 16, project, 0)
    s.read[...] = s.proj[:, 0:512].astype(BF16)
    inject, values = s.proj[:, 512:640], s.proj[:, 640:768]
    raw = s.proj[:, 768:896]
    step, decay, step_t, decay_t = steps_of(raw, params)
    causal = iota(0) >= iota(1)
    inject_t = jnp.transpose(inject)
    for h in range(HEADS):
        row, col, step_row = decay_t[h : h + 1, :], decay[:, h : h + 1], step_t[h : h + 1, :]
        last = row[:, T - 1 : T]
        s.fade[h] = jnp.exp(jnp.where(causal, col - row, -1e30))
        s.plain[h] = s.fade[h] * mm_t(s.read[:, head(h)], inject)
        s.through[:, head(h)] = mm(s.plain[h] * step_row, values) + skip_row[:, h : h + 1] * values
        s.state[m, :, head(h)] = mm(inject_t * (jnp.exp(last - row) * step_row), values).astype(BF16)
    s.decays[m] = jnp.broadcast_to(decay[T - 1 : T, :], (8, 128))
    states = States(s.state, s.sums, s.s_send, s.s_recv)
    ends = States(s.decays, None, s.d_send, s.d_recv)
    ends.begin()
    states.begin()
    gather.leg("RO2").start()
    gather.leg("LO1").start()

    loads[9].wait()
    normalise(s.lhs, mine, gain_mlp)
    gather.arrive("RO1", "RA")
    gather.arrive("LO2", "LB")
    gather.arrive("YO1", "RX1")
    gather.arrive("YO2", "LX2", "RX2", "LX1")

    def teacher_move(k):
        ref = s.lhs.at[pl.ds(pl.multiple_of(y * T + k * (T // 2), T // 2), T // 2), :]
        return pltpu.make_async_remote_copy(
            src_ref=ref,
            dst_ref=ref,
            send_sem=s.a_send.at[k],
            recv_sem=s.a_recv.at[k],
            device_id={"dp": other},
            device_id_type=MESH,
        )

    def teacher_landed(k):
        ref = s.lhs.at[pl.ds(pl.multiple_of((1 - y) * T + k * (T // 2), T // 2), T // 2), :]
        return pltpu.make_async_remote_copy(
            src_ref=ref,
            dst_ref=ref,
            send_sem=s.a_send.at[k],
            recv_sem=s.a_recv.at[k],
            device_id={"dp": other},
            device_id_type=MESH,
        )

    teacher_move(0).start()
    ends.gathered()
    states.gathered()
    inside, whole, lead = state_weights(s.decays, m, True)
    for h in range(HEADS):
        s.sums[0, :, head(h)] = combine(s.state, whole, h).astype(BF16)
    states.across().start()
    states.across().wait_recv()
    after = (y == 1).astype(F32)
    for h in range(HEADS):
        total = combine(s.state, inside, h)
        total = total + (after * lead[:, h : h + 1]) * s.sums[1, :, head(h)].astype(F32)
        entering = total.astype(BF16)
        s.enter[:, head(h)] = entering
        grown = jnp.exp(decay[:, h : h + 1]) * mm(s.read[:, head(h)], entering)
        s.mixer_out[:, head(h)] = (s.through[:, head(h)] + grown).astype(BF16)

    def move(phase, ky, kt, src, dst):
        return pltpu.make_async_remote_copy(
            src_ref=src,
            dst_ref=dst,
            send_sem=s.t_send.at[phase, ky * TP + kt],
            recv_sem=s.t_recv.at[phase, ky * TP + kt],
            device_id={"dp": other if ky else me, "tensor": (t + kt) % TP},
            device_id_type=MESH,
        )

    def out_move(kt):
        return move(0, 0, kt, s.p_send.at[0, kt], s.p_recv.at[0, kt])

    def stream_move(ky, kt):
        return move(1, ky, kt, s.strm.at[y, t], s.strm.at[y, t])

    def stream_landed(ky, kt):
        at = s.strm.at[(1 - y) if ky else y, (t - kt + TP) % TP]
        return move(1, ky, kt, at, at)

    def mid_move(ky, kt):
        return move(2, ky, kt, s.p_send.at[(1 - y) if ky else y, kt], s.p_recv.at[ky, kt])

    def gained_move(kt):
        return move(3, 0, kt, s.gained.at[t], s.gained.at[t])

    def gained_landed(kt):
        at = s.gained.at[(t - kt + TP) % TP]
        return move(3, 0, kt, at, at)

    peers = [(ky, kt) for kt in range(TP) for ky in range(2) if ky + kt > 0]

    def out_part(p):
        return jnp.dot(s.mixer_out[...], s.v_out[:, columns(p)], preferred_element_type=F32)

    loads[10].wait()
    loads[11].wait()

    def out_send(k, _):
        s.p_send[0, k] = out_part((t + k) % TP).astype(BF16)
        out_move(k).start()
        return 0

    lax.fori_loop(1, TP, out_send, 0)
    teacher_move(1).start()
    stream = out_part(t) + s.v_resid[...].astype(F32)
    gather.arrive("RO2")
    gather.arrive("LO1")
    for k in range(1, TP):
        out_move(k).wait_recv()
        stream = stream + s.p_recv[0, k].astype(F32)
    s.strm[y, t] = stream.astype(BF16)
    for ky, kt in peers:
        stream_move(ky, kt).start()

    upper_rows, lower_rows = pl.ds(0, 2 * T), pl.ds(2 * T, 2 * T)

    def use(flip, dz):
        base = gather.block(flip, dz, 0)

        def one(n, _):
            at = chunk(n)
            s.acc[upper_rows, at] += jnp.dot(
                s.lhs[upper_rows, chunk(base)], s.held[base, :, at], preferred_element_type=F32
            ) + jnp.dot(
                s.lhs[upper_rows, chunk(base + 1)], s.held[base + 1, :, at], preferred_element_type=F32
            )
            return 0

        lax.fori_loop(0, HID // 256, one, 0)

    def turn(k, _):
        s.nin_t[k] = jnp.transpose(s.nin[:, chunk(k)].astype(F32)).astype(BF16)
        return 0

    lax.fori_loop(0, DP, turn, 0)
    s.acc[upper_rows, :] = jnp.zeros((2 * T, HID), F32)
    gather.arrive("RX1", "RXA")
    gather.arrive("LX2", "LXB")
    gather.arrive("RA")
    gather.arrive("LB")
    teacher_landed(0).wait_recv()
    teacher_landed(1).wait_recv()
    gather.side_arrive("own")
    use(0, 0)
    gather.side_arrive("YO1", "YO2")
    use(1, 0)
    gather.side_arrive("RO1", "RO2")
    use(0, -1)
    gather.side_arrive("LO1", "LO2")
    use(0, 1)
    gather.side_arrive("RA", "LB")
    use(0, 2)
    gather.arrive("RX2")
    gather.arrive("LX1")
    gather.side_arrive("RX1", "RX2")
    use(1, -1)
    gather.side_arrive("LX1", "LX2")
    use(1, 1)
    for ky, kt in peers:
        stream_landed(ky, kt).wait_recv()

    def square(p, totals):
        parts = [s.strm[yy, p].astype(F32) for yy in range(2)]
        return tuple(
            total + jnp.sum(part * part, axis=1, keepdims=True) for total, part in zip(totals, parts)
        )

    none = jnp.zeros((T, 1), F32)
    squares = lax.fori_loop(0, TP, square, (none, none))
    scales = [lax.rsqrt(total / D + EPS) for total in squares]
    scale = jnp.where(y == 0, scales[0], scales[1])

    def write(p, _):
        for yy in range(2):
            s.lhs[pl.ds((2 + yy) * T, T), columns(p)] = (
                s.strm[yy, p].astype(F32) * scales[yy] * gain_mlp[:, columns(p)]
            ).astype(BF16)
        return 0

    lax.fori_loop(0, TP, write, 0)
    gather.arrive("RXA")
    gather.arrive("LXB")
    gather.side_arrive("RXA", "LXB")
    use(1, 2)

    def student(n, _):
        at = chunk(n)
        total = jnp.zeros((2 * T, 256), F32)
        for j in range(DP):
            total = total + jnp.dot(
                s.lhs[lower_rows, pl.ds(j * 256, 256)], s.held[j, :, at], preferred_element_type=F32
            )
        s.acc[lower_rows, at] = total
        return 0

    lax.fori_loop(0, HID // 256, student, 0)

    def column_copy(k):
        to = (me + k) % DP
        return pltpu.make_async_remote_copy(
            src_ref=s.nin_t.at[to],
            dst_ref=s.cols.at[me],
            send_sem=s.c_send.at[k - 1],
            recv_sem=s.c_recv.at[k - 1],
            device_id={"dp": to},
            device_id_type=MESH,
        )

    def column_landed(k):
        at = (me - k + DP) % DP
        return pltpu.make_async_remote_copy(
            src_ref=s.nin_t.at[at],
            dst_ref=s.cols.at[at],
            send_sem=s.c_send.at[k - 1],
            recv_sem=s.c_recv.at[k - 1],
            device_id={"dp": at},
            device_id_type=MESH,
        )

    def hidden(n, _):
        at, beside = chunk(n, 128), pl.ds(pl.multiple_of(half + n * 128, 128), 128)
        aim_gate = s.acc[upper_rows, at]
        aim = aim_gate * jax.nn.sigmoid(aim_gate) * s.acc[upper_rows, beside]
        gate, up = s.acc[lower_rows, at], s.acc[lower_rows, beside]
        sigma = jax.nn.sigmoid(gate)
        silu = gate * sigma
        grad = (2.0 / math.sqrt(FF)) * (silu * up - aim)
        s.grads[:, at] = (grad * up * sigma * (1.0 + gate * (1.0 - sigma))).astype(BF16)
        s.grads[:, beside] = (grad * silu).astype(BF16)
        return 0

    lax.fori_loop(0, half // 128, hidden, 0)

    for k in range(1, TP):
        out_move(k).wait_send()

    def back(kt):
        p = (t + kt) % TP
        for i in range(2):
            part = mm_t(s.grads[...], s.held[2 * p + i]).astype(BF16)
            for yy in range(2):
                s.p_send[yy, kt, :, i * 256 : (i + 1) * 256] = part[yy * T : (yy + 1) * T, :]

    def back_send(kt, _):
        back(kt)
        mid_move(0, kt).start()
        mid_move(1, kt).start()
        return 0

    lax.fori_loop(1, TP, back_send, 0)
    back(0)
    mid_move(1, 0).start()
    for k in range(1, DP):
        column_copy(k).start()
    s.cols[me] = s.nin_t[me]
    mid = s.p_send[y, 0].astype(F32)
    for ky, kt in peers:
        mid_move(ky, kt).wait_recv()
        mid = mid + s.p_recv[ky, kt].astype(F32)
    s.gained[t] = (mid * gain_mlp[:, columns(t)]).astype(BF16)
    for k in range(1, TP):
        gained_move(k).start()
    for k in range(1, TP):
        gained_landed(k).wait_recv()

    def product(p, total):
        return total + jnp.sum(s.gained[p].astype(F32) * s.strm[y, p].astype(F32), axis=1, keepdims=True)

    inner = lax.fori_loop(0, TP, product, jnp.zeros((T, 1), F32))
    pull = scale * scale * scale * (inner / D)
    s.out_grad[...] = jnp.zeros_like(s.out_grad)

    def unproject(p, _):
        delta = (s.gained[p].astype(F32) * scale - s.strm[y, p].astype(F32) * pull).astype(BF16)
        s.out_grad[...] += mm_t(delta, s.v_out[:, columns(p)])
        return 0

    lax.fori_loop(0, TP, unproject, 0)

    inject, values = s.proj[:, 512:640], s.proj[:, 640:768]
    raw = s.proj[:, 768:896]
    step, decay, step_t, decay_t = steps_of(raw, params)
    growth, growth_t = jnp.exp(decay), jnp.exp(decay_t)
    for h in range(HEADS):
        read_t = jnp.transpose(s.read[:, head(h)].astype(F32))
        s.b_state[m, :, head(h)] = mm(read_t * growth_t[h : h + 1, :], s.out_grad[:, head(h)]).astype(BF16)
    states_back = States(s.b_state, s.b_sums, s.b_send, s.b_recv)
    states_back.begin()
    lanes = lax.broadcasted_iota(jnp.int32, (1, 128), 1)
    s.dinject[...] = jnp.zeros_like(s.dinject)
    s.dvalue[...] = jnp.zeros_like(s.dvalue)
    step_rows, decay_rows, decay_cols = [], [], []
    for h in range(HEADS):
        step_row = step_t[h : h + 1, :]
        read_h, grad_h = s.read[:, head(h)], s.out_grad[:, head(h)]
        dweight = mm_t(grad_h, values)
        direct = dweight * s.plain[h]
        dscore = dweight * s.fade[h] * step_row
        weight = s.plain[h] * step_row
        through = mm_t(grad_h, s.enter[:, head(h)])
        s.dread[:, head(h)] = mm(dscore, inject) + growth[:, h : h + 1] * through
        s.dinject[...] += mm(jnp.transpose(dscore), read_h)
        s.dvalue[...] += mm(jnp.transpose(weight), grad_h) + skip_row[:, h : h + 1] * grad_h
        column = jnp.sum(direct, axis=0, keepdims=True)
        step_rows.append(column)
        decay_rows.append(-column * step_row)
        along = growth[:, h : h + 1] * jnp.sum(through * read_h.astype(F32), axis=1, keepdims=True)
        decay_cols.append(jnp.sum(direct * step_row, axis=1, keepdims=True) + along)
    states_back.gathered()
    inside, whole, lead = state_weights(s.decays, m, False)
    for h in range(HEADS):
        s.b_sums[0, :, head(h)] = combine(s.b_state, whole, h).astype(BF16)
    states_back.across().start()
    states_back.across().wait_recv()
    before = (y == 0).astype(F32)
    dstep = jnp.zeros((T, 128), F32)
    ddecay = jnp.zeros((T, 128), F32)
    for h in range(HEADS):
        behind = combine(s.b_state, inside, h)
        behind = behind + (before * lead[:, h : h + 1]) * s.b_sums[1, :, head(h)].astype(F32)
        tail_col = jnp.exp(decay[T - 1 : T, h : h + 1] - decay[:, h : h + 1])
        scaled_col = tail_col * step[:, h : h + 1]
        pulled = mm_t(values, behind)
        s.dinject[...] += scaled_col * pulled
        s.dvalue[...] += scaled_col * mm(inject, behind)
        drawn = tail_col * jnp.sum(inject * pulled, axis=1, keepdims=True)
        moved = drawn * step[:, h : h + 1]
        kept = jnp.exp(decay[T - 1 : T, h : h + 1]) * jnp.sum(
            jnp.sum(behind * s.enter[:, head(h)].astype(F32), axis=1, keepdims=True), axis=0, keepdims=True
        )
        end = kept + jnp.sum(moved, axis=0, keepdims=True)
        onehot = (lanes == h).astype(F32)
        final = (lax.broadcasted_iota(jnp.int32, (T, 1), 0) == T - 1).astype(F32)
        dstep = dstep + drawn * onehot
        ddecay = ddecay + (decay_cols[h] - moved + final * end) * onehot
    zero = jnp.zeros((128 - HEADS, 128), F32)
    dstep = dstep + jnp.transpose(jnp.concatenate(step_rows + [zero], axis=0))
    ddecay = ddecay + jnp.transpose(jnp.concatenate(decay_rows + [zero], axis=0))
    upper = (iota(0) <= iota(1)).astype(F32)
    later = jnp.dot(upper, ddecay, preferred_element_type=F32, precision=lax.Precision.HIGHEST)
    draw = (dstep - rate_row * later) * jax.nn.sigmoid(raw + bias_row)
    s.packed[me, :, 0:512] = s.dread[...].astype(BF16)
    s.packed[me, :, 512:640] = s.dinject[...].astype(BF16)
    s.packed[me, :, 640:768] = s.dvalue[...].astype(BF16)
    s.packed[me, :, 768:896] = draw.astype(BF16)

    last = Gather(
        LEGS, lambda j, start, size: s.packed.at[j, pl.ds(start, size), :], T, 48, 48, s.h_send, s.h_recv
    )
    last.begin("RO", "LO", "YO")
    out[...] = jnp.zeros_like(out)
    for k in range(1, DP):
        column_landed(k).wait_recv()

    def add(flip, dz):
        base = last.block(flip, dz, 0)
        out[...] += jnp.dot(s.cols[base], s.packed[base], preferred_element_type=F32) + jnp.dot(
            s.cols[base + 1], s.packed[base + 1], preferred_element_type=F32
        )

    last.arrive("YO", "RQ", "LQ")
    last.arrive("RO", "RA", "YL")
    last.arrive("LO", "LB", "YR")
    last.side_arrive("own")
    add(0, 0)
    last.side_arrive("YO")
    add(1, 0)
    last.arrive("RQ", "RQA")
    last.arrive("LQ", "LQB")
    last.arrive("RA", "YO2")
    last.arrive("LB")
    last.arrive("YL")
    last.arrive("YR")
    last.side_arrive("RO")
    add(0, -1)
    last.side_arrive("LO")
    add(0, 1)
    last.arrive("RQA")
    last.arrive("LQB")
    last.arrive("YO2")
    last.side_arrive("RA", "LB")
    add(0, 2)
    last.side_arrive("RQ", "YL")
    add(1, -1)
    last.side_arrive("LQ", "YR")
    add(1, 1)
    last.side_arrive("RQA", "LQB", "YO2")
    add(1, 2)

    gather.finish()
    last.finish()
    states.finish()
    states_back.finish()
    for k in range(1, 8):
        ends.peer(k).wait_send()
    for k in range(1, DP):
        column_copy(k).wait_send()
    for k in range(2):
        teacher_move(k).wait_send()
    for ky, kt in peers:
        stream_move(ky, kt).wait_send()
        mid_move(ky, kt).wait_send()
    for k in range(1, TP):
        gained_move(k).wait_send()


def split_kernel(packed, grad_c, grad_b, grad_x, grad_dt):
    grad_c[...] = packed[:, 0:512]
    grad_b[...] = packed[:, 512:640]
    grad_x[...] = packed[:, 640:768]
    grad_dt[...] = jnp.transpose(packed[:, 768:896])[0:HEADS, :]


VM = pl.BlockSpec(memory_space=pltpu.VMEM)
SM = pl.BlockSpec(memory_space=pltpu.SMEM)
ANY = pl.BlockSpec(memory_space=pl.ANY)


def struct(shape, dtype):
    return jax.ShapeDtypeStruct(shape, dtype)


def local(
    resid, teacher_mixed, gain_mix, gain_mlp, w_c, w_b, w_x, w_dt, dt_bias, decay_rate, skip, w_out,
    w_gate, w_up,
):
    gain_mix, gain_mlp = gain_mix.reshape(1, D), gain_mlp.reshape(1, D)
    packed = pl.pallas_call(
        whole_kernel,
        out_shape=struct((ROWS, PACK), F32),
        in_specs=[ANY, ANY, VM, VM, ANY, ANY, ANY, ANY, SM, SM, SM, ANY, ANY, ANY],
        out_specs=VM,
        scratch_shapes=list(SCRATCH.values()),
        compiler_params=pltpu.CompilerParams(
            collective_id=0, has_side_effects=True, vmem_limit_bytes=63 * MIB
        ),
        name="whole",
    )(
        resid, teacher_mixed, gain_mix, gain_mlp, w_c, w_b, w_x, w_dt.T, dt_bias, decay_rate, skip, w_out,
        w_gate, w_up,
    )
    grad_c, grad_b, grad_x, grad_dt = pl.pallas_call(
        split_kernel,
        out_shape=(
            struct((ROWS, 512), F32),
            struct((ROWS, 128), F32),
            struct((ROWS, 128), F32),
            struct((HEADS, ROWS), F32),
        ),
        in_specs=[VM],
        out_specs=(VM,) * 4,
        name="split",
    )(packed)
    return grad_c, grad_b, grad_x, grad_dt.T


def solution(mesh):
    in_specs = (
        P("dp", None),
        P("dp", None),
        P(),
        P(),
        P(None, "tensor"),
        P(None, "tensor"),
        P(None, "tensor"),
        P(None, "tensor"),
        P("tensor"),
        P("tensor"),
        P("tensor"),
        P("tensor", None),
        P("dp", "tensor"),
        P("dp", "tensor"),
    )
    out_specs = (P("dp", "tensor"), P("dp", "tensor"), P("dp", "tensor"), P("dp", "tensor"))
    return jax.shard_map(local, mesh=mesh, in_specs=in_specs, out_specs=out_specs, check_vma=False)
```

```python
import math
from types import SimpleNamespace

import jax
import jax.numpy as jnp
from jax import lax
from jax.experimental import pallas as pl
from jax.experimental.pallas import tpu as pltpu
from jax.sharding import PartitionSpec as P

D = 4096
FF = 14336
EPS = 1e-05
T = 128
HEADS = 4
DP = 16
TP = 8
HID = 1792
ROWS = 256
WIDTH = 512
PACK = 896
F32 = jnp.float32
BF16 = jnp.bfloat16
MESH = pl.DeviceIdType.MESH
MIB = 1024 * 1024

LEGS = {
    "RO": ("R", 0, 0, "full", 0, -1),
    "LO": ("L", 0, 0, "full", 0, 1),
    "YO": ("Y", 0, 0, "full", 1, 0),
    "RQ": ("R", 1, 0, "Q", 1, -1),
    "LQ": ("L", 1, 0, "Q", 1, 1),
    "RA": ("R", 0, -1, "A", 0, 2),
    "LB": ("L", 0, 1, "B", 0, 2),
    "YL": ("Y", 0, -1, "P", 1, -1),
    "YR": ("Y", 0, 1, "P", 1, 1),
    "RQA": ("R", 1, -1, "QA", 1, 2),
    "LQB": ("L", 1, 1, "QB", 1, 2),
    "YO2": ("Y", 0, 2, "P", 1, 2),
}
HALVES = {
    "RO1": ("R", 0, 0, "A", 0, -1),
    "RO2": ("R", 0, 0, "B", 0, -1),
    "LO1": ("L", 0, 0, "A", 0, 1),
    "LO2": ("L", 0, 0, "B", 0, 1),
    "YO1": ("Y", 0, 0, "A", 1, 0),
    "YO2": ("Y", 0, 0, "B", 1, 0),
    "RX1": ("R", 1, 0, "A", 1, -1),
    "RX2": ("R", 1, 0, "B", 1, -1),
    "LX1": ("L", 1, 0, "A", 1, 1),
    "LX2": ("L", 1, 0, "B", 1, 1),
    "RA": ("R", 0, -1, "A", 0, 2),
    "LB": ("L", 0, 1, "B", 0, 2),
    "RXA": ("R", 1, -1, "A", 1, 2),
    "LXB": ("L", 1, 1, "B", 1, 2),
}
NSEM = 2 * len(LEGS) + 1
NSEM_HALF = 2 * len(HALVES) + 1


def place():
    me = lax.axis_index("dp")
    return me, me // 8, (me % 8) // 2, me % 2


class Gather:
    def __init__(self, legs, piece, rows, p, qa, send, recv, give=None):
        self.legs, self.order = legs, list(legs)
        self.piece, self.send, self.recv, self.give = piece, send, recv, give
        self.me, self.y, self.z, self.c = place()
        half = rows // 2
        self.rows = {
            "full": (0, rows),
            "P": (0, p),
            "Q": (p, rows - p),
            "A": (0, half),
            "B": (half, rows - half),
            "QA": (p, qa),
            "QB": (p + qa, rows - p - qa),
        }

    def block(self, flip, dz, core):
        y = (1 - self.y) if flip else self.y
        return y * 8 + ((self.z + dz + 4) % 4) * 2 + core

    def target(self, name):
        if name == "R":
            return self.block(0, 1, self.c)
        if name == "L":
            return self.block(0, -1, self.c)
        if name == "Y":
            return self.block(1, 0, self.c)
        return self.block(0, 0, 1 - self.c)

    def copy(self, src, ref, sem, to):
        return pltpu.make_async_remote_copy(
            src_ref=src,
            dst_ref=ref,
            send_sem=self.send.at[sem],
            recv_sem=self.recv.at[sem],
            device_id={"dp": to},
            device_id_type=MESH,
        )

    def leg(self, name):
        to, flip, dz, rows, _, _ = self.legs[name]
        ref = self.piece(self.block(flip, dz, self.c), *self.rows[rows])
        src = ref
        if to == "Y" and self.give is not None:
            src = self.give(*self.rows[rows])
        return self.copy(src, ref, self.order.index(name), self.target(to))

    def landed(self, name):
        to, _, _, rows, flip, dz = self.legs[name]
        ref = self.piece(self.block(flip, dz, self.c), *self.rows[rows])
        return self.copy(ref, ref, self.order.index(name), self.target(to))

    def side(self, name, core):
        if name == "own":
            flip, dz, rows, sem = 0, 0, "full", len(self.order)
        else:
            _, _, _, rows, flip, dz = self.legs[name]
            sem = len(self.order) + 1 + self.order.index(name)
        ref = self.piece(self.block(flip, dz, core), *self.rows[rows])
        return self.copy(ref, ref, sem, self.target("S"))

    def begin(self, *names):
        for name in names:
            self.leg(name).start()
        self.side("own", self.c).start()

    def arrive(self, name, *then):
        self.landed(name).wait_recv()
        for other in then:
            self.leg(other).start()
        self.side(name, self.c).start()

    def side_arrive(self, *names):
        for name in names:
            self.side(name, 1 - self.c).wait_recv()

    def finish(self):
        for name in self.order:
            self.leg(name).wait_send()
        for name in ["own"] + self.order:
            self.side(name, self.c).wait_send()


def iota(axis):
    return lax.broadcasted_iota(jnp.int32, (T, T), axis)


def mm(a, b):
    return jnp.dot(a.astype(BF16), b.astype(BF16), preferred_element_type=F32)


def mm_t(a, b):
    return lax.dot_general(
        a.astype(BF16), b.astype(BF16), (((1,), (1,)), ((), ())), preferred_element_type=F32
    )


def softplus(v):
    return jnp.maximum(v, 0.0) + jnp.log1p(jnp.exp(-jnp.abs(v)))


def steps_of(raw, params):
    step = softplus(raw + params[0:1, :])
    lower = (iota(0) >= iota(1)).astype(F32)
    decay = jnp.dot(
        lower, -step * params[1:2, :], preferred_element_type=F32, precision=lax.Precision.HIGHEST
    )
    return step, decay, jnp.transpose(step), jnp.transpose(decay)


def head(k):
    return slice(k * 128, (k + 1) * 128)


class States:
    def __init__(self, slots, sums, send, recv):
        self.slots, self.sums, self.send, self.recv = slots, sums, send, recv
        self.me, self.y, self.z, self.c = place()
        self.m = self.me % 8

    def peer(self, k):
        at = (self.m + k) % 8
        return pltpu.make_async_remote_copy(
            src_ref=self.slots.at[self.m],
            dst_ref=self.slots.at[self.m],
            send_sem=self.send.at[k - 1],
            recv_sem=self.recv.at[k - 1],
            device_id={"dp": self.y * 8 + at},
            device_id_type=MESH,
        )

    def from_peer(self, k):
        at = (self.m - k + 8) % 8
        return pltpu.make_async_remote_copy(
            src_ref=self.slots.at[at],
            dst_ref=self.slots.at[at],
            send_sem=self.send.at[k - 1],
            recv_sem=self.recv.at[k - 1],
            device_id={"dp": self.y * 8 + at},
            device_id_type=MESH,
        )

    def across(self):
        return pltpu.make_async_remote_copy(
            src_ref=self.sums.at[0],
            dst_ref=self.sums.at[1],
            send_sem=self.send.at[7],
            recv_sem=self.recv.at[7],
            device_id={"dp": (1 - self.y) * 8 + self.m},
            device_id_type=MESH,
        )

    def begin(self):
        for k in range(1, 8):
            self.peer(k).start()

    def gathered(self):
        for k in range(1, 8):
            self.from_peer(k).wait_recv()

    def finish(self):
        for k in range(1, 8):
            self.peer(k).wait_send()
        self.across().wait_send()


def spread(scalars):
    lane = lax.broadcasted_iota(jnp.int32, (1, 128), 1)
    row = jnp.zeros((1, 128), F32)
    for h in range(HEADS):
        row = jnp.where(lane == h, scalars[h], row)
    return row


SCRATCH = {
    "held": pltpu.VMEM((DP, ROWS, HID), BF16),
    "give": pltpu.VMEM((ROWS, HID), BF16),
    "v_wc": pltpu.VMEM((D, 512), BF16),
    "v_wb": pltpu.VMEM((D, 128), BF16),
    "v_wx": pltpu.VMEM((D, 128), BF16),
    "v_wdt": pltpu.VMEM((HEADS, D), BF16),
    "v_out": pltpu.VMEM((512, D), BF16),
    "v_resid": pltpu.VMEM((T, WIDTH), BF16),
    "nin": pltpu.VMEM((T, D), BF16),
    "nin_t": pltpu.VMEM((DP, 256, T), BF16),
    "cols": pltpu.VMEM((DP, 256, T), BF16),
    "lhs": pltpu.VMEM((4 * T, D), BF16),
    "acc": pltpu.VMEM((4 * T, HID), F32),
    "proj": pltpu.VMEM((T, PACK), F32),
    "read": pltpu.VMEM((T, WIDTH), BF16),
    "state": pltpu.VMEM((8, 128, WIDTH), BF16),
    "sums": pltpu.VMEM((2, 128, WIDTH), BF16),
    "decays": pltpu.VMEM((8, 8, 128), F32),
    "enter": pltpu.VMEM((128, WIDTH), BF16),
    "through": pltpu.VMEM((T, WIDTH), F32),
    "mixer_out": pltpu.VMEM((T, WIDTH), BF16),
    "fade": pltpu.VMEM((HEADS, T, T), F32),
    "plain": pltpu.VMEM((HEADS, T, T), F32),
    "p_send": pltpu.VMEM((2, TP, T, WIDTH), BF16),
    "p_recv": pltpu.VMEM((2, TP, T, WIDTH), BF16),
    "strm": pltpu.VMEM((2, TP, T, WIDTH), BF16),
    "gained": pltpu.VMEM((TP, T, WIDTH), BF16),
    "grads": pltpu.VMEM((2 * T, HID), BF16),
    "squares": pltpu.VMEM((2, T, 128), F32),
    "out_grad": pltpu.VMEM((T, WIDTH), F32),
    "along": pltpu.VMEM((T, WIDTH), F32),
    "b_state": pltpu.VMEM((8, 128, WIDTH), BF16),
    "b_sums": pltpu.VMEM((2, 128, WIDTH), BF16),
    "packed": pltpu.VMEM((DP, T, PACK), BF16),
    "dread": pltpu.VMEM((T, WIDTH), F32),
    "dinject": pltpu.VMEM((T, 128), F32),
    "dvalue": pltpu.VMEM((T, 128), F32),
    "in_sem": pltpu.SemaphoreType.DMA((12,)),
    "g_send": pltpu.SemaphoreType.DMA((NSEM_HALF,)),
    "g_recv": pltpu.SemaphoreType.DMA((NSEM_HALF,)),
    "a_send": pltpu.SemaphoreType.DMA((2,)),
    "a_recv": pltpu.SemaphoreType.DMA((2,)),
    "h_send": pltpu.SemaphoreType.DMA((NSEM,)),
    "h_recv": pltpu.SemaphoreType.DMA((NSEM,)),
    "s_send": pltpu.SemaphoreType.DMA((8,)),
    "s_recv": pltpu.SemaphoreType.DMA((8,)),
    "d_send": pltpu.SemaphoreType.DMA((8,)),
    "d_recv": pltpu.SemaphoreType.DMA((8,)),
    "b_send": pltpu.SemaphoreType.DMA((8,)),
    "b_recv": pltpu.SemaphoreType.DMA((8,)),
    "c_send": pltpu.SemaphoreType.DMA((DP - 1,)),
    "c_recv": pltpu.SemaphoreType.DMA((DP - 1,)),
    "t_send": pltpu.SemaphoreType.DMA((4, DP)),
    "t_recv": pltpu.SemaphoreType.DMA((4, DP)),
}


def chunk(k, size=256):
    return pl.ds(pl.multiple_of(k * size, size), size)


def columns(p):
    return chunk(p, WIDTH)


def normalise(ref, rows, gain):
    def square(k, total):
        part = ref[rows, chunk(k, 512)].astype(F32)
        return total + jnp.sum(part * part, axis=1, keepdims=True)

    scale = lax.rsqrt(lax.fori_loop(0, 8, square, jnp.zeros((T, 1), F32)) / D + EPS)

    def write(k, _):
        at = chunk(k, 512)
        ref[rows, at] = (ref[rows, at].astype(F32) * scale * gain[:, at]).astype(BF16)
        return 0

    lax.fori_loop(0, 8, write, 0)


def state_weights(decays, m, forward):
    run_in, run_all = jnp.zeros((1, 128), F32), jnp.zeros((1, 128), F32)
    inside, whole = [None] * 8, [None] * 8
    for j in reversed(range(8)) if forward else range(8):
        reached = ((j < m) if forward else (j > m)).astype(F32)
        inside[j] = reached * jnp.exp(run_in)
        whole[j] = jnp.exp(run_all)
        end = decays[j, 0:1, :]
        run_in = run_in + reached * end
        run_all = run_all + end
    return inside, whole, jnp.exp(run_in)


def combine(state, weights, h):
    total = jnp.zeros((128, 128), F32)
    for j in range(8):
        total = total + weights[j][:, h : h + 1] * state[j, :, head(h)].astype(F32)
    return total


def whole_kernel(
    resid, teacher, gain_mix, gain_mlp, w_c, w_b, w_x, w_dt, bias, rate, skip, w_out, w_gate, w_up, out, *scratch
):
    s = SimpleNamespace(**dict(zip(SCRATCH, scratch)))
    me, y, z, c = place()
    m = me % 8
    t = lax.axis_index("tensor")
    other = (1 - y) * 8 + m
    half = HID // 2
    keep = pl.ds(pl.multiple_of(y * half, 128), half)
    rest = pl.ds(pl.multiple_of((1 - y) * half, 128), half)
    mine = pl.ds(pl.multiple_of(y * T, T), T)
    pairs = (
        (w_gate.at[:, keep], s.held.at[me, :, 0:half]),
        (w_up.at[:, keep], s.held.at[me, :, half:HID]),
        (w_gate.at[:, rest], s.give.at[:, 0:half]),
        (w_up.at[:, rest], s.give.at[:, half:HID]),
        (resid, s.nin),
        (w_c, s.v_wc),
        (w_b, s.v_wb),
        (w_x, s.v_wx),
        (w_dt, s.v_wdt),
        (teacher, s.lhs.at[mine, :]),
        (w_out, s.v_out),
        (resid.at[:, columns(t)], s.v_resid),
    )
    loads = [pltpu.make_async_copy(a, b, s.in_sem.at[k]) for k, (a, b) in enumerate(pairs)]
    for copy in loads:
        copy.start()
    sem = pltpu.get_barrier_semaphore()
    for k in range(1, DP):
        pl.semaphore_signal(sem, inc=1, device_id={"dp": (me + k) % DP}, device_id_type=MESH)
    for k in range(1, TP):
        for dp in (me, other):
            pl.semaphore_signal(
                sem, inc=1, device_id={"dp": dp, "tensor": (t + k) % TP}, device_id_type=MESH
            )
    loads[4].wait()
    normalise(s.nin, slice(None), gain_mix)
    pl.semaphore_wait(sem, DP - 1 + 2 * (TP - 1))
    for copy in loads[0:4]:
        copy.wait()
    gather = Gather(
        HALVES,
        lambda j, start, size: s.held.at[j, pl.ds(start, size), :],
        ROWS,
        112,
        64,
        s.g_send,
        s.g_recv,
        lambda start, size: s.give.at[pl.ds(start, size), :],
    )
    gather.begin("RO1", "LO2", "YO1", "YO2")

    bias_row, rate_row, skip_row = spread(bias), spread(rate), spread(skip)
    params = jnp.concatenate([bias_row, rate_row, skip_row, jnp.zeros((5, 128), F32)], axis=0)
    for copy in loads[5:9]:
        copy.wait()
    s.proj[...] = jnp.zeros_like(s.proj)

    def project(k, _):
        at = chunk(k, 1024)
        rows = s.nin[:, at]
        s.proj[:, 0:512] += jnp.dot(rows, s.v_wc[at, :], preferred_element_type=F32)
        s.proj[:, 512:640] += jnp.dot(rows, s.v_wb[at, :], preferred_element_type=F32)
        s.proj[:, 640:768] += jnp.dot(rows, s.v_wx[at, :], preferred_element_type=F32)
        s.proj[:, 768 : 768 + HEADS] += mm_t(rows, s.v_wdt[:, at])
        return 0

    lax.fori_loop(0, 4, project, 0)
    s.read[...] = s.proj[:, 0:512].astype(BF16)
    inject, values = s.proj[:, 512:640], s.proj[:, 640:768]
    raw = s.proj[:, 768:896]
    step, decay, step_t, decay_t = steps_of(raw, params)
    causal = iota(0) >= iota(1)
    inject_t = jnp.transpose(inject)
    for h in range(HEADS):
        row, col, step_row = decay_t[h : h + 1, :], decay[:, h : h + 1], step_t[h : h + 1, :]
        last = row[:, T - 1 : T]
        s.fade[h] = jnp.exp(jnp.where(causal, col - row, -1e30))
        s.plain[h] = s.fade[h] * mm_t(s.read[:, head(h)], inject)
        s.through[:, head(h)] = mm(s.plain[h] * step_row, values) + skip_row[:, h : h + 1] * values
        s.state[m, :, head(h)] = mm(inject_t * (jnp.exp(last - row) * step_row), values).astype(BF16)
    s.decays[m] = jnp.broadcast_to(decay[T - 1 : T, :], (8, 128))
    states = States(s.state, s.sums, s.s_send, s.s_recv)
    ends = States(s.decays, None, s.d_send, s.d_recv)
    ends.begin()
    states.begin()
    gather.leg("RO2").start()
    gather.leg("LO1").start()

    loads[9].wait()
    normalise(s.lhs, mine, gain_mlp)
    gather.arrive("RO1", "RA")
    gather.arrive("LO2", "LB")
    gather.arrive("YO1", "RX1")
    gather.arrive("YO2", "LX2", "RX2", "LX1")

    def teacher_move(k):
        ref = s.lhs.at[pl.ds(pl.multiple_of(y * T + k * (T // 2), T // 2), T // 2), :]
        return pltpu.make_async_remote_copy(
            src_ref=ref,
            dst_ref=ref,
            send_sem=s.a_send.at[k],
            recv_sem=s.a_recv.at[k],
            device_id={"dp": other, "tensor": (t + 4 * k) % TP},
            device_id_type=MESH,
        )

    def teacher_landed(k):
        ref = s.lhs.at[pl.ds(pl.multiple_of((1 - y) * T + k * (T // 2), T // 2), T // 2), :]
        return pltpu.make_async_remote_copy(
            src_ref=ref,
            dst_ref=ref,
            send_sem=s.a_send.at[k],
            recv_sem=s.a_recv.at[k],
            device_id={"dp": other, "tensor": (t + 4 * k) % TP},
            device_id_type=MESH,
        )

    teacher_move(0).start()
    teacher_move(1).start()
    ends.gathered()
    states.gathered()
    inside, whole, lead = state_weights(s.decays, m, True)
    for h in range(HEADS):
        s.sums[0, :, head(h)] = combine(s.state, whole, h).astype(BF16)
    states.across().start()
    states.across().wait_recv()
    after = (y == 1).astype(F32)
    for h in range(HEADS):
        total = combine(s.state, inside, h)
        total = total + (after * lead[:, h : h + 1]) * s.sums[1, :, head(h)].astype(F32)
        entering = total.astype(BF16)
        s.enter[:, head(h)] = entering
        grown = jnp.exp(decay[:, h : h + 1]) * mm(s.read[:, head(h)], entering)
        s.mixer_out[:, head(h)] = (s.through[:, head(h)] + grown).astype(BF16)

    def move(phase, ky, kt, src, dst):
        return pltpu.make_async_remote_copy(
            src_ref=src,
            dst_ref=dst,
            send_sem=s.t_send.at[phase, ky * TP + kt],
            recv_sem=s.t_recv.at[phase, ky * TP + kt],
            device_id={"dp": other if ky else me, "tensor": (t + kt) % TP},
            device_id_type=MESH,
        )

    def out_move(kt):
        return move(0, 0, kt, s.p_send.at[0, kt], s.p_recv.at[0, kt])

    def stream_move(ky, kt):
        return move(1, ky, kt, s.strm.at[y, t], s.strm.at[y, t])

    def stream_landed(ky, kt):
        at = s.strm.at[(1 - y) if ky else y, (t - kt + TP) % TP]
        return move(1, ky, kt, at, at)

    def mid_move(ky, kt):
        return move(2, ky, kt, s.p_send.at[(1 - y) if ky else y, kt], s.p_recv.at[ky, kt])

    def gained_move(kt):
        return move(3, 0, kt, s.gained.at[t], s.gained.at[t])

    def gained_landed(kt):
        at = s.gained.at[(t - kt + TP) % TP]
        return move(3, 0, kt, at, at)

    peers = [(ky, kt) for kt in range(TP) for ky in range(2) if ky + kt > 0]

    def out_part(p):
        return jnp.dot(s.mixer_out[...], s.v_out[:, columns(p)], preferred_element_type=F32)

    loads[10].wait()
    loads[11].wait()

    def out_send(k, _):
        s.p_send[0, k] = out_part((t + k) % TP).astype(BF16)
        out_move(k).start()
        return 0

    lax.fori_loop(1, TP, out_send, 0)
    stream = out_part(t) + s.v_resid[...].astype(F32)
    gather.arrive("RO2")
    gather.arrive("LO1")
    for k in range(1, TP):
        out_move(k).wait_recv()
        stream = stream + s.p_recv[0, k].astype(F32)
    s.strm[y, t] = stream.astype(BF16)
    for ky, kt in peers:
        stream_move(ky, kt).start()

    upper_rows, lower_rows = pl.ds(0, 2 * T), pl.ds(2 * T, 2 * T)

    def use(flip, dz):
        base = gather.block(flip, dz, 0)

        def one(n, _):
            at = chunk(n)
            s.acc[upper_rows, at] += jnp.dot(
                s.lhs[upper_rows, chunk(base)], s.held[base, :, at], preferred_element_type=F32
            ) + jnp.dot(
                s.lhs[upper_rows, chunk(base + 1)], s.held[base + 1, :, at], preferred_element_type=F32
            )
            return 0

        lax.fori_loop(0, HID // 256, one, 0)

    def turn(k, _):
        s.nin_t[k] = jnp.transpose(s.nin[:, chunk(k)].astype(F32)).astype(BF16)
        return 0

    lax.fori_loop(0, DP, turn, 0)
    s.acc[upper_rows, :] = jnp.zeros((2 * T, HID), F32)
    gather.arrive("RX1", "RXA")
    gather.arrive("LX2", "LXB")
    gather.arrive("RA")
    gather.arrive("LB")
    teacher_landed(0).wait_recv()
    teacher_landed(1).wait_recv()
    gather.side_arrive("own")
    use(0, 0)
    gather.side_arrive("YO1", "YO2")
    use(1, 0)
    gather.side_arrive("RO1", "RO2")
    use(0, -1)
    gather.side_arrive("LO1", "LO2")
    use(0, 1)
    gather.side_arrive("RA", "LB")
    use(0, 2)
    gather.arrive("RX2")
    gather.arrive("LX1")
    gather.side_arrive("RX1", "RX2")
    use(1, -1)
    gather.side_arrive("LX1", "LX2")
    use(1, 1)

    s.acc[lower_rows, :] = jnp.zeros((2 * T, HID), F32)
    s.squares[...] = jnp.zeros_like(s.squares)
    late = gather.block(1, 2, 0) // 2

    def student(p):
        for yy in range(2):
            part = s.strm[yy, p].astype(F32)
            s.squares[yy] += jnp.broadcast_to(jnp.sum(part * part, axis=1, keepdims=True), (T, 128))
            s.lhs[pl.ds((2 + yy) * T, T), columns(p)] = (part * gain_mlp[:, columns(p)]).astype(BF16)

        def one(n, _):
            at = chunk(n)
            s.acc[lower_rows, at] += jnp.dot(
                s.lhs[lower_rows, chunk(2 * p)], s.held[2 * p, :, at], preferred_element_type=F32
            ) + jnp.dot(
                s.lhs[lower_rows, chunk(2 * p + 1)], s.held[2 * p + 1, :, at], preferred_element_type=F32
            )
            return 0

        lax.fori_loop(0, HID // 256, one, 0)

    def student_early(kt, _):
        @pl.when(kt > 0)
        def _():
            stream_landed(0, kt).wait_recv()

        stream_landed(1, kt).wait_recv()
        p = (t - kt + TP) % TP

        @pl.when(p != late)
        def _():
            student(p)

        return 0

    lax.fori_loop(0, TP, student_early, 0)
    gather.arrive("RXA")
    gather.arrive("LXB")
    gather.side_arrive("RXA", "LXB")
    use(1, 2)
    student(late)
    scales = [lax.rsqrt(s.squares[yy, :, 0:1] / D + EPS) for yy in range(2)]
    scale = jnp.where(y == 0, scales[0], scales[1])
    both = jnp.concatenate(scales, axis=0)

    def column_copy(k):
        to = (me + k) % DP
        return pltpu.make_async_remote_copy(
            src_ref=s.nin_t.at[to],
            dst_ref=s.cols.at[me],
            send_sem=s.c_send.at[k - 1],
            recv_sem=s.c_recv.at[k - 1],
            device_id={"dp": to},
            device_id_type=MESH,
        )

    def column_landed(k):
        at = (me - k + DP) % DP
        return pltpu.make_async_remote_copy(
            src_ref=s.nin_t.at[at],
            dst_ref=s.cols.at[at],
            send_sem=s.c_send.at[k - 1],
            recv_sem=s.c_recv.at[k - 1],
            device_id={"dp": at},
            device_id_type=MESH,
        )

    def hidden(n, _):
        at, beside = chunk(n, 128), pl.ds(pl.multiple_of(half + n * 128, 128), 128)
        aim_gate = s.acc[upper_rows, at]
        aim = aim_gate * jax.nn.sigmoid(aim_gate) * s.acc[upper_rows, beside]
        gate, up = s.acc[lower_rows, at] * both, s.acc[lower_rows, beside] * both
        sigma = jax.nn.sigmoid(gate)
        silu = gate * sigma
        grad = (2.0 / math.sqrt(FF)) * (silu * up - aim)
        s.grads[:, at] = (grad * up * sigma * (1.0 + gate * (1.0 - sigma))).astype(BF16)
        s.grads[:, beside] = (grad * silu).astype(BF16)
        return 0

    lax.fori_loop(0, half // 128, hidden, 0)

    for k in range(1, TP):
        out_move(k).wait_send()

    def back(kt):
        p = (t + kt) % TP
        for i in range(2):
            part = mm_t(s.grads[...], s.held[2 * p + i]).astype(BF16)
            for yy in range(2):
                s.p_send[yy, kt, :, i * 256 : (i + 1) * 256] = part[yy * T : (yy + 1) * T, :]

    def back_send(kt, _):
        back(kt)
        mid_move(0, kt).start()
        mid_move(1, kt).start()
        return 0

    lax.fori_loop(1, TP, back_send, 0)
    back(0)
    mid_move(1, 0).start()
    for k in range(1, DP):
        column_copy(k).start()
    s.cols[me] = s.nin_t[me]
    s.along[...] = jnp.zeros_like(s.along)

    def stream_part(p, _):
        s.along[...] += mm_t(s.strm[y, p], s.v_out[:, columns(p)])
        return 0

    lax.fori_loop(0, TP, stream_part, 0)
    mid = s.p_send[y, 0].astype(F32)
    for ky, kt in peers:
        mid_move(ky, kt).wait_recv()
        mid = mid + s.p_recv[ky, kt].astype(F32)
    s.gained[t] = (mid * gain_mlp[:, columns(t)]).astype(BF16)
    for k in range(1, TP):
        gained_move(k).start()
    s.out_grad[...] = jnp.zeros_like(s.out_grad)

    def unproject(kt, inner):
        @pl.when(kt > 0)
        def _():
            gained_landed(kt).wait_recv()

        p = (t - kt + TP) % TP
        part = s.gained[p]
        s.out_grad[...] += mm_t(part, s.v_out[:, columns(p)])
        return inner + jnp.sum(part.astype(F32) * s.strm[y, p].astype(F32), axis=1, keepdims=True)

    inner = lax.fori_loop(0, TP, unproject, jnp.zeros((T, 1), F32))
    pull = scale * scale * scale * (inner / D)
    s.out_grad[...] = s.out_grad[...] * scale - s.along[...] * pull

    inject, values = s.proj[:, 512:640], s.proj[:, 640:768]
    raw = s.proj[:, 768:896]
    step, decay, step_t, decay_t = steps_of(raw, params)
    growth, growth_t = jnp.exp(decay), jnp.exp(decay_t)
    for h in range(HEADS):
        read_t = jnp.transpose(s.read[:, head(h)].astype(F32))
        s.b_state[m, :, head(h)] = mm(read_t * growth_t[h : h + 1, :], s.out_grad[:, head(h)]).astype(BF16)
    states_back = States(s.b_state, s.b_sums, s.b_send, s.b_recv)
    states_back.begin()
    lanes = lax.broadcasted_iota(jnp.int32, (1, 128), 1)
    s.dinject[...] = jnp.zeros_like(s.dinject)
    s.dvalue[...] = jnp.zeros_like(s.dvalue)
    step_rows, decay_rows, decay_cols = [], [], []
    for h in range(HEADS):
        step_row = step_t[h : h + 1, :]
        read_h, grad_h = s.read[:, head(h)], s.out_grad[:, head(h)]
        dweight = mm_t(grad_h, values)
        direct = dweight * s.plain[h]
        dscore = dweight * s.fade[h] * step_row
        weight = s.plain[h] * step_row
        through = mm_t(grad_h, s.enter[:, head(h)])
        s.dread[:, head(h)] = mm(dscore, inject) + growth[:, h : h + 1] * through
        s.dinject[...] += mm(jnp.transpose(dscore), read_h)
        s.dvalue[...] += mm(jnp.transpose(weight), grad_h) + skip_row[:, h : h + 1] * grad_h
        column = jnp.sum(direct, axis=0, keepdims=True)
        step_rows.append(column)
        decay_rows.append(-column * step_row)
        along = growth[:, h : h + 1] * jnp.sum(through * read_h.astype(F32), axis=1, keepdims=True)
        decay_cols.append(jnp.sum(direct * step_row, axis=1, keepdims=True) + along)
    states_back.gathered()
    inside, whole, lead = state_weights(s.decays, m, False)
    for h in range(HEADS):
        s.b_sums[0, :, head(h)] = combine(s.b_state, whole, h).astype(BF16)
    states_back.across().start()
    states_back.across().wait_recv()
    before = (y == 0).astype(F32)
    dstep = jnp.zeros((T, 128), F32)
    ddecay = jnp.zeros((T, 128), F32)
    for h in range(HEADS):
        behind = combine(s.b_state, inside, h)
        behind = behind + (before * lead[:, h : h + 1]) * s.b_sums[1, :, head(h)].astype(F32)
        tail_col = jnp.exp(decay[T - 1 : T, h : h + 1] - decay[:, h : h + 1])
        scaled_col = tail_col * step[:, h : h + 1]
        pulled = mm_t(values, behind)
        s.dinject[...] += scaled_col * pulled
        s.dvalue[...] += scaled_col * mm(inject, behind)
        drawn = tail_col * jnp.sum(inject * pulled, axis=1, keepdims=True)
        moved = drawn * step[:, h : h + 1]
        kept = jnp.exp(decay[T - 1 : T, h : h + 1]) * jnp.sum(
            jnp.sum(behind * s.enter[:, head(h)].astype(F32), axis=1, keepdims=True), axis=0, keepdims=True
        )
        end = kept + jnp.sum(moved, axis=0, keepdims=True)
        onehot = (lanes == h).astype(F32)
        final = (lax.broadcasted_iota(jnp.int32, (T, 1), 0) == T - 1).astype(F32)
        dstep = dstep + drawn * onehot
        ddecay = ddecay + (decay_cols[h] - moved + final * end) * onehot
    zero = jnp.zeros((128 - HEADS, 128), F32)
    dstep = dstep + jnp.transpose(jnp.concatenate(step_rows + [zero], axis=0))
    ddecay = ddecay + jnp.transpose(jnp.concatenate(decay_rows + [zero], axis=0))
    upper = (iota(0) <= iota(1)).astype(F32)
    later = jnp.dot(upper, ddecay, preferred_element_type=F32, precision=lax.Precision.HIGHEST)
    draw = (dstep - rate_row * later) * jax.nn.sigmoid(raw + bias_row)
    s.packed[me, :, 0:512] = s.dread[...].astype(BF16)
    s.packed[me, :, 512:640] = s.dinject[...].astype(BF16)
    s.packed[me, :, 640:768] = s.dvalue[...].astype(BF16)
    s.packed[me, :, 768:896] = draw.astype(BF16)

    last = Gather(
        LEGS, lambda j, start, size: s.packed.at[j, pl.ds(start, size), :], T, 48, 48, s.h_send, s.h_recv
    )
    last.begin("RO", "LO", "YO")
    out[...] = jnp.zeros_like(out)
    for k in range(1, DP):
        column_landed(k).wait_recv()

    def add(flip, dz):
        base = last.block(flip, dz, 0)
        out[...] += jnp.dot(s.cols[base], s.packed[base], preferred_element_type=F32) + jnp.dot(
            s.cols[base + 1], s.packed[base + 1], preferred_element_type=F32
        )

    last.arrive("YO", "RQ", "LQ")
    last.arrive("RO", "RA", "YL")
    last.arrive("LO", "LB", "YR")
    last.side_arrive("own")
    add(0, 0)
    last.side_arrive("YO")
    add(1, 0)
    last.arrive("RQ", "RQA")
    last.arrive("LQ", "LQB")
    last.arrive("RA", "YO2")
    last.arrive("LB")
    last.arrive("YL")
    last.arrive("YR")
    last.side_arrive("RO")
    add(0, -1)
    last.side_arrive("LO")
    add(0, 1)
    last.arrive("RQA")
    last.arrive("LQB")
    last.arrive("YO2")
    last.side_arrive("RA", "LB")
    add(0, 2)
    last.side_arrive("RQ", "YL")
    add(1, -1)
    last.side_arrive("LQ", "YR")
    add(1, 1)
    last.side_arrive("RQA", "LQB", "YO2")
    add(1, 2)

    gather.finish()
    last.finish()
    states.finish()
    states_back.finish()
    for k in range(1, 8):
        ends.peer(k).wait_send()
    for k in range(1, DP):
        column_copy(k).wait_send()
    for k in range(2):
        teacher_move(k).wait_send()
    for ky, kt in peers:
        stream_move(ky, kt).wait_send()
        mid_move(ky, kt).wait_send()
    for k in range(1, TP):
        gained_move(k).wait_send()


def split_kernel(packed, grad_c, grad_b, grad_x, grad_dt):
    grad_c[...] = packed[:, 0:512]
    grad_b[...] = packed[:, 512:640]
    grad_x[...] = packed[:, 640:768]
    grad_dt[...] = jnp.transpose(packed[:, 768:896])[0:HEADS, :]


VM = pl.BlockSpec(memory_space=pltpu.VMEM)
SM = pl.BlockSpec(memory_space=pltpu.SMEM)
ANY = pl.BlockSpec(memory_space=pl.ANY)


def struct(shape, dtype):
    return jax.ShapeDtypeStruct(shape, dtype)


def local(
    resid, teacher_mixed, gain_mix, gain_mlp, w_c, w_b, w_x, w_dt, dt_bias, decay_rate, skip, w_out,
    w_gate, w_up,
):
    gain_mix, gain_mlp = gain_mix.reshape(1, D), gain_mlp.reshape(1, D)
    packed = pl.pallas_call(
        whole_kernel,
        out_shape=struct((ROWS, PACK), F32),
        in_specs=[ANY, ANY, VM, VM, ANY, ANY, ANY, ANY, SM, SM, SM, ANY, ANY, ANY],
        out_specs=VM,
        scratch_shapes=list(SCRATCH.values()),
        compiler_params=pltpu.CompilerParams(
            collective_id=0, has_side_effects=True, vmem_limit_bytes=63 * MIB
        ),
        name="whole",
    )(
        resid, teacher_mixed, gain_mix, gain_mlp, w_c, w_b, w_x, w_dt.T, dt_bias, decay_rate, skip, w_out,
        w_gate, w_up,
    )
    grad_c, grad_b, grad_x, grad_dt = pl.pallas_call(
        split_kernel,
        out_shape=(
            struct((ROWS, 512), F32),
            struct((ROWS, 128), F32),
            struct((ROWS, 128), F32),
            struct((HEADS, ROWS), F32),
        ),
        in_specs=[VM],
        out_specs=(VM,) * 4,
        name="split",
    )(packed)
    return grad_c, grad_b, grad_x, grad_dt.T


def solution(mesh):
    in_specs = (
        P("dp", None),
        P("dp", None),
        P(),
        P(),
        P(None, "tensor"),
        P(None, "tensor"),
        P(None, "tensor"),
        P(None, "tensor"),
        P("tensor"),
        P("tensor"),
        P("tensor"),
        P("tensor", None),
        P("dp", "tensor"),
        P("dp", "tensor"),
    )
    out_specs = (P("dp", "tensor"), P("dp", "tensor"), P("dp", "tensor"), P("dp", "tensor"))
    return jax.shard_map(local, mesh=mesh, in_specs=in_specs, out_specs=out_specs, check_vma=False)
```

```python
import math
from types import SimpleNamespace

import jax
import jax.numpy as jnp
from jax import lax
from jax.experimental import pallas as pl
from jax.experimental.pallas import tpu as pltpu
from jax.sharding import PartitionSpec as P

D = 4096
FF = 14336
EPS = 1e-05
T = 128
HEADS = 4
DP = 16
TP = 8
HID = 1792
ROWS = 256
WIDTH = 512
PACK = 896
F32 = jnp.float32
BF16 = jnp.bfloat16
MESH = pl.DeviceIdType.MESH
MIB = 1024 * 1024

LEGS = {
    "RO": ("R", 0, 0, "full", 0, -1),
    "LO": ("L", 0, 0, "full", 0, 1),
    "YO": ("Y", 0, 0, "full", 1, 0),
    "RQ": ("R", 1, 0, "Q", 1, -1),
    "LQ": ("L", 1, 0, "Q", 1, 1),
    "RA": ("R", 0, -1, "A", 0, 2),
    "LB": ("L", 0, 1, "B", 0, 2),
    "YL": ("Y", 0, -1, "P", 1, -1),
    "YR": ("Y", 0, 1, "P", 1, 1),
    "RQA": ("R", 1, -1, "QA", 1, 2),
    "LQB": ("L", 1, 1, "QB", 1, 2),
    "YO2": ("Y", 0, 2, "P", 1, 2),
}
HALVES = {
    "RO1": ("R", 0, 0, "A", 0, -1),
    "RO2": ("R", 0, 0, "B", 0, -1),
    "LO1": ("L", 0, 0, "A", 0, 1),
    "LO2": ("L", 0, 0, "B", 0, 1),
    "YO1": ("Y", 0, 0, "A", 1, 0),
    "YO2": ("Y", 0, 0, "B", 1, 0),
    "RX1": ("R", 1, 0, "A", 1, -1),
    "RX2": ("R", 1, 0, "B", 1, -1),
    "LX1": ("L", 1, 0, "A", 1, 1),
    "LX2": ("L", 1, 0, "B", 1, 1),
    "RA": ("R", 0, -1, "A", 0, 2),
    "LB": ("L", 0, 1, "B", 0, 2),
    "RXA": ("R", 1, -1, "A", 1, 2),
    "LXB": ("L", 1, 1, "B", 1, 2),
}
NSEM = 2 * len(LEGS) + 1
NSEM_HALF = 2 * len(HALVES) + 1


def place():
    me = lax.axis_index("dp")
    return me, me // 8, (me % 8) // 2, me % 2


class Gather:
    def __init__(self, legs, piece, rows, p, qa, send, recv, give=None):
        self.legs, self.order = legs, list(legs)
        self.piece, self.send, self.recv, self.give = piece, send, recv, give
        self.me, self.y, self.z, self.c = place()
        half = rows // 2
        self.rows = {
            "full": (0, rows),
            "P": (0, p),
            "Q": (p, rows - p),
            "A": (0, half),
            "B": (half, rows - half),
            "QA": (p, qa),
            "QB": (p + qa, rows - p - qa),
        }

    def block(self, flip, dz, core):
        y = (1 - self.y) if flip else self.y
        return y * 8 + ((self.z + dz + 4) % 4) * 2 + core

    def target(self, name):
        if name == "R":
            return self.block(0, 1, self.c)
        if name == "L":
            return self.block(0, -1, self.c)
        if name == "Y":
            return self.block(1, 0, self.c)
        return self.block(0, 0, 1 - self.c)

    def copy(self, src, ref, sem, to):
        return pltpu.make_async_remote_copy(
            src_ref=src,
            dst_ref=ref,
            send_sem=self.send.at[sem],
            recv_sem=self.recv.at[sem],
            device_id={"dp": to},
            device_id_type=MESH,
        )

    def leg(self, name):
        to, flip, dz, rows, _, _ = self.legs[name]
        ref = self.piece(self.block(flip, dz, self.c), *self.rows[rows])
        src = ref
        if to == "Y" and self.give is not None:
            src = self.give(*self.rows[rows])
        return self.copy(src, ref, self.order.index(name), self.target(to))

    def landed(self, name):
        to, _, _, rows, flip, dz = self.legs[name]
        ref = self.piece(self.block(flip, dz, self.c), *self.rows[rows])
        return self.copy(ref, ref, self.order.index(name), self.target(to))

    def side(self, name, core):
        if name == "own":
            flip, dz, rows, sem = 0, 0, "full", len(self.order)
        else:
            _, _, _, rows, flip, dz = self.legs[name]
            sem = len(self.order) + 1 + self.order.index(name)
        ref = self.piece(self.block(flip, dz, core), *self.rows[rows])
        return self.copy(ref, ref, sem, self.target("S"))

    def begin(self, *names):
        for name in names:
            self.leg(name).start()
        self.side("own", self.c).start()

    def arrive(self, name, *then):
        self.landed(name).wait_recv()
        for other in then:
            self.leg(other).start()
        self.side(name, self.c).start()

    def side_arrive(self, *names):
        for name in names:
            self.side(name, 1 - self.c).wait_recv()

    def finish(self):
        for name in self.order:
            self.leg(name).wait_send()
        for name in ["own"] + self.order:
            self.side(name, self.c).wait_send()


def iota(axis):
    return lax.broadcasted_iota(jnp.int32, (T, T), axis)


def mm(a, b):
    return jnp.dot(a.astype(BF16), b.astype(BF16), preferred_element_type=F32)


def mm_t(a, b):
    return lax.dot_general(
        a.astype(BF16), b.astype(BF16), (((1,), (1,)), ((), ())), preferred_element_type=F32
    )


def softplus(v):
    return jnp.maximum(v, 0.0) + jnp.log1p(jnp.exp(-jnp.abs(v)))


def steps_of(raw, params):
    step = softplus(raw + params[0:1, :])
    lower = (iota(0) >= iota(1)).astype(F32)
    decay = jnp.dot(
        lower, -step * params[1:2, :], preferred_element_type=F32, precision=lax.Precision.HIGHEST
    )
    return step, decay, jnp.transpose(step), jnp.transpose(decay)


def head(k):
    return slice(k * 128, (k + 1) * 128)


class States:
    def __init__(self, slots, sums, send, recv):
        self.slots, self.sums, self.send, self.recv = slots, sums, send, recv
        self.me, self.y, self.z, self.c = place()
        self.m = self.me % 8

    def peer(self, k):
        at = (self.m + k) % 8
        return pltpu.make_async_remote_copy(
            src_ref=self.slots.at[self.m],
            dst_ref=self.slots.at[self.m],
            send_sem=self.send.at[k - 1],
            recv_sem=self.recv.at[k - 1],
            device_id={"dp": self.y * 8 + at},
            device_id_type=MESH,
        )

    def from_peer(self, k):
        at = (self.m - k + 8) % 8
        return pltpu.make_async_remote_copy(
            src_ref=self.slots.at[at],
            dst_ref=self.slots.at[at],
            send_sem=self.send.at[k - 1],
            recv_sem=self.recv.at[k - 1],
            device_id={"dp": self.y * 8 + at},
            device_id_type=MESH,
        )

    def across(self):
        return pltpu.make_async_remote_copy(
            src_ref=self.sums.at[0],
            dst_ref=self.sums.at[1],
            send_sem=self.send.at[7],
            recv_sem=self.recv.at[7],
            device_id={"dp": (1 - self.y) * 8 + self.m},
            device_id_type=MESH,
        )

    def begin(self):
        for k in range(1, 8):
            self.peer(k).start()

    def gathered(self):
        for k in range(1, 8):
            self.from_peer(k).wait_recv()

    def finish(self):
        for k in range(1, 8):
            self.peer(k).wait_send()
        self.across().wait_send()


def spread(scalars):
    lane = lax.broadcasted_iota(jnp.int32, (1, 128), 1)
    row = jnp.zeros((1, 128), F32)
    for h in range(HEADS):
        row = jnp.where(lane == h, scalars[h], row)
    return row


SCRATCH = {
    "held": pltpu.VMEM((DP, ROWS, HID), BF16),
    "give": pltpu.VMEM((ROWS, HID), BF16),
    "v_wc": pltpu.VMEM((D, 512), BF16),
    "v_wb": pltpu.VMEM((D, 128), BF16),
    "v_wx": pltpu.VMEM((D, 128), BF16),
    "v_wdt": pltpu.VMEM((HEADS, D), BF16),
    "v_out": pltpu.VMEM((TP, 512, WIDTH), BF16),
    "v_resid": pltpu.VMEM((T, WIDTH), BF16),
    "nin": pltpu.VMEM((T, D), BF16),
    "nin_t": pltpu.VMEM((DP, 256, T), BF16),
    "cols": pltpu.VMEM((DP, 256, T), BF16),
    "lhs": pltpu.VMEM((4 * T, D), BF16),
    "acc": pltpu.VMEM((4 * T, HID), F32),
    "proj": pltpu.VMEM((T, PACK), F32),
    "read": pltpu.VMEM((T, WIDTH), BF16),
    "state": pltpu.VMEM((8, 128, WIDTH), BF16),
    "sums": pltpu.VMEM((2, 128, WIDTH), BF16),
    "decays": pltpu.VMEM((8, 8, 128), F32),
    "enter": pltpu.VMEM((128, WIDTH), BF16),
    "through": pltpu.VMEM((T, WIDTH), F32),
    "mixer_out": pltpu.VMEM((T, WIDTH), BF16),
    "fade": pltpu.VMEM((HEADS, T, T), F32),
    "plain": pltpu.VMEM((HEADS, T, T), F32),
    "p_send": pltpu.VMEM((TP, T, WIDTH), BF16),
    "p_recv": pltpu.VMEM((TP, T, WIDTH), BF16),
    "str_a": pltpu.VMEM((4, 4, T // 2, WIDTH), BF16),
    "str_b": pltpu.VMEM((4, 4, T // 2, WIDTH), BF16),
    "mid_a": pltpu.VMEM((4, 4, T // 2, WIDTH), BF16),
    "mid_b": pltpu.VMEM((4, 4, T // 2, WIDTH), BF16),
    "got_a": pltpu.VMEM((3, 4, T // 2, WIDTH), BF16),
    "got_b": pltpu.VMEM((3, 4, T // 2, WIDTH), BF16),
    "sum_a": pltpu.VMEM((4, T // 2, WIDTH), BF16),
    "sum_b": pltpu.VMEM((4, T // 2, WIDTH), BF16),
    "end_a": pltpu.VMEM((3, T // 2, WIDTH), BF16),
    "end_b": pltpu.VMEM((3, T // 2, WIDTH), BF16),
    "gained": pltpu.VMEM((TP, T, WIDTH), BF16),
    "grads": pltpu.VMEM((2 * T, HID), BF16),
    "squares": pltpu.VMEM((2, T, 128), F32),
    "out_grad": pltpu.VMEM((T, WIDTH), F32),
    "along": pltpu.VMEM((T, WIDTH), F32),
    "b_state": pltpu.VMEM((8, 128, WIDTH), BF16),
    "b_sums": pltpu.VMEM((2, 128, WIDTH), BF16),
    "packed": pltpu.VMEM((DP, T, PACK), BF16),
    "dread": pltpu.VMEM((T, WIDTH), F32),
    "dinject": pltpu.VMEM((T, 128), F32),
    "dvalue": pltpu.VMEM((T, 128), F32),
    "in_sem": pltpu.SemaphoreType.DMA((11 + TP,)),
    "g_send": pltpu.SemaphoreType.DMA((NSEM_HALF,)),
    "g_recv": pltpu.SemaphoreType.DMA((NSEM_HALF,)),
    "a_send": pltpu.SemaphoreType.DMA((2,)),
    "a_recv": pltpu.SemaphoreType.DMA((2,)),
    "h_send": pltpu.SemaphoreType.DMA((NSEM,)),
    "h_recv": pltpu.SemaphoreType.DMA((NSEM,)),
    "s_send": pltpu.SemaphoreType.DMA((8,)),
    "s_recv": pltpu.SemaphoreType.DMA((8,)),
    "d_send": pltpu.SemaphoreType.DMA((8,)),
    "d_recv": pltpu.SemaphoreType.DMA((8,)),
    "b_send": pltpu.SemaphoreType.DMA((8,)),
    "b_recv": pltpu.SemaphoreType.DMA((8,)),
    "c_send": pltpu.SemaphoreType.DMA((DP - 1,)),
    "c_recv": pltpu.SemaphoreType.DMA((DP - 1,)),
    "t_send": pltpu.SemaphoreType.DMA((2, TP)),
    "t_recv": pltpu.SemaphoreType.DMA((2, TP)),
    "p1_send": pltpu.SemaphoreType.DMA((12,)),
    "p1_recv": pltpu.SemaphoreType.DMA((12,)),
    "p2_send": pltpu.SemaphoreType.DMA((12,)),
    "p2_recv": pltpu.SemaphoreType.DMA((12,)),
}


def chunk(k, size=256):
    return pl.ds(pl.multiple_of(k * size, size), size)


def columns(p):
    return chunk(p, WIDTH)


def normalise(ref, rows, gain):
    total = jnp.zeros((T, 1), F32)
    for k in range(8):
        part = ref[rows, k * 512 : (k + 1) * 512].astype(F32)
        total = total + jnp.sum(part * part, axis=1, keepdims=True)
    scale = lax.rsqrt(total / D + EPS)
    for k in range(8):
        at = slice(k * 512, (k + 1) * 512)
        ref[rows, at] = (ref[rows, at].astype(F32) * scale * gain[:, at]).astype(BF16)


def state_weights(decays, m, forward):
    run_in, run_all = jnp.zeros((1, 128), F32), jnp.zeros((1, 128), F32)
    inside, whole = [None] * 8, [None] * 8
    for j in reversed(range(8)) if forward else range(8):
        reached = ((j < m) if forward else (j > m)).astype(F32)
        inside[j] = reached * jnp.exp(run_in)
        whole[j] = jnp.exp(run_all)
        end = decays[j, 0:1, :]
        run_in = run_in + reached * end
        run_all = run_all + end
    return inside, whole, jnp.exp(run_in)


def combine(state, weights, h):
    total = jnp.zeros((128, 128), F32)
    for j in range(8):
        total = total + weights[j][:, h : h + 1] * state[j, :, head(h)].astype(F32)
    return total


def whole_kernel(
    resid, teacher, gain_mix, gain_mlp, w_c, w_b, w_x, w_dt, bias, rate, skip, w_out, w_gate, w_up, out, *scratch
):
    s = SimpleNamespace(**dict(zip(SCRATCH, scratch)))
    me, y, z, c = place()
    m = me % 8
    t = lax.axis_index("tensor")
    other = (1 - y) * 8 + m
    half = HID // 2
    keep = pl.ds(pl.multiple_of(y * half, 128), half)
    rest = pl.ds(pl.multiple_of((1 - y) * half, 128), half)
    mine = pl.ds(pl.multiple_of(y * T, T), T)
    pairs = (
        (w_gate.at[:, keep], s.held.at[me, :, 0:half]),
        (w_up.at[:, keep], s.held.at[me, :, half:HID]),
        (w_gate.at[:, rest], s.give.at[:, 0:half]),
        (w_up.at[:, rest], s.give.at[:, half:HID]),
        (resid, s.nin),
        (w_c, s.v_wc),
        (w_b, s.v_wb),
        (w_x, s.v_wx),
        (w_dt, s.v_wdt),
        (teacher, s.lhs.at[mine, :]),
        (resid.at[:, columns(t)], s.v_resid),
    ) + tuple((w_out.at[:, p * WIDTH : (p + 1) * WIDTH], s.v_out.at[p]) for p in range(TP))
    loads = [pltpu.make_async_copy(a, b, s.in_sem.at[k]) for k, (a, b) in enumerate(pairs)]
    for copy in loads:
        copy.start()
    sem = pltpu.get_barrier_semaphore()
    for k in range(1, DP):
        pl.semaphore_signal(sem, inc=1, device_id={"dp": (me + k) % DP}, device_id_type=MESH)
    for k in range(1, TP):
        for dp in (me, other):
            pl.semaphore_signal(
                sem, inc=1, device_id={"dp": dp, "tensor": (t + k) % TP}, device_id_type=MESH
            )
    loads[4].wait()
    normalise(s.nin, slice(None), gain_mix)
    pl.semaphore_wait(sem, DP - 1 + 2 * (TP - 1))
    for copy in loads[0:4]:
        copy.wait()
    gather = Gather(
        HALVES,
        lambda j, start, size: s.held.at[j, pl.ds(start, size), :],
        ROWS,
        112,
        64,
        s.g_send,
        s.g_recv,
        lambda start, size: s.give.at[pl.ds(start, size), :],
    )
    gather.begin("RO1", "LO2", "YO1", "YO2")

    bias_row, rate_row, skip_row = spread(bias), spread(rate), spread(skip)
    params = jnp.concatenate([bias_row, rate_row, skip_row, jnp.zeros((5, 128), F32)], axis=0)
    for copy in loads[5:9]:
        copy.wait()
    rows = s.nin[...]
    s.proj[:, 0:512] = jnp.dot(rows, s.v_wc[...], preferred_element_type=F32)
    s.proj[:, 512:640] = jnp.dot(rows, s.v_wb[...], preferred_element_type=F32)
    s.proj[:, 640:768] = jnp.dot(rows, s.v_wx[...], preferred_element_type=F32)
    s.proj[:, 768:896] = jnp.zeros((T, 128), F32)
    s.proj[:, 768 : 768 + HEADS] = mm_t(rows, s.v_wdt[...])
    s.read[...] = s.proj[:, 0:512].astype(BF16)
    inject, values = s.proj[:, 512:640], s.proj[:, 640:768]
    raw = s.proj[:, 768:896]
    step, decay, step_t, decay_t = steps_of(raw, params)
    causal = iota(0) >= iota(1)
    inject_t = jnp.transpose(inject)
    for h in range(HEADS):
        row, col, step_row = decay_t[h : h + 1, :], decay[:, h : h + 1], step_t[h : h + 1, :]
        last = row[:, T - 1 : T]
        s.fade[h] = jnp.exp(jnp.where(causal, col - row, -1e30))
        s.plain[h] = s.fade[h] * mm_t(s.read[:, head(h)], inject)
        s.through[:, head(h)] = mm(s.plain[h] * step_row, values) + skip_row[:, h : h + 1] * values
        s.state[m, :, head(h)] = mm(inject_t * (jnp.exp(last - row) * step_row), values).astype(BF16)
    s.decays[m] = jnp.broadcast_to(decay[T - 1 : T, :], (8, 128))
    states = States(s.state, s.sums, s.s_send, s.s_recv)
    ends = States(s.decays, None, s.d_send, s.d_recv)
    ends.begin()
    states.begin()
    gather.leg("RO2").start()
    gather.leg("LO1").start()

    loads[9].wait()
    normalise(s.lhs, mine, gain_mlp)
    gather.arrive("RO1", "RA")
    gather.arrive("LO2", "LB")
    gather.arrive("YO1", "RX1")
    gather.arrive("YO2", "LX2", "RX2", "LX1")

    def teacher_move(k):
        ref = s.lhs.at[pl.ds(pl.multiple_of(y * T + k * (T // 2), T // 2), T // 2), :]
        return pltpu.make_async_remote_copy(
            src_ref=ref,
            dst_ref=ref,
            send_sem=s.a_send.at[k],
            recv_sem=s.a_recv.at[k],
            device_id={"dp": other, "tensor": (t + 4 * k) % TP},
            device_id_type=MESH,
        )

    def teacher_landed(k):
        ref = s.lhs.at[pl.ds(pl.multiple_of((1 - y) * T + k * (T // 2), T // 2), T // 2), :]
        return pltpu.make_async_remote_copy(
            src_ref=ref,
            dst_ref=ref,
            send_sem=s.a_send.at[k],
            recv_sem=s.a_recv.at[k],
            device_id={"dp": other, "tensor": (t + 4 * k) % TP},
            device_id_type=MESH,
        )

    teacher_move(0).start()
    teacher_move(1).start()
    ends.gathered()
    states.gathered()
    inside, whole, lead = state_weights(s.decays, m, True)
    for h in range(HEADS):
        s.sums[0, :, head(h)] = combine(s.state, whole, h).astype(BF16)
    states.across().start()
    states.across().wait_recv()
    after = (y == 1).astype(F32)
    for h in range(HEADS):
        total = combine(s.state, inside, h)
        total = total + (after * lead[:, h : h + 1]) * s.sums[1, :, head(h)].astype(F32)
        entering = total.astype(BF16)
        s.enter[:, head(h)] = entering
        grown = jnp.exp(decay[:, h : h + 1]) * mm(s.read[:, head(h)], entering)
        s.mixer_out[:, head(h)] = (s.through[:, head(h)] + grown).astype(BF16)

    def move(phase, kt, src, dst):
        return pltpu.make_async_remote_copy(
            src_ref=src,
            dst_ref=dst,
            send_sem=s.t_send.at[phase, kt],
            recv_sem=s.t_recv.at[phase, kt],
            device_id={"tensor": (t + kt) % TP},
            device_id_type=MESH,
        )

    def out_move(kt):
        return move(0, kt, s.p_send.at[kt], s.p_recv.at[kt])

    def gained_move(kt):
        return move(1, kt, s.gained.at[t], s.gained.at[t])

    def gained_landed(kt):
        at = s.gained.at[(t - kt + TP) % TP]
        return move(1, kt, at, at)

    px, py = t % 4, (t // 4) * 2 + y

    def plane(sems, leg, over_x, k, src, dst):
        xx = (px + k) % 4 if over_x else px
        yy = py if over_x else (py + k) % 4
        return pltpu.make_async_remote_copy(
            src_ref=src,
            dst_ref=dst,
            send_sem=sems[0].at[3 * leg + k - 1],
            recv_sem=sems[1].at[3 * leg + k - 1],
            device_id={"dp": (yy % 2) * 8 + m, "tensor": (yy // 2) * 4 + xx},
            device_id_type=MESH,
        )

    def stream_leg(leg, k, landing=False):
        d = (4 - k) if landing else 0
        ref = (
            s.str_a.at[py, (px + d) % 4],
            s.str_b.at[px, (py + d) % 4],
            s.str_a.at[(py + d) % 4],
            s.str_b.at[(px + d) % 4],
        )[leg]
        return plane((s.p1_send, s.p1_recv), leg, leg in (0, 3), k, ref, ref)

    def mid_leg(leg, k):
        src, dst = (
            (s.mid_a.at[(px + k) % 4], s.got_a.at[k - 1]),
            (s.mid_b.at[(py + k) % 4], s.got_b.at[k - 1]),
            (s.sum_a.at[(py + k) % 4], s.end_a.at[k - 1]),
            (s.sum_b.at[(px + k) % 4], s.end_b.at[k - 1]),
        )[leg]
        return plane((s.p2_send, s.p2_recv), leg, leg in (0, 3), k, src, dst)

    def stream_block(yy, p):
        row, col = 2 * (p // 4) + yy, p % 4
        return jnp.concatenate([s.str_a[row, col], s.str_b[col, row]], axis=0)

    def out_part(p):
        return jnp.dot(s.mixer_out[...], s.v_out[p], preferred_element_type=F32)

    for copy in loads[10:]:
        copy.wait()

    def out_send(k, _):
        s.p_send[k] = out_part((t + k) % TP).astype(BF16)
        out_move(k).start()
        return 0

    lax.fori_loop(1, TP, out_send, 0)
    stream = out_part(t) + s.v_resid[...].astype(F32)
    gather.arrive("RO2")
    gather.arrive("LO1")
    for k in range(1, TP):
        out_move(k).wait_recv()
        stream = stream + s.p_recv[k].astype(F32)
    half_rows = T // 2
    s.str_a[py, px] = stream[0:half_rows].astype(BF16)
    s.str_b[px, py] = stream[half_rows:T].astype(BF16)
    for k in (2, 1, 3):
        stream_leg(0, k).start()
        stream_leg(1, k).start()

    upper_rows, lower_rows = pl.ds(0, 2 * T), pl.ds(2 * T, 2 * T)

    def use(flip, dz):
        base = gather.block(flip, dz, 0)

        s.acc[upper_rows, :] += jnp.dot(
            s.lhs[upper_rows, chunk(base)], s.held[base], preferred_element_type=F32
        ) + jnp.dot(s.lhs[upper_rows, chunk(base + 1)], s.held[base + 1], preferred_element_type=F32)

    def turn(k, _):
        s.nin_t[k] = jnp.transpose(s.nin[:, chunk(k)].astype(F32)).astype(BF16)
        return 0

    lax.fori_loop(0, DP, turn, 0)
    s.acc[upper_rows, :] = jnp.zeros((2 * T, HID), F32)
    teacher_landed(0).wait_recv()
    teacher_landed(1).wait_recv()
    gather.side_arrive("own")
    use(0, 0)
    gather.side_arrive("YO1", "YO2")
    use(1, 0)
    for k in (2, 1, 3):
        stream_leg(0, k, True).wait_recv()
    for k in (2, 1, 3):
        stream_leg(2, k).start()
    for k in (2, 1, 3):
        stream_leg(1, k, True).wait_recv()
    for k in (2, 1, 3):
        stream_leg(3, k).start()
    gather.arrive("RX1", "RXA")
    gather.arrive("LX2", "LXB")
    gather.arrive("RA")
    gather.arrive("LB")
    gather.side_arrive("RO1", "RO2")
    use(0, -1)
    gather.side_arrive("LO1", "LO2")
    use(0, 1)
    gather.side_arrive("RA", "LB")
    use(0, 2)
    gather.arrive("RX2")
    gather.arrive("LX1")
    gather.side_arrive("RX1", "RX2")
    use(1, -1)
    gather.side_arrive("LX1", "LX2")
    use(1, 1)

    for leg in (2, 3):
        for k in (2, 1, 3):
            stream_leg(leg, k, True).wait_recv()
    s.squares[...] = jnp.zeros_like(s.squares)

    def student_rows(p, _):
        for yy in range(2):
            part = stream_block(yy, p).astype(F32)
            s.squares[yy] += jnp.broadcast_to(jnp.sum(part * part, axis=1, keepdims=True), (T, 128))
            s.lhs[pl.ds((2 + yy) * T, T), columns(p)] = (part * gain_mlp[:, columns(p)]).astype(BF16)
        return 0

    lax.fori_loop(0, TP, student_rows, 0)
    gather.arrive("RXA")
    gather.arrive("LXB")
    gather.side_arrive("RXA", "LXB")
    use(1, 2)
    for n in range(HID // 256):
        at = slice(n * 256, (n + 1) * 256)
        s.acc[lower_rows, at] = jnp.dot(
            s.lhs[lower_rows, :], s.held[:, :, at].reshape(D, 256), preferred_element_type=F32
        )
    scales = [lax.rsqrt(s.squares[yy, :, 0:1] / D + EPS) for yy in range(2)]
    scale = jnp.where(y == 0, scales[0], scales[1])
    both = jnp.concatenate(scales, axis=0)

    def column_copy(k):
        to = (me + k) % DP
        return pltpu.make_async_remote_copy(
            src_ref=s.nin_t.at[to],
            dst_ref=s.cols.at[me],
            send_sem=s.c_send.at[k - 1],
            recv_sem=s.c_recv.at[k - 1],
            device_id={"dp": to},
            device_id_type=MESH,
        )

    def column_landed(k):
        at = (me - k + DP) % DP
        return pltpu.make_async_remote_copy(
            src_ref=s.nin_t.at[at],
            dst_ref=s.cols.at[at],
            send_sem=s.c_send.at[k - 1],
            recv_sem=s.c_recv.at[k - 1],
            device_id={"dp": at},
            device_id_type=MESH,
        )

    for n in range(half // 128):
        at, beside = slice(n * 128, (n + 1) * 128), slice(half + n * 128, half + (n + 1) * 128)
        aim_gate = s.acc[upper_rows, at]
        aim = aim_gate * jax.nn.sigmoid(aim_gate) * s.acc[upper_rows, beside]
        gate, up = s.acc[lower_rows, at] * both, s.acc[lower_rows, beside] * both
        sigma = jax.nn.sigmoid(gate)
        silu = gate * sigma
        grad = (2.0 / math.sqrt(FF)) * (silu * up - aim)
        s.grads[:, at] = (grad * up * sigma * (1.0 + gate * (1.0 - sigma))).astype(BF16)
        s.grads[:, beside] = (grad * silu).astype(BF16)

    def back(yh, xx):
        for i in range(2):
            part = mm_t(s.grads[...], s.held[2 * (yh * 4 + xx) + i]).astype(BF16)
            lanes_at = slice(i * 256, (i + 1) * 256)
            for yy in range(2):
                s.mid_a[xx, 2 * yh + yy, :, lanes_at] = part[yy * T : yy * T + half_rows, :]
                s.mid_b[2 * yh + yy, xx, :, lanes_at] = part[yy * T + half_rows : (yy + 1) * T, :]

    def back_far(xx, _):
        back(1 - t // 4, xx)
        return 0

    lax.fori_loop(0, 4, back_far, 0)
    mid_leg(1, 2).start()

    @pl.when(y == 0)
    def _():
        mid_leg(1, 3).start()

    @pl.when(y == 1)
    def _():
        mid_leg(1, 1).start()

    back(t // 4, (px + 2) % 4)
    mid_leg(0, 2).start()
    back(t // 4, (px + 1) % 4)
    mid_leg(0, 1).start()
    back(t // 4, (px + 3) % 4)
    mid_leg(0, 3).start()
    back(t // 4, px)

    @pl.when(y == 0)
    def _():
        mid_leg(1, 1).start()

    @pl.when(y == 1)
    def _():
        mid_leg(1, 3).start()

    for k in range(1, DP):
        column_copy(k).start()
    s.cols[me] = s.nin_t[me]
    s.along[...] = jnp.zeros_like(s.along)

    def stream_part(p, _):
        s.along[...] += mm_t(stream_block(y, p), s.v_out[p])
        return 0

    lax.fori_loop(0, TP, stream_part, 0)

    def fold(own, got, sums):
        for at in range(4):
            total = own[at].astype(F32)
            for k in range(3):
                total = total + got[k, at].astype(F32)
            sums[at] = total.astype(BF16)

    for k in (2, 1, 3):
        mid_leg(0, k).wait_recv()
    fold(s.mid_a.at[px], s.got_a, s.sum_a)
    for k in (2, 1, 3):
        mid_leg(2, k).start()
    for k in (2, 1, 3):
        mid_leg(1, k).wait_recv()
    fold(s.mid_b.at[py], s.got_b, s.sum_b)
    for k in (2, 1, 3):
        mid_leg(3, k).start()
    parts = []
    for leg, own, ends_of in ((2, s.sum_a.at[py], s.end_a), (3, s.sum_b.at[px], s.end_b)):
        total = own[...].astype(F32)
        for k in (2, 1, 3):
            mid_leg(leg, k).wait_recv()
            total = total + ends_of[k - 1].astype(F32)
        parts.append(total)
    mid = jnp.concatenate(parts, axis=0)
    s.gained[t] = (mid * gain_mlp[:, columns(t)]).astype(BF16)
    for k in range(1, TP):
        gained_move(k).start()
    s.out_grad[...] = jnp.zeros_like(s.out_grad)

    def unproject(kt, inner):
        @pl.when(kt > 0)
        def _():
            gained_landed(kt).wait_recv()

        p = (t - kt + TP) % TP
        part = s.gained[p]
        s.out_grad[...] += mm_t(part, s.v_out[p])
        return inner + jnp.sum(part.astype(F32) * stream_block(y, p).astype(F32), axis=1, keepdims=True)

    inner = lax.fori_loop(0, TP, unproject, jnp.zeros((T, 1), F32))
    pull = scale * scale * scale * (inner / D)
    s.out_grad[...] = s.out_grad[...] * scale - s.along[...] * pull

    inject, values = s.proj[:, 512:640], s.proj[:, 640:768]
    raw = s.proj[:, 768:896]
    step, decay, step_t, decay_t = steps_of(raw, params)
    growth, growth_t = jnp.exp(decay), jnp.exp(decay_t)
    for h in range(HEADS):
        read_t = jnp.transpose(s.read[:, head(h)].astype(F32))
        s.b_state[m, :, head(h)] = mm(read_t * growth_t[h : h + 1, :], s.out_grad[:, head(h)]).astype(BF16)
    states_back = States(s.b_state, s.b_sums, s.b_send, s.b_recv)
    states_back.begin()
    lanes = lax.broadcasted_iota(jnp.int32, (1, 128), 1)
    s.dinject[...] = jnp.zeros_like(s.dinject)
    s.dvalue[...] = jnp.zeros_like(s.dvalue)
    step_rows, decay_rows, decay_cols = [], [], []
    for h in range(HEADS):
        step_row = step_t[h : h + 1, :]
        read_h, grad_h = s.read[:, head(h)], s.out_grad[:, head(h)]
        dweight = mm_t(grad_h, values)
        direct = dweight * s.plain[h]
        dscore = dweight * s.fade[h] * step_row
        weight = s.plain[h] * step_row
        through = mm_t(grad_h, s.enter[:, head(h)])
        s.dread[:, head(h)] = mm(dscore, inject) + growth[:, h : h + 1] * through
        s.dinject[...] += mm(jnp.transpose(dscore), read_h)
        s.dvalue[...] += mm(jnp.transpose(weight), grad_h) + skip_row[:, h : h + 1] * grad_h
        column = jnp.sum(direct, axis=0, keepdims=True)
        step_rows.append(column)
        decay_rows.append(-column * step_row)
        along = growth[:, h : h + 1] * jnp.sum(through * read_h.astype(F32), axis=1, keepdims=True)
        decay_cols.append(jnp.sum(direct * step_row, axis=1, keepdims=True) + along)
    states_back.gathered()
    inside, whole, lead = state_weights(s.decays, m, False)
    for h in range(HEADS):
        s.b_sums[0, :, head(h)] = combine(s.b_state, whole, h).astype(BF16)
    states_back.across().start()
    states_back.across().wait_recv()
    before = (y == 0).astype(F32)
    dstep = jnp.zeros((T, 128), F32)
    ddecay = jnp.zeros((T, 128), F32)
    for h in range(HEADS):
        behind = combine(s.b_state, inside, h)
        behind = behind + (before * lead[:, h : h + 1]) * s.b_sums[1, :, head(h)].astype(F32)
        tail_col = jnp.exp(decay[T - 1 : T, h : h + 1] - decay[:, h : h + 1])
        scaled_col = tail_col * step[:, h : h + 1]
        pulled = mm_t(values, behind)
        s.dinject[...] += scaled_col * pulled
        s.dvalue[...] += scaled_col * mm(inject, behind)
        drawn = tail_col * jnp.sum(inject * pulled, axis=1, keepdims=True)
        moved = drawn * step[:, h : h + 1]
        kept = jnp.exp(decay[T - 1 : T, h : h + 1]) * jnp.sum(
            jnp.sum(behind * s.enter[:, head(h)].astype(F32), axis=1, keepdims=True), axis=0, keepdims=True
        )
        end = kept + jnp.sum(moved, axis=0, keepdims=True)
        onehot = (lanes == h).astype(F32)
        final = (lax.broadcasted_iota(jnp.int32, (T, 1), 0) == T - 1).astype(F32)
        dstep = dstep + drawn * onehot
        ddecay = ddecay + (decay_cols[h] - moved + final * end) * onehot
    zero = jnp.zeros((128 - HEADS, 128), F32)
    dstep = dstep + jnp.transpose(jnp.concatenate(step_rows + [zero], axis=0))
    ddecay = ddecay + jnp.transpose(jnp.concatenate(decay_rows + [zero], axis=0))
    upper = (iota(0) <= iota(1)).astype(F32)
    later = jnp.dot(upper, ddecay, preferred_element_type=F32, precision=lax.Precision.HIGHEST)
    draw = (dstep - rate_row * later) * jax.nn.sigmoid(raw + bias_row)
    s.packed[me, :, 0:512] = s.dread[...].astype(BF16)
    s.packed[me, :, 512:640] = s.dinject[...].astype(BF16)
    s.packed[me, :, 640:768] = s.dvalue[...].astype(BF16)
    s.packed[me, :, 768:896] = draw.astype(BF16)

    last = Gather(
        LEGS, lambda j, start, size: s.packed.at[j, pl.ds(start, size), :], T, 48, 48, s.h_send, s.h_recv
    )
    last.begin("RO", "LO", "YO")
    out[...] = jnp.zeros_like(out)
    for k in range(1, DP):
        column_landed(k).wait_recv()

    def add(flip, dz):
        base = last.block(flip, dz, 0)
        out[...] += jnp.dot(s.cols[base], s.packed[base], preferred_element_type=F32) + jnp.dot(
            s.cols[base + 1], s.packed[base + 1], preferred_element_type=F32
        )

    last.arrive("YO", "RQ", "LQ")
    last.arrive("RO", "RA", "YL")
    last.arrive("LO", "LB", "YR")
    last.side_arrive("own")
    add(0, 0)
    last.side_arrive("YO")
    add(1, 0)
    last.arrive("RQ", "RQA")
    last.arrive("LQ", "LQB")
    last.arrive("RA", "YO2")
    last.arrive("LB")
    last.arrive("YL")
    last.arrive("YR")
    last.side_arrive("RO")
    add(0, -1)
    last.side_arrive("LO")
    add(0, 1)
    last.arrive("RQA")
    last.arrive("LQB")
    last.arrive("YO2")
    last.side_arrive("RA", "LB")
    add(0, 2)
    last.side_arrive("RQ", "YL")
    add(1, -1)
    last.side_arrive("LQ", "YR")
    add(1, 1)
    last.side_arrive("RQA", "LQB", "YO2")
    add(1, 2)

    gather.finish()
    last.finish()
    states.finish()
    states_back.finish()
    for k in range(1, 8):
        ends.peer(k).wait_send()
    for k in range(1, DP):
        column_copy(k).wait_send()
    for k in range(2):
        teacher_move(k).wait_send()
    for leg in range(4):
        for k in (1, 2, 3):
            stream_leg(leg, k).wait_send()
            mid_leg(leg, k).wait_send()
    for k in range(1, TP):
        out_move(k).wait_send()
        gained_move(k).wait_send()


def split_kernel(packed, grad_c, grad_b, grad_x, grad_dt):
    grad_c[...] = packed[:, 0:512]
    grad_b[...] = packed[:, 512:640]
    grad_x[...] = packed[:, 640:768]
    grad_dt[...] = jnp.transpose(packed[:, 768:896])[0:HEADS, :]


VM = pl.BlockSpec(memory_space=pltpu.VMEM)
SM = pl.BlockSpec(memory_space=pltpu.SMEM)
ANY = pl.BlockSpec(memory_space=pl.ANY)


def struct(shape, dtype):
    return jax.ShapeDtypeStruct(shape, dtype)


def local(
    resid, teacher_mixed, gain_mix, gain_mlp, w_c, w_b, w_x, w_dt, dt_bias, decay_rate, skip, w_out,
    w_gate, w_up,
):
    gain_mix, gain_mlp = gain_mix.reshape(1, D), gain_mlp.reshape(1, D)
    packed = pl.pallas_call(
        whole_kernel,
        out_shape=struct((ROWS, PACK), F32),
        in_specs=[ANY, ANY, VM, VM, ANY, ANY, ANY, ANY, SM, SM, SM, ANY, ANY, ANY],
        out_specs=VM,
        scratch_shapes=list(SCRATCH.values()),
        compiler_params=pltpu.CompilerParams(
            collective_id=0, has_side_effects=True, vmem_limit_bytes=63 * MIB
        ),
        name="whole",
    )(
        resid, teacher_mixed, gain_mix, gain_mlp, w_c, w_b, w_x, w_dt.T, dt_bias, decay_rate, skip, w_out,
        w_gate, w_up,
    )
    grad_c, grad_b, grad_x, grad_dt = pl.pallas_call(
        split_kernel,
        out_shape=(
            struct((ROWS, 512), F32),
            struct((ROWS, 128), F32),
            struct((ROWS, 128), F32),
            struct((HEADS, ROWS), F32),
        ),
        in_specs=[VM],
        out_specs=(VM,) * 4,
        name="split",
    )(packed)
    return grad_c, grad_b, grad_x, grad_dt.T


def solution(mesh):
    in_specs = (
        P("dp", None),
        P("dp", None),
        P(),
        P(),
        P(None, "tensor"),
        P(None, "tensor"),
        P(None, "tensor"),
        P(None, "tensor"),
        P("tensor"),
        P("tensor"),
        P("tensor"),
        P("tensor", None),
        P("dp", "tensor"),
        P("dp", "tensor"),
    )
    out_specs = (P("dp", "tensor"), P("dp", "tensor"), P("dp", "tensor"), P("dp", "tensor"))
    return jax.shard_map(local, mesh=mesh, in_specs=in_specs, out_specs=out_specs, check_vma=False)
```

```python
import math
from types import SimpleNamespace

import jax
import jax.numpy as jnp
from jax import lax
from jax.experimental import pallas as pl
from jax.experimental.pallas import tpu as pltpu
from jax.sharding import PartitionSpec as P

D = 4096
FF = 14336
EPS = 1e-05
T = 128
HEADS = 4
DP = 16
TP = 8
HID = 1792
ROWS = 256
WIDTH = 512
PACK = 896
F32 = jnp.float32
BF16 = jnp.bfloat16
MESH = pl.DeviceIdType.MESH
MIB = 1024 * 1024

RIGHT, LEFT, ACROSS, SIDE = range(4)
FULL, PART, REST, HALF_A, HALF_B, REST_A, REST_B, HALF_A1, HALF_A2, HALF_B1, HALF_B2 = range(11)
RO, LO, YO, RQ, LQ, RA, LB, YL, YR, RQA, LQB, YO2, RO1, RO2, RO3, LO1, LO2, LO3, YO1, RX1, RX2, LX1, LX2, RXA, LXB, OWN = range(26)

LEGS = {
    RO: (RIGHT, 0, 0, FULL, 0, -1),
    LO: (LEFT, 0, 0, FULL, 0, 1),
    YO: (ACROSS, 0, 0, FULL, 1, 0),
    RQ: (RIGHT, 1, 0, REST, 1, -1),
    LQ: (LEFT, 1, 0, REST, 1, 1),
    RA: (RIGHT, 0, -1, HALF_A, 0, 2),
    LB: (LEFT, 0, 1, HALF_B, 0, 2),
    YL: (ACROSS, 0, -1, PART, 1, -1),
    YR: (ACROSS, 0, 1, PART, 1, 1),
    RQA: (RIGHT, 1, -1, REST_A, 1, 2),
    LQB: (LEFT, 1, 1, REST_B, 1, 2),
    YO2: (ACROSS, 0, 2, PART, 1, 2),
}
HALVES = {
    RO1: (RIGHT, 0, 0, HALF_A, 0, -1),
    RO2: (RIGHT, 0, 0, HALF_B1, 0, -1),
    RO3: (RIGHT, 0, 0, HALF_B2, 0, -1),
    LO2: (LEFT, 0, 0, HALF_B, 0, 1),
    LO1: (LEFT, 0, 0, HALF_A1, 0, 1),
    LO3: (LEFT, 0, 0, HALF_A2, 0, 1),
    YO1: (ACROSS, 0, 0, HALF_A, 1, 0),
    YO2: (ACROSS, 0, 0, HALF_B, 1, 0),
    RX1: (RIGHT, 1, 0, HALF_A, 1, -1),
    RX2: (RIGHT, 1, 0, HALF_B, 1, -1),
    LX1: (LEFT, 1, 0, HALF_A, 1, 1),
    LX2: (LEFT, 1, 0, HALF_B, 1, 1),
    RA: (RIGHT, 0, -1, HALF_A, 0, 2),
    LB: (LEFT, 0, 1, HALF_B, 0, 2),
    RXA: (RIGHT, 1, -1, HALF_A, 1, 2),
    LXB: (LEFT, 1, 1, HALF_B, 1, 2),
}
NSEM = 2 * len(LEGS) + 1
NSEM_HALF = 2 * len(HALVES) + 1


def place():
    me = lax.axis_index("dp")
    return me, me // 8, (me % 8) // 2, me % 2


class Gather:
    def __init__(self, legs, piece, rows, p, qa, send, recv, give=None):
        self.legs, self.order = legs, list(legs)
        self.piece, self.send, self.recv, self.give = piece, send, recv, give
        self.me, self.y, self.z, self.c = place()
        half = rows // 2
        self.rows = {
            FULL: (0, rows),
            PART: (0, p),
            REST: (p, rows - p),
            HALF_A: (0, half),
            HALF_B: (half, rows - half),
            HALF_A1: (0, half // 2),
            HALF_A2: (half // 2, half - half // 2),
            HALF_B1: (half, half // 2),
            HALF_B2: (half + half // 2, half - half // 2),
            REST_A: (p, qa),
            REST_B: (p + qa, rows - p - qa),
        }

    def block(self, flip, dz, core):
        y = self.y + flip - 2 * flip * self.y
        return y * 8 + ((self.z + dz + 4) % 4) * 2 + core

    def target(self, name):
        if name == RIGHT:
            return self.block(0, 1, self.c)
        if name == LEFT:
            return self.block(0, -1, self.c)
        if name == ACROSS:
            return self.block(1, 0, self.c)
        return self.block(0, 0, 1 - self.c)

    def copy(self, src, ref, sem, to):
        return pltpu.make_async_remote_copy(
            src_ref=src,
            dst_ref=ref,
            send_sem=self.send.at[sem],
            recv_sem=self.recv.at[sem],
            device_id={"dp": to},
            device_id_type=MESH,
        )

    def leg(self, name):
        to, flip, dz, rows, _, _ = self.legs[name]
        ref = self.piece(self.block(flip, dz, self.c), *self.rows[rows])
        src = ref
        if to == ACROSS and self.give is not None:
            src = self.give(*self.rows[rows])
        return self.copy(src, ref, self.order.index(name), self.target(to))

    def landed(self, name):
        to, _, _, rows, flip, dz = self.legs[name]
        ref = self.piece(self.block(flip, dz, self.c), *self.rows[rows])
        return self.copy(ref, ref, self.order.index(name), self.target(to))

    def side(self, name, core):
        if name == OWN:
            flip, dz, rows, sem = 0, 0, FULL, len(self.order)
        else:
            _, _, _, rows, flip, dz = self.legs[name]
            sem = len(self.order) + 1 + self.order.index(name)
        ref = self.piece(self.block(flip, dz, core), *self.rows[rows])
        return self.copy(ref, ref, sem, self.target(SIDE))

    def begin(self, *names):
        for name in names:
            self.leg(name).start()
        self.side(OWN, self.c).start()

    def arrive(self, name, *then):
        self.landed(name).wait_recv()
        for other in then:
            self.leg(other).start()
        self.side(name, self.c).start()

    def side_arrive(self, *names):
        for name in names:
            self.side(name, 1 - self.c).wait_recv()

    def finish(self):
        for name in self.order:
            self.leg(name).wait_send()
        for name in [OWN] + self.order:
            self.side(name, self.c).wait_send()


def iota(axis):
    return lax.broadcasted_iota(jnp.int32, (T, T), axis)


def mm(a, b):
    return jnp.dot(a.astype(BF16), b.astype(BF16), preferred_element_type=F32)


def mm_t(a, b):
    return lax.dot_general(
        a.astype(BF16), b.astype(BF16), (((1,), (1,)), ((), ())), preferred_element_type=F32
    )


def softplus(v):
    return jnp.maximum(v, 0.0) + jnp.log1p(jnp.exp(-jnp.abs(v)))


def steps_of(raw, params):
    step = softplus(raw + params[0:1, :])
    lower = (iota(0) >= iota(1)).astype(F32)
    decay = jnp.dot(
        lower, -step * params[1:2, :], preferred_element_type=F32, precision=lax.Precision.HIGHEST
    )
    return step, decay, jnp.transpose(step), jnp.transpose(decay)


def head(k):
    return slice(k * 128, (k + 1) * 128)


class States:
    def __init__(self, own, sib, chips, result, out, send, recv):
        self.own, self.sib, self.chips, self.result, self.out = own, sib, chips, result, out
        self.send, self.recv = send, recv
        self.me, self.y, self.z, self.c = place()
        self.q = self.me // 2
        self.mine = pl.ds(pl.multiple_of(self.c * 256, 256), 256)
        self.rest = pl.ds(pl.multiple_of((1 - self.c) * 256, 256), 256)

    def copy(self, src, dst, sem, to):
        return pltpu.make_async_remote_copy(
            src_ref=src,
            dst_ref=dst,
            send_sem=self.send.at[sem],
            recv_sem=self.recv.at[sem],
            device_id={"dp": to},
            device_id_type=MESH,
        )

    def share(self):
        return self.copy(self.own.at[:, self.rest], self.sib, 0, self.q * 2 + 1 - self.c)

    def peer(self, k, landing=False):
        at = self.chips.at[(self.q + 8 - k) % 8 if landing else self.q]
        return self.copy(at, at, k, ((self.q + k) % 8) * 2 + self.c)

    def hand(self, landing=False):
        lanes = self.rest if landing else self.mine
        return self.copy(self.result, self.out.at[:, lanes], 8, self.q * 2 + 1 - self.c)

    def wide(self, row):
        pick = [jnp.where(self.c == 0, row[:, i : i + 1], row[:, 2 + i : 3 + i]) for i in range(2)]
        lane = lax.broadcasted_iota(jnp.int32, (1, 256), 1)
        return jnp.where(lane < 128, pick[0], pick[1])

    def pair(self):
        mine, theirs = self.own[:, self.mine].astype(F32), self.sib[...].astype(F32)
        return jnp.where(self.c == 0, mine, theirs), jnp.where(self.c == 0, theirs, mine)

    def join(self, ends, forward):
        self.share().wait_recv()
        first, second = self.pair()
        if forward:
            total = self.wide(jnp.exp(ends[1])) * first + second
        else:
            total = first + self.wide(jnp.exp(ends[0])) * second
        self.chips[self.q] = total.astype(BF16)
        for k in (4, 1, 7, 2, 6, 3, 5):
            self.peer(k).start()

    def solve(self, ends, weights, forward):
        for k in range(1, 8):
            self.peer(k, True).wait_recv()
        total = jnp.zeros((128, 256), F32)
        for j in range(8):
            total = total + self.wide(weights[j : j + 1, :]) * self.chips[j].astype(F32)
        first, second = self.pair()
        if forward:
            near, far = total, self.wide(jnp.exp(ends[0])) * total + first
        else:
            near, far = second + self.wide(jnp.exp(ends[1])) * total, total
        self.result[...] = jnp.where(self.c == 0, far, near).astype(BF16)
        self.hand().start()
        self.out[:, self.mine] = jnp.where(self.c == 0, near, far).astype(BF16)

    def finish(self):
        self.share().wait_send()
        for k in range(1, 8):
            self.peer(k).wait_send()
        self.hand().wait_send()


def state_weights(decays, q, put):
    ends = [decays[2 * j, 0:1, :] + decays[2 * j + 1, 0:1, :] for j in range(8)]
    for at, order in enumerate((range(7, -1, -1), range(8))):
        run = jnp.zeros((1, 128), F32)
        for j in order:
            reached = ((j < q) if at == 0 else (j > q)).astype(F32)
            put[at, j : j + 1, :] = reached * jnp.exp(run)
            run = run + reached * ends[j]


def spread(scalars):
    lane = lax.broadcasted_iota(jnp.int32, (1, 128), 1)
    row = jnp.zeros((1, 128), F32)
    for h in range(HEADS):
        row = jnp.where(lane == h, scalars[h], row)
    return row


SCRATCH = dict(
    held=pltpu.VMEM((DP, ROWS, HID), BF16),
    give=pltpu.VMEM((ROWS, HID), BF16),
    v_wc=pltpu.VMEM((D, 512), BF16),
    v_wb=pltpu.VMEM((D, 128), BF16),
    v_wx=pltpu.VMEM((D, 128), BF16),
    v_wdt=pltpu.VMEM((HEADS, D), BF16),
    v_out=pltpu.VMEM((TP, 512, WIDTH), BF16),
    v_resid=pltpu.VMEM((T, WIDTH), BF16),
    nin=pltpu.VMEM((T, D), BF16),
    lhs=pltpu.VMEM((4 * T, D), BF16),
    acc=pltpu.VMEM((4 * T, HID), F32),
    proj=pltpu.VMEM((T, PACK), F32),
    read=pltpu.VMEM((T, WIDTH), BF16),
    state=pltpu.VMEM((128, WIDTH), BF16),
    sib=pltpu.VMEM((128, 256), BF16),
    chips=pltpu.VMEM((8, 128, 256), BF16),
    result=pltpu.VMEM((128, 256), BF16),
    decays=pltpu.VMEM((DP, 8, 128), F32),
    weights=pltpu.VMEM((2, 8, 128), F32),
    steps=pltpu.VMEM((4, T, 128), F32),
    read_t=pltpu.VMEM((HEADS, 128, T), BF16),
    enter=pltpu.VMEM((128, WIDTH), BF16),
    through=pltpu.VMEM((T, WIDTH), F32),
    mixer_out=pltpu.VMEM((T, WIDTH), BF16),
    fade=pltpu.VMEM((HEADS, T, T), F32),
    plain=pltpu.VMEM((HEADS, T, T), F32),
    p_send=pltpu.VMEM((TP, T, WIDTH), BF16),
    p_recv=pltpu.VMEM((TP, T, WIDTH), BF16),
    str_a=pltpu.VMEM((4, 4, T // 2, WIDTH), BF16),
    str_b=pltpu.VMEM((4, 4, T // 2, WIDTH), BF16),
    mid_a=pltpu.VMEM((4, 4, T // 2, WIDTH), BF16),
    mid_b=pltpu.VMEM((4, 4, T // 2, WIDTH), BF16),
    got_a=pltpu.VMEM((3, 4, T // 2, WIDTH), BF16),
    got_b=pltpu.VMEM((3, 4, T // 2, WIDTH), BF16),
    sum_a=pltpu.VMEM((4, T // 2, WIDTH), BF16),
    sum_b=pltpu.VMEM((4, T // 2, WIDTH), BF16),
    end_a=pltpu.VMEM((3, T // 2, WIDTH), BF16),
    end_b=pltpu.VMEM((3, T // 2, WIDTH), BF16),
    gained=pltpu.VMEM((TP, T, WIDTH), BF16),
    grads=pltpu.VMEM((2 * T, HID), BF16),
    squares=pltpu.VMEM((2, T, 128), F32),
    out_grad=pltpu.VMEM((T, WIDTH), F32),
    along=pltpu.VMEM((T, WIDTH), F32),
    b_state=pltpu.VMEM((128, WIDTH), BF16),
    b_sib=pltpu.VMEM((128, 256), BF16),
    b_chips=pltpu.VMEM((8, 128, 256), BF16),
    b_result=pltpu.VMEM((128, 256), BF16),
    behind=pltpu.VMEM((128, WIDTH), BF16),
    packed=pltpu.VMEM((DP, T, PACK - WIDTH), BF16),
    read4=pltpu.VMEM((HEADS * T, 128), BF16),
    weight4=pltpu.VMEM((HEADS * T, T), BF16),
    grad4=pltpu.VMEM((HEADS * T, 128), BF16),
    dscore4=pltpu.VMEM((HEADS * T, T), BF16),
    across=pltpu.VMEM((HEADS, T, 128), F32),
    dinject=pltpu.VMEM((T, 128), F32),
    dvalue=pltpu.VMEM((T, 128), F32),
    in_sem=pltpu.SemaphoreType.DMA((11 + TP,)),
    g_send=pltpu.SemaphoreType.DMA((NSEM_HALF,)),
    g_recv=pltpu.SemaphoreType.DMA((NSEM_HALF,)),
    a_send=pltpu.SemaphoreType.DMA((2,)),
    a_recv=pltpu.SemaphoreType.DMA((2,)),
    h_send=pltpu.SemaphoreType.DMA((NSEM,)),
    h_recv=pltpu.SemaphoreType.DMA((NSEM,)),
    i_send=pltpu.SemaphoreType.DMA((NSEM,)),
    i_recv=pltpu.SemaphoreType.DMA((NSEM,)),
    s_send=pltpu.SemaphoreType.DMA((9,)),
    s_recv=pltpu.SemaphoreType.DMA((9,)),
    d_send=pltpu.SemaphoreType.DMA((DP - 1,)),
    d_recv=pltpu.SemaphoreType.DMA((DP - 1,)),
    b_send=pltpu.SemaphoreType.DMA((9,)),
    b_recv=pltpu.SemaphoreType.DMA((9,)),
    c_send=pltpu.SemaphoreType.DMA((DP - 1,)),
    c_recv=pltpu.SemaphoreType.DMA((DP - 1,)),
    t_send=pltpu.SemaphoreType.DMA((2, TP)),
    t_recv=pltpu.SemaphoreType.DMA((2, TP)),
    p1_send=pltpu.SemaphoreType.DMA((12,)),
    p1_recv=pltpu.SemaphoreType.DMA((12,)),
    p2_send=pltpu.SemaphoreType.DMA((12,)),
    p2_recv=pltpu.SemaphoreType.DMA((12,)),
)


def chunk(k, size=256):
    return pl.ds(pl.multiple_of(k * size, size), size)


def columns(p):
    return chunk(p, WIDTH)


def normalise(ref, rows, gain):
    total = jnp.zeros((T, 1), F32)
    for k in range(8):
        part = ref[rows, k * 512 : (k + 1) * 512].astype(F32)
        total = total + jnp.sum(part * part, axis=1, keepdims=True)
    scale = lax.rsqrt(total / D + EPS)
    for k in range(8):
        at = slice(k * 512, (k + 1) * 512)
        ref[rows, at] = (ref[rows, at].astype(F32) * scale * gain[:, at]).astype(BF16)


def whole_kernel(
    resid, teacher, gain_mix, gain_mlp, w_c, w_b, w_x, w_dt, bias, rate, skip, w_out, w_gate, w_up, out, *scratch
):
    s = SimpleNamespace(**dict(zip(SCRATCH, scratch)))
    me, y, z, c = place()
    m = me % 8
    t = lax.axis_index("tensor")
    other = (1 - y) * 8 + m
    half = HID // 2
    keep = pl.ds(pl.multiple_of(y * half, 128), half)
    rest = pl.ds(pl.multiple_of((1 - y) * half, 128), half)
    mine = pl.ds(pl.multiple_of(y * T, T), T)
    pairs = (
        (w_gate.at[:, keep], s.held.at[me, :, 0:half]),
        (w_up.at[:, keep], s.held.at[me, :, half:HID]),
        (w_gate.at[:, rest], s.give.at[:, 0:half]),
        (w_up.at[:, rest], s.give.at[:, half:HID]),
        (resid, s.nin),
        (w_c, s.v_wc),
        (w_b, s.v_wb),
        (w_x, s.v_wx),
        (w_dt, s.v_wdt),
        (teacher, s.lhs.at[mine, :]),
        (resid.at[:, columns(t)], s.v_resid),
    ) + tuple((w_out.at[:, p * WIDTH : (p + 1) * WIDTH], s.v_out.at[p]) for p in range(TP))
    loads = [pltpu.make_async_copy(a, b, s.in_sem.at[k]) for k, (a, b) in enumerate(pairs)]
    for copy in loads:
        copy.start()
    sem = pltpu.get_barrier_semaphore()
    for k in range(1, DP):
        pl.semaphore_signal(sem, inc=1, device_id={"dp": (me + k) % DP}, device_id_type=MESH)
    for k in range(1, TP):
        for dp in (me, other):
            pl.semaphore_signal(
                sem, inc=1, device_id={"dp": dp, "tensor": (t + k) % TP}, device_id_type=MESH
            )
    loads[4].wait()
    normalise(s.nin, slice(None), gain_mix)
    pl.semaphore_wait(sem, DP - 1 + 2 * (TP - 1))
    for copy in loads[0:4]:
        copy.wait()
    gather = Gather(
        HALVES,
        lambda j, start, size: s.held.at[j, pl.ds(start, size), :],
        ROWS,
        112,
        64,
        s.g_send,
        s.g_recv,
        lambda start, size: s.give.at[pl.ds(start, size), :],
    )
    gather.begin(RO1, LO2, YO1)

    bias_row, rate_row, skip_row = spread(bias), spread(rate), spread(skip)
    params = jnp.concatenate([bias_row, rate_row, skip_row, jnp.zeros((5, 128), F32)], axis=0)
    for copy in loads[5:9]:
        copy.wait()
    rows = s.nin[...]
    s.proj[:, 0:512] = jnp.dot(rows, s.v_wc[...], preferred_element_type=F32)
    s.proj[:, 512:640] = jnp.dot(rows, s.v_wb[...], preferred_element_type=F32)
    s.proj[:, 640:768] = jnp.dot(rows, s.v_wx[...], preferred_element_type=F32)
    s.proj[:, 768:896] = jnp.zeros((T, 128), F32)
    s.proj[:, 768 : 768 + HEADS] = mm_t(rows, s.v_wdt[...])
    s.read[...] = s.proj[:, 0:512].astype(BF16)
    inject, values = s.proj[:, 512:640], s.proj[:, 640:768]
    raw = s.proj[:, 768:896]
    gather.leg(RO2).start()
    gather.leg(LO1).start()
    step, decay, step_t, decay_t = steps_of(raw, params)
    s.decays[me] = jnp.broadcast_to(decay[T - 1 : T, :], (8, 128))

    def ends_move(k):
        ref = s.decays.at[me]
        return pltpu.make_async_remote_copy(
            src_ref=ref,
            dst_ref=ref,
            send_sem=s.d_send.at[k - 1],
            recv_sem=s.d_recv.at[k - 1],
            device_id={"dp": (me + k) % DP},
            device_id_type=MESH,
        )

    def ends_landed(k):
        ref = s.decays.at[(me - k + DP) % DP]
        return pltpu.make_async_remote_copy(
            src_ref=ref,
            dst_ref=ref,
            send_sem=s.d_send.at[k - 1],
            recv_sem=s.d_recv.at[k - 1],
            device_id={"dp": (me + k) % DP},
            device_id_type=MESH,
        )

    for k in range(1, DP):
        ends_move(k).start()
    causal = iota(0) >= iota(1)
    inject_t = jnp.transpose(inject)
    for h in range(HEADS):
        s.read4[head(h), :] = s.read[:, head(h)]
    score = mm_t(s.read4[...], inject)
    pulls = []
    for h in range(HEADS):
        row, col, step_row = decay_t[h : h + 1, :], decay[:, h : h + 1], step_t[h : h + 1, :]
        s.fade[h] = jnp.exp(jnp.where(causal, col - row, -1e30))
        s.plain[h] = s.fade[h] * score[head(h), :]
        s.weight4[head(h), :] = (s.plain[h] * step_row).astype(BF16)
        pulls.append(inject_t * (jnp.exp(row[:, T - 1 : T] - row) * step_row))
    carried = mm(jnp.concatenate(pulls, axis=0), values)
    for h in range(HEADS):
        s.state[:, head(h)] = carried[head(h), :].astype(BF16)
    q = me // 2
    states = States(s.state, s.sib, s.chips, s.result, s.enter, s.s_send, s.s_recv)
    states.share().start()
    through = mm(s.weight4[...], values)
    for h in range(HEADS):
        s.through[:, head(h)] = through[head(h), :] + skip_row[:, h : h + 1] * values
    for k, value in enumerate((step, decay, step_t, decay_t)):
        s.steps[k] = value
    ends_landed(jnp.where(c == 0, DP - 1, 1)).wait_recv()
    chip_ends = [s.decays[2 * q + i, 0:1, :] for i in range(2)]
    states.join(chip_ends, True)
    gather.leg(YO2).start()
    gather.leg(RO3).start()
    gather.leg(LO3).start()

    loads[9].wait()
    normalise(s.lhs, mine, gain_mlp)
    gather.arrive(RO1, RA)
    gather.arrive(LO2, LB)
    gather.arrive(YO1, RX1, LX1)

    def teacher_move(k):
        ref = s.lhs.at[pl.ds(pl.multiple_of(y * T + k * (T // 2), T // 2), T // 2), :]
        return pltpu.make_async_remote_copy(
            src_ref=ref,
            dst_ref=ref,
            send_sem=s.a_send.at[k],
            recv_sem=s.a_recv.at[k],
            device_id={"dp": other, "tensor": (t + 4 * k) % TP},
            device_id_type=MESH,
        )

    def teacher_landed(k):
        ref = s.lhs.at[pl.ds(pl.multiple_of((1 - y) * T + k * (T // 2), T // 2), T // 2), :]
        return pltpu.make_async_remote_copy(
            src_ref=ref,
            dst_ref=ref,
            send_sem=s.a_send.at[k],
            recv_sem=s.a_recv.at[k],
            device_id={"dp": other, "tensor": (t + 4 * k) % TP},
            device_id_type=MESH,
        )

    for k in range(2, DP - 1):
        ends_landed(k).wait_recv()
    ends_landed(jnp.where(c == 0, 1, DP - 1)).wait_recv()
    state_weights(s.decays, q, s.weights)
    states.solve(chip_ends, s.weights[0], True)
    states.hand(True).wait_recv()
    for h in range(HEADS):
        grown = jnp.exp(decay[:, h : h + 1]) * mm(s.read[:, head(h)], s.enter[:, head(h)])
        s.mixer_out[:, head(h)] = (s.through[:, head(h)] + grown).astype(BF16)

    def move(phase, kt, src, dst):
        return pltpu.make_async_remote_copy(
            src_ref=src,
            dst_ref=dst,
            send_sem=s.t_send.at[phase, kt],
            recv_sem=s.t_recv.at[phase, kt],
            device_id={"tensor": (t + kt) % TP},
            device_id_type=MESH,
        )

    def out_move(kt):
        return move(0, kt, s.p_send.at[kt], s.p_recv.at[kt])

    def gained_move(kt):
        return move(1, kt, s.gained.at[t], s.gained.at[t])

    def gained_landed(kt):
        at = s.gained.at[(t - kt + TP) % TP]
        return move(1, kt, at, at)

    px, py = t % 4, (t // 4) * 2 + y

    def plane(sems, leg, over_x, k, src, dst):
        xx = (px + k) % 4 if over_x else px
        yy = py if over_x else (py + k) % 4
        return pltpu.make_async_remote_copy(
            src_ref=src,
            dst_ref=dst,
            send_sem=sems[0].at[3 * leg + k - 1],
            recv_sem=sems[1].at[3 * leg + k - 1],
            device_id={"dp": (yy % 2) * 8 + m, "tensor": (yy // 2) * 4 + xx},
            device_id_type=MESH,
        )

    def stream_leg(leg, k, landing=False):
        d = (4 - k) if landing else 0
        ref = (
            s.str_a.at[py, (px + d) % 4],
            s.str_b.at[px, (py + d) % 4],
            s.str_a.at[(py + d) % 4],
            s.str_b.at[(px + d) % 4],
        )[leg]
        return plane((s.p1_send, s.p1_recv), leg, leg in (0, 3), k, ref, ref)

    def mid_leg(leg, k):
        src, dst = (
            (s.mid_a.at[(px + k) % 4], s.got_a.at[k - 1]),
            (s.mid_b.at[(py + k) % 4], s.got_b.at[k - 1]),
            (s.sum_a.at[(py + k) % 4], s.end_a.at[k - 1]),
            (s.sum_b.at[(px + k) % 4], s.end_b.at[k - 1]),
        )[leg]
        return plane((s.p2_send, s.p2_recv), leg, leg in (0, 3), k, src, dst)

    def stream_block(yy, p):
        row, col = 2 * (p // 4) + yy, p % 4
        return jnp.concatenate([s.str_a[row, col], s.str_b[col, row]], axis=0)

    def out_part(p):
        return jnp.dot(s.mixer_out[...], s.v_out[p], preferred_element_type=F32)

    for copy in loads[10:]:
        copy.wait()

    def out_send(k, _):
        s.p_send[k] = out_part((t + k) % TP).astype(BF16)
        out_move(k).start()
        return 0

    lax.fori_loop(1, TP, out_send, 0)
    stream = out_part(t) + s.v_resid[...].astype(F32)
    gather.arrive(YO2, LX2, RX2)
    gather.arrive(RO2)
    gather.arrive(LO1)
    gather.arrive(RO3)
    gather.arrive(LO3)
    for k in range(1, TP):
        out_move(k).wait_recv()
        stream = stream + s.p_recv[k].astype(F32)
    half_rows = T // 2
    s.str_a[py, px] = stream[0:half_rows].astype(BF16)
    s.str_b[px, py] = stream[half_rows:T].astype(BF16)
    for k in (2, 1, 3):
        stream_leg(0, k).start()
        stream_leg(1, k).start()

    def column_copy(k):
        to = (k // 8 + y) % 2 * 8 + (m + k) % 8
        return pltpu.make_async_remote_copy(
            src_ref=s.v_wx.at[chunk(to), :],
            dst_ref=s.v_wb.at[chunk(me), :],
            send_sem=s.c_send.at[k - 1],
            recv_sem=s.c_recv.at[k - 1],
            device_id={"dp": to},
            device_id_type=MESH,
        )

    def column_landed(k):
        at = (k // 8 + y) % 2 * 8 + (m - k + DP) % 8
        return pltpu.make_async_remote_copy(
            src_ref=s.v_wx.at[chunk(at), :],
            dst_ref=s.v_wb.at[chunk(at), :],
            send_sem=s.c_send.at[k - 1],
            recv_sem=s.c_recv.at[k - 1],
            device_id={"dp": at},
            device_id_type=MESH,
        )

    near, far = range(1, 8), range(8, DP)

    upper_rows, lower_rows = pl.ds(0, 2 * T), pl.ds(2 * T, 2 * T)

    def use(flip, dz, rows=upper_rows):
        base = gather.block(flip, dz, 0)
        s.acc[rows, :] += jnp.dot(
            s.lhs[rows, chunk(base)], s.held[base], preferred_element_type=F32
        ) + jnp.dot(s.lhs[rows, chunk(base + 1)], s.held[base + 1], preferred_element_type=F32)

    def turn(k, _):
        s.v_wx[chunk(k), :] = jnp.transpose(s.nin[:, chunk(k)].astype(F32)).astype(BF16)
        return 0

    lax.fori_loop(0, DP, turn, 0)
    growth_t = jnp.exp(s.steps[3])
    for h in range(HEADS):
        s.read_t[h] = (jnp.transpose(s.read[:, head(h)].astype(F32)) * growth_t[h : h + 1, :]).astype(BF16)
    s.acc[...] = jnp.zeros_like(s.acc)
    for k in (2, 1, 3):
        stream_leg(0, k, True).wait_recv()
    for k in (2, 1, 3):
        stream_leg(2, k).start()
    for k in (2, 1, 3):
        stream_leg(1, k, True).wait_recv()
    for k in (2, 1, 3):
        stream_leg(3, k).start()
    teacher_move(0).start()
    teacher_move(1).start()
    gather.arrive(RX1, RXA)
    gather.arrive(RA)
    gather.arrive(LB)
    gather.arrive(LX1)
    gather.arrive(LX2, LXB)
    gather.arrive(RX2)

    for leg in (2, 3):
        for k in (2, 1, 3):
            stream_leg(leg, k, True).wait_recv()
    s.squares[...] = jnp.zeros_like(s.squares)

    def student_rows(p, _):
        for yy in range(2):
            part = stream_block(yy, p).astype(F32)
            s.squares[yy] += jnp.broadcast_to(jnp.sum(part * part, axis=1, keepdims=True), (T, 128))
            s.lhs[pl.ds((2 + yy) * T, T), columns(p)] = (part * gain_mlp[:, columns(p)]).astype(BF16)
        return 0

    lax.fori_loop(0, TP, student_rows, 0)

    def student(i, _):
        use(i % 2, jnp.where(i < 2, 0, jnp.where(i < 4, 3, jnp.where(i < 6, 1, 2))), lower_rows)
        return 0

    gather.side_arrive(OWN, YO1, YO2, RO1, RO2, RO3, LO1, LO2, LO3, RA, LB, RX1, RX2, LX1, LX2)
    lax.fori_loop(0, 7, student, 0)
    teacher_landed(0).wait_recv()
    teacher_landed(1).wait_recv()
    for k in far:
        column_copy(k).start()
    gather.arrive(RXA)
    gather.arrive(LXB)

    def teach(i, _):
        use(i % 2, jnp.where(i < 2, 0, jnp.where(i < 4, 3, jnp.where(i < 6, 1, 2))))
        return 0

    lax.fori_loop(0, 7, teach, 0)
    gather.side_arrive(RXA, LXB)
    use(1, 2, slice(None))
    scales = [lax.rsqrt(s.squares[yy, :, 0:1] / D + EPS) for yy in range(2)]
    scale = jnp.where(y == 0, scales[0], scales[1])
    both = jnp.concatenate(scales, axis=0)

    for n in range(half // 128):
        at, beside = slice(n * 128, (n + 1) * 128), slice(half + n * 128, half + (n + 1) * 128)
        aim_gate = s.acc[upper_rows, at]
        aim = aim_gate * jax.nn.sigmoid(aim_gate) * s.acc[upper_rows, beside]
        gate, up = s.acc[lower_rows, at] * both, s.acc[lower_rows, beside] * both
        sigma = jax.nn.sigmoid(gate)
        silu = gate * sigma
        grad = (2.0 / math.sqrt(FF)) * (silu * up - aim)
        s.grads[:, at] = (grad * up * sigma * (1.0 + gate * (1.0 - sigma))).astype(BF16)
        s.grads[:, beside] = (grad * silu).astype(BF16)

    def back(yh, xx):
        for i in range(2):
            part = mm_t(s.grads[...], s.held[2 * (yh * 4 + xx) + i]).astype(BF16)
            lanes_at = slice(i * 256, (i + 1) * 256)
            for yy in range(2):
                s.mid_a[xx, 2 * yh + yy, :, lanes_at] = part[yy * T : yy * T + half_rows, :]
                s.mid_b[2 * yh + yy, xx, :, lanes_at] = part[yy * T + half_rows : (yy + 1) * T, :]

    def back_far(xx, _):
        back(1 - t // 4, xx)
        return 0

    lax.fori_loop(0, 4, back_far, 0)
    mid_leg(1, 2).start()

    @pl.when(y == 0)
    def _():
        mid_leg(1, 3).start()

    @pl.when(y == 1)
    def _():
        mid_leg(1, 1).start()

    back(t // 4, (px + 2) % 4)
    mid_leg(0, 2).start()
    back(t // 4, (px + 1) % 4)
    mid_leg(0, 1).start()
    back(t // 4, (px + 3) % 4)
    mid_leg(0, 3).start()
    back(t // 4, px)

    @pl.when(y == 0)
    def _():
        mid_leg(1, 1).start()

    @pl.when(y == 1)
    def _():
        mid_leg(1, 3).start()

    for k in near:
        column_copy(k).start()
    s.v_wb[chunk(me), :] = s.v_wx[chunk(me), :]
    s.along[...] = jnp.zeros_like(s.along)

    def stream_part(p, _):
        s.along[...] += mm_t(stream_block(y, p), s.v_out[p])
        return 0

    lax.fori_loop(0, TP, stream_part, 0)

    def fold(own, got, sums):
        for at in range(4):
            total = own[at].astype(F32)
            for k in range(3):
                total = total + got[k, at].astype(F32)
            sums[at] = total.astype(BF16)

    for k in (2, 1, 3):
        mid_leg(0, k).wait_recv()
    fold(s.mid_a.at[px], s.got_a, s.sum_a)
    for k in (2, 1, 3):
        mid_leg(2, k).start()
    for k in (2, 1, 3):
        mid_leg(1, k).wait_recv()
    fold(s.mid_b.at[py], s.got_b, s.sum_b)
    for k in (2, 1, 3):
        mid_leg(3, k).start()
    parts = []
    for leg, own, ends_of in ((2, s.sum_a.at[py], s.end_a), (3, s.sum_b.at[px], s.end_b)):
        total = own[...].astype(F32)
        for k in (2, 1, 3):
            mid_leg(leg, k).wait_recv()
            total = total + ends_of[k - 1].astype(F32)
        parts.append(total)
    mid = jnp.concatenate(parts, axis=0)
    s.gained[t] = (mid * gain_mlp[:, columns(t)]).astype(BF16)
    for k in range(1, TP):
        gained_move(k).start()
    s.out_grad[...] = jnp.zeros_like(s.out_grad)

    def unproject(kt, inner):
        @pl.when(kt > 0)
        def _():
            gained_landed(kt).wait_recv()

        p = (t - kt + TP) % TP
        part = s.gained[p]
        s.out_grad[...] += mm_t(part, s.v_out[p])
        return inner + jnp.sum(part.astype(F32) * stream_block(y, p).astype(F32), axis=1, keepdims=True)

    inner = lax.fori_loop(0, TP, unproject, jnp.zeros((T, 1), F32))
    pull = scale * scale * scale * (inner / D)
    s.out_grad[...] = s.out_grad[...] * scale - s.along[...] * pull

    inject, values = s.proj[:, 512:640], s.proj[:, 640:768]
    raw = s.proj[:, 768:896]
    step, decay, step_t, decay_t = [s.steps[k] for k in range(4)]
    growth = jnp.exp(decay)
    for h in range(HEADS):
        s.b_state[:, head(h)] = mm(s.read_t[h], s.out_grad[:, head(h)]).astype(BF16)
    states_back = States(s.b_state, s.b_sib, s.b_chips, s.b_result, s.behind, s.b_send, s.b_recv)
    states_back.share().start()
    early = Gather(
        LEGS, lambda j, start, size: s.v_wc.at[pl.ds(pl.multiple_of(j * T + start, 16), size), :], T, 48, 48, s.h_send, s.h_recv
    )
    last = Gather(
        LEGS, lambda j, start, size: s.packed.at[j, pl.ds(start, size), :], T, 48, 48, s.i_send, s.i_recv
    )
    lanes = lax.broadcasted_iota(jnp.int32, (1, 128), 1)
    for h in range(HEADS):
        s.grad4[head(h), :] = s.out_grad[:, head(h)].astype(BF16)
    dweight = mm_t(s.grad4[...], values)
    for h in range(HEADS):
        s.dscore4[head(h), :] = (dweight[head(h), :] * s.fade[h] * step_t[h : h + 1, :]).astype(BF16)
        s.across[h] = growth[:, h : h + 1] * mm_t(s.grad4[head(h), :], s.enter[:, head(h)])
    inner_read = mm(s.dscore4[...], inject)
    chip_ends = [s.decays[2 * q + i, 0:1, :] for i in range(2)]
    states_back.join(chip_ends, False)
    for h in range(HEADS):
        s.v_wc[chunk(me, T), head(h)] = (inner_read[head(h), :] + s.across[h]).astype(BF16)
    early.begin(RO, LO, YO)
    step_rows, decay_rows, decay_cols = [], [], []
    skipped = jnp.zeros((T, 128), F32)
    for h in range(HEADS):
        step_row = step_t[h : h + 1, :]
        direct = dweight[head(h), :] * s.plain[h]
        skipped = skipped + skip_row[:, h : h + 1] * s.out_grad[:, head(h)]
        column = jnp.sum(direct, axis=0, keepdims=True)
        step_rows.append(column)
        decay_rows.append(-column * step_row)
        both_ways = direct * step_row + s.across[h] * s.read[:, head(h)].astype(F32)
        decay_cols.append(jnp.sum(both_ways, axis=1, keepdims=True))
    rows_dot = (((0,), (0,)), ((), ()))
    s.dinject[...] = lax.dot_general(s.dscore4[...], s.read4[...], rows_dot, preferred_element_type=F32)
    s.dvalue[...] = skipped + lax.dot_general(
        s.weight4[...], s.grad4[...], rows_dot, preferred_element_type=F32
    )
    states_back.solve(chip_ends, s.weights[1], False)
    early.arrive(YO, RQ, LQ)
    early.arrive(RO, RA, YL)
    early.arrive(LO, LB, YR)
    states_back.hand(True).wait_recv()
    dstep = jnp.zeros((T, 128), F32)
    ddecay = jnp.zeros((T, 128), F32)
    drawn_values = mm(inject, s.behind[...])
    dinject, dvalue = s.dinject[...], s.dvalue[...]
    final = (lax.broadcasted_iota(jnp.int32, (T, 1), 0) == T - 1).astype(F32)
    tails = jnp.exp(decay[T - 1 : T, :] - decay)
    for h in range(HEADS):
        tail_col = tails[:, h : h + 1]
        scaled_col = tail_col * step[:, h : h + 1]
        pulled = mm_t(values, s.behind[:, head(h)])
        dinject = dinject + scaled_col * pulled
        dvalue = dvalue + scaled_col * drawn_values[:, head(h)]
        drawn = tail_col * jnp.sum(inject * pulled, axis=1, keepdims=True)
        moved = drawn * step[:, h : h + 1]
        product = s.behind[:, head(h)].astype(F32) * s.enter[:, head(h)].astype(F32)
        kept = jnp.exp(decay[T - 1 : T, h : h + 1]) * jnp.sum(
            jnp.sum(product, axis=0, keepdims=True), axis=1, keepdims=True
        )
        end = kept + jnp.sum(moved, axis=0, keepdims=True)
        onehot = (lanes == h).astype(F32)
        dstep = dstep + drawn * onehot
        ddecay = ddecay + (decay_cols[h] - moved + final * end) * onehot
    s.packed[me, :, 0:128] = dinject.astype(BF16)
    s.packed[me, :, 128:256] = dvalue.astype(BF16)
    zero = jnp.zeros((128 - HEADS, 128), F32)
    dstep = dstep + jnp.transpose(jnp.concatenate(step_rows + [zero], axis=0))
    ddecay = ddecay + jnp.transpose(jnp.concatenate(decay_rows + [zero], axis=0))
    upper = (iota(0) <= iota(1)).astype(F32)
    later = jnp.dot(upper, ddecay, preferred_element_type=F32, precision=lax.Precision.HIGHEST)
    draw = (dstep - rate_row * later) * jax.nn.sigmoid(raw + bias_row)
    s.packed[me, :, 256:384] = draw.astype(BF16)

    last.begin(RO, LO, YO)
    out[...] = jnp.zeros_like(out)
    for k in range(1, DP):
        column_landed(k).wait_recv()

    def add(lanes_at, base, first, second):
        out[:, lanes_at] += jnp.dot(s.v_wb[chunk(base), :], first, preferred_element_type=F32) + jnp.dot(
            s.v_wb[chunk(base + 1), :], second, preferred_element_type=F32
        )

    def add_c(flip, dz):
        base = early.block(flip, dz, 0)
        add(slice(0, WIDTH), base, s.v_wc[chunk(base, T), :], s.v_wc[chunk(base + 1, T), :])

    def add_rest(flip, dz):
        base = last.block(flip, dz, 0)
        add(slice(WIDTH, PACK), base, s.packed[base], s.packed[base + 1])

    early.arrive(RQ, RQA)
    early.arrive(LQ, LQB)
    early.arrive(RA, YO2)
    early.arrive(LB)
    early.arrive(YL)
    early.arrive(YR)
    early.side_arrive(OWN)
    add_c(0, 0)
    early.side_arrive(YO)
    add_c(1, 0)
    last.arrive(YO, RQ, LQ)
    last.arrive(RO, RA, YL)
    last.arrive(LO, LB, YR)
    early.arrive(RQA)
    early.arrive(LQB)
    early.arrive(YO2)
    early.side_arrive(RO)
    add_c(0, -1)
    early.side_arrive(LO)
    add_c(0, 1)
    last.arrive(RQ, RQA)
    last.arrive(LQ, LQB)
    last.arrive(RA, YO2)
    last.arrive(LB)
    last.arrive(YL)
    last.arrive(YR)
    early.side_arrive(RA, LB)
    add_c(0, 2)
    early.side_arrive(RQ, YL)
    add_c(1, -1)
    early.side_arrive(LQ, YR)
    add_c(1, 1)
    early.side_arrive(RQA, LQB, YO2)
    add_c(1, 2)
    last.arrive(RQA)
    last.arrive(LQB)
    last.arrive(YO2)
    last.side_arrive(OWN)
    add_rest(0, 0)
    last.side_arrive(YO)
    add_rest(1, 0)
    last.side_arrive(RO)
    add_rest(0, -1)
    last.side_arrive(LO)
    add_rest(0, 1)
    last.side_arrive(RA, LB)
    add_rest(0, 2)
    last.side_arrive(RQ, YL)
    add_rest(1, -1)
    last.side_arrive(LQ, YR)
    add_rest(1, 1)
    last.side_arrive(RQA, LQB, YO2)
    add_rest(1, 2)

    gather.finish()
    early.finish()
    last.finish()
    states.finish()
    states_back.finish()
    for k in range(1, DP):
        ends_move(k).wait_send()
        column_copy(k).wait_send()
    for k in range(2):
        teacher_move(k).wait_send()
    for leg in range(4):
        for k in (1, 2, 3):
            stream_leg(leg, k).wait_send()
            mid_leg(leg, k).wait_send()
    for k in range(1, TP):
        out_move(k).wait_send()
        gained_move(k).wait_send()


def split_kernel(packed, grad_c, grad_b, grad_x, grad_dt):
    grad_c[...] = packed[:, 0:512]
    grad_b[...] = packed[:, 512:640]
    grad_x[...] = packed[:, 640:768]
    grad_dt[...] = jnp.transpose(packed[:, 768:896])[0:HEADS, :]


VM = pl.BlockSpec(memory_space=pltpu.VMEM)
SM = pl.BlockSpec(memory_space=pltpu.SMEM)
ANY = pl.BlockSpec(memory_space=pl.ANY)


def struct(shape, dtype):
    return jax.ShapeDtypeStruct(shape, dtype)


def local(
    resid, teacher_mixed, gain_mix, gain_mlp, w_c, w_b, w_x, w_dt, dt_bias, decay_rate, skip, w_out,
    w_gate, w_up,
):
    gain_mix, gain_mlp = gain_mix.reshape(1, D), gain_mlp.reshape(1, D)
    packed = pl.pallas_call(
        whole_kernel,
        out_shape=struct((ROWS, PACK), F32),
        in_specs=[ANY, ANY, VM, VM, ANY, ANY, ANY, ANY, SM, SM, SM, ANY, ANY, ANY],
        out_specs=VM,
        scratch_shapes=list(SCRATCH.values()),
        compiler_params=pltpu.CompilerParams(
            collective_id=0, has_side_effects=True, vmem_limit_bytes=63 * MIB
        ),
        name="whole",
    )(
        resid, teacher_mixed, gain_mix, gain_mlp, w_c, w_b, w_x, w_dt.T, dt_bias, decay_rate, skip, w_out,
        w_gate, w_up,
    )
    grad_c, grad_b, grad_x, grad_dt = pl.pallas_call(
        split_kernel,
        out_shape=(
            struct((ROWS, 512), F32),
            struct((ROWS, 128), F32),
            struct((ROWS, 128), F32),
            struct((HEADS, ROWS), F32),
        ),
        in_specs=[VM],
        out_specs=(VM,) * 4,
        name="split",
    )(packed)
    return grad_c, grad_b, grad_x, grad_dt.T


def solution(mesh):
    in_specs = (
        P("dp", None),
        P("dp", None),
        P(),
        P(),
        P(None, "tensor"),
        P(None, "tensor"),
        P(None, "tensor"),
        P(None, "tensor"),
        P("tensor"),
        P("tensor"),
        P("tensor"),
        P("tensor", None),
        P("dp", "tensor"),
        P("dp", "tensor"),
    )
    out_specs = (P("dp", "tensor"), P("dp", "tensor"), P("dp", "tensor"), P("dp", "tensor"))
    return jax.shard_map(local, mesh=mesh, in_specs=in_specs, out_specs=out_specs, check_vma=False)
```

```python
import math
from types import SimpleNamespace

import jax
import jax.numpy as jnp
from jax import lax
from jax.experimental import pallas as pl
from jax.experimental.pallas import tpu as pltpu
from jax.sharding import PartitionSpec as P

D = 4096
FF = 14336
EPS = 1e-05
T = 128
HEADS = 4
DP = 16
TP = 8
HID = 1792
ROWS = 256
WIDTH = 512
PACK = 896
F32 = jnp.float32
BF16 = jnp.bfloat16
MESH = pl.DeviceIdType.MESH
MIB = 1024 * 1024

RIGHT, LEFT, ACROSS, SIDE = range(4)
FULL, PART, REST, HALF_A, HALF_B, REST_A, REST_B, HALF_A1, HALF_A2, HALF_B1, HALF_B2 = range(11)
RO, LO, YO, RQ, LQ, RA, LB, YL, YR, RQA, LQB, YO2, RO1, RO2, RO3, LO1, LO2, LO3, YO1, RX1, RX2, LX1, LX2, RXA, LXB, OWN = range(26)

LEGS = {
    RO: (RIGHT, 0, 0, FULL, 0, -1),
    LO: (LEFT, 0, 0, FULL, 0, 1),
    YO: (ACROSS, 0, 0, FULL, 1, 0),
    RQ: (RIGHT, 1, 0, REST, 1, -1),
    LQ: (LEFT, 1, 0, REST, 1, 1),
    RA: (RIGHT, 0, -1, HALF_A, 0, 2),
    LB: (LEFT, 0, 1, HALF_B, 0, 2),
    YL: (ACROSS, 0, -1, PART, 1, -1),
    YR: (ACROSS, 0, 1, PART, 1, 1),
    RQA: (RIGHT, 1, -1, REST_A, 1, 2),
    LQB: (LEFT, 1, 1, REST_B, 1, 2),
    YO2: (ACROSS, 0, 2, PART, 1, 2),
}
HALVES = {
    RO1: (RIGHT, 0, 0, HALF_A, 0, -1),
    RO2: (RIGHT, 0, 0, HALF_B1, 0, -1),
    RO3: (RIGHT, 0, 0, HALF_B2, 0, -1),
    LO2: (LEFT, 0, 0, HALF_B, 0, 1),
    LO1: (LEFT, 0, 0, HALF_A1, 0, 1),
    LO3: (LEFT, 0, 0, HALF_A2, 0, 1),
    YO1: (ACROSS, 0, 0, HALF_A, 1, 0),
    YO2: (ACROSS, 0, 0, HALF_B, 1, 0),
    RX1: (RIGHT, 1, 0, HALF_A, 1, -1),
    RX2: (RIGHT, 1, 0, HALF_B, 1, -1),
    LX1: (LEFT, 1, 0, HALF_A, 1, 1),
    LX2: (LEFT, 1, 0, HALF_B, 1, 1),
    RA: (RIGHT, 0, -1, HALF_A, 0, 2),
    LB: (LEFT, 0, 1, HALF_B, 0, 2),
    RXA: (RIGHT, 1, -1, HALF_A, 1, 2),
    LXB: (LEFT, 1, 1, HALF_B, 1, 2),
}
NSEM = 2 * len(LEGS) + 1
NSEM_HALF = 2 * len(HALVES) + 1


def place():
    me = lax.axis_index("dp")
    return me, me // 8, (me % 8) // 2, me % 2


class Gather:
    def __init__(self, legs, piece, rows, p, qa, send, recv, give=None):
        self.legs, self.order = legs, list(legs)
        self.piece, self.send, self.recv, self.give = piece, send, recv, give
        self.me, self.y, self.z, self.c = place()
        half = rows // 2
        self.rows = {
            FULL: (0, rows),
            PART: (0, p),
            REST: (p, rows - p),
            HALF_A: (0, half),
            HALF_B: (half, rows - half),
            HALF_A1: (0, half // 2),
            HALF_A2: (half // 2, half - half // 2),
            HALF_B1: (half, half // 2),
            HALF_B2: (half + half // 2, half - half // 2),
            REST_A: (p, qa),
            REST_B: (p + qa, rows - p - qa),
        }

    def block(self, flip, dz, core):
        y = self.y + flip - 2 * flip * self.y
        return y * 8 + ((self.z + dz + 4) % 4) * 2 + core

    def target(self, name):
        if name == RIGHT:
            return self.block(0, 1, self.c)
        if name == LEFT:
            return self.block(0, -1, self.c)
        if name == ACROSS:
            return self.block(1, 0, self.c)
        return self.block(0, 0, 1 - self.c)

    def copy(self, src, ref, sem, to):
        return pltpu.make_async_remote_copy(
            src_ref=src,
            dst_ref=ref,
            send_sem=self.send.at[sem],
            recv_sem=self.recv.at[sem],
            device_id={"dp": to},
            device_id_type=MESH,
        )

    def leg(self, name):
        to, flip, dz, rows, _, _ = self.legs[name]
        ref = self.piece(self.block(flip, dz, self.c), *self.rows[rows])
        src = ref
        if to == ACROSS and self.give is not None:
            src = self.give(*self.rows[rows])
        return self.copy(src, ref, self.order.index(name), self.target(to))

    def landed(self, name):
        to, _, _, rows, flip, dz = self.legs[name]
        ref = self.piece(self.block(flip, dz, self.c), *self.rows[rows])
        return self.copy(ref, ref, self.order.index(name), self.target(to))

    def side(self, name, core):
        if name == OWN:
            flip, dz, rows, sem = 0, 0, FULL, len(self.order)
        else:
            _, _, _, rows, flip, dz = self.legs[name]
            sem = len(self.order) + 1 + self.order.index(name)
        ref = self.piece(self.block(flip, dz, core), *self.rows[rows])
        return self.copy(ref, ref, sem, self.target(SIDE))

    def begin(self, *names):
        for name in names:
            self.leg(name).start()
        self.side(OWN, self.c).start()

    def arrive(self, name, *then):
        self.landed(name).wait_recv()
        for other in then:
            self.leg(other).start()
        self.side(name, self.c).start()

    def side_arrive(self, *names):
        for name in names:
            self.side(name, 1 - self.c).wait_recv()

    def finish(self):
        for name in self.order:
            self.leg(name).wait_send()
        for name in [OWN] + self.order:
            self.side(name, self.c).wait_send()


def iota(axis):
    return lax.broadcasted_iota(jnp.int32, (T, T), axis)


def mm(a, b):
    return jnp.dot(a.astype(BF16), b.astype(BF16), preferred_element_type=F32)


def mm_t(a, b):
    return lax.dot_general(
        a.astype(BF16), b.astype(BF16), (((1,), (1,)), ((), ())), preferred_element_type=F32
    )


def softplus(v):
    return jnp.maximum(v, 0.0) + jnp.log1p(jnp.exp(-jnp.abs(v)))


def steps_of(raw, params):
    step = softplus(raw + params[0:1, :])
    lower = (iota(0) >= iota(1)).astype(F32)
    decay = jnp.dot(
        lower, -step * params[1:2, :], preferred_element_type=F32, precision=lax.Precision.HIGHEST
    )
    return step, decay, jnp.transpose(step), jnp.transpose(decay)


def head(k):
    return slice(k * 128, (k + 1) * 128)


class States:
    def __init__(self, own, sib, chips, result, out, send, recv):
        self.own, self.sib, self.chips, self.result, self.out = own, sib, chips, result, out
        self.send, self.recv = send, recv
        self.me, self.y, self.z, self.c = place()
        self.q = self.me // 2
        self.mine = pl.ds(pl.multiple_of(self.c * 256, 256), 256)
        self.rest = pl.ds(pl.multiple_of((1 - self.c) * 256, 256), 256)

    def copy(self, src, dst, sem, to):
        return pltpu.make_async_remote_copy(
            src_ref=src,
            dst_ref=dst,
            send_sem=self.send.at[sem],
            recv_sem=self.recv.at[sem],
            device_id={"dp": to},
            device_id_type=MESH,
        )

    def share(self):
        return self.copy(self.own.at[:, self.rest], self.sib, 0, self.q * 2 + 1 - self.c)

    def peer(self, k, landing=False):
        at = self.chips.at[(self.q + 8 - k) % 8 if landing else self.q]
        return self.copy(at, at, k, ((self.q + k) % 8) * 2 + self.c)

    def hand(self, landing=False):
        lanes = self.rest if landing else self.mine
        return self.copy(self.result, self.out.at[:, lanes], 8, self.q * 2 + 1 - self.c)

    def wide(self, row):
        pick = [jnp.where(self.c == 0, row[:, i : i + 1], row[:, 2 + i : 3 + i]) for i in range(2)]
        lane = lax.broadcasted_iota(jnp.int32, (1, 256), 1)
        return jnp.where(lane < 128, pick[0], pick[1])

    def pair(self):
        mine, theirs = self.own[:, self.mine].astype(F32), self.sib[...].astype(F32)
        return jnp.where(self.c == 0, mine, theirs), jnp.where(self.c == 0, theirs, mine)

    def join(self, ends, forward):
        self.share().wait_recv()
        first, second = self.pair()
        if forward:
            total = self.wide(jnp.exp(ends[1])) * first + second
        else:
            total = first + self.wide(jnp.exp(ends[0])) * second
        self.chips[self.q] = total.astype(BF16)
        for k in (4, 1, 7, 2, 6, 3, 5):
            self.peer(k).start()

    def solve(self, ends, weights, forward):
        for k in range(1, 8):
            self.peer(k, True).wait_recv()
        total = jnp.zeros((128, 256), F32)
        for j in range(8):
            total = total + self.wide(weights[j : j + 1, :]) * self.chips[j].astype(F32)
        first, second = self.pair()
        if forward:
            near, far = total, self.wide(jnp.exp(ends[0])) * total + first
        else:
            near, far = second + self.wide(jnp.exp(ends[1])) * total, total
        self.result[...] = jnp.where(self.c == 0, far, near).astype(BF16)
        self.hand().start()
        self.out[:, self.mine] = jnp.where(self.c == 0, near, far).astype(BF16)

    def finish(self):
        self.share().wait_send()
        for k in range(1, 8):
            self.peer(k).wait_send()
        self.hand().wait_send()


def state_weights(decays, q, put):
    ends = [decays[2 * j, 0:1, :] + decays[2 * j + 1, 0:1, :] for j in range(8)]
    for at, order in enumerate((range(7, -1, -1), range(8))):
        run = jnp.zeros((1, 128), F32)
        for j in order:
            reached = ((j < q) if at == 0 else (j > q)).astype(F32)
            put[at, j : j + 1, :] = reached * jnp.exp(run)
            run = run + reached * ends[j]


def spread(scalars):
    lane = lax.broadcasted_iota(jnp.int32, (1, 128), 1)
    row = jnp.zeros((1, 128), F32)
    for h in range(HEADS):
        row = jnp.where(lane == h, scalars[h], row)
    return row


SCRATCH = dict(
    held=pltpu.VMEM((DP, ROWS, HID), BF16),
    give=pltpu.VMEM((ROWS, HID), BF16),
    v_wc=pltpu.VMEM((D, 512), BF16),
    v_wb=pltpu.VMEM((D, 128), BF16),
    v_wx=pltpu.VMEM((D, 128), BF16),
    v_wdt=pltpu.VMEM((HEADS, D), BF16),
    v_out=pltpu.VMEM((TP, 512, WIDTH), BF16),
    v_resid=pltpu.VMEM((T, WIDTH), BF16),
    nin=pltpu.VMEM((T, D), BF16),
    lhs=pltpu.VMEM((4 * T, D), BF16),
    acc=pltpu.VMEM((4 * T, HID), F32),
    proj=pltpu.VMEM((T, PACK), F32),
    read=pltpu.VMEM((T, WIDTH), BF16),
    state=pltpu.VMEM((128, WIDTH), BF16),
    sib=pltpu.VMEM((128, 256), BF16),
    chips=pltpu.VMEM((8, 128, 256), BF16),
    result=pltpu.VMEM((128, 256), BF16),
    decays=pltpu.VMEM((DP, 8, 128), F32),
    weights=pltpu.VMEM((2, 8, 128), F32),
    steps=pltpu.VMEM((4, T, 128), F32),
    read_t=pltpu.VMEM((HEADS, 128, T), BF16),
    enter=pltpu.VMEM((128, WIDTH), BF16),
    through=pltpu.VMEM((T, WIDTH), F32),
    mixer_out=pltpu.VMEM((T, WIDTH), BF16),
    fade=pltpu.VMEM((HEADS, T, T), F32),
    plain=pltpu.VMEM((HEADS, T, T), F32),
    p_send=pltpu.VMEM((TP, T, WIDTH), BF16),
    p_recv=pltpu.VMEM((TP, T, WIDTH), BF16),
    str_a=pltpu.VMEM((4, 4, T // 2, WIDTH), BF16),
    str_b=pltpu.VMEM((4, 4, T // 2, WIDTH), BF16),
    mid_a=pltpu.VMEM((4, 4, T // 2, WIDTH), BF16),
    mid_b=pltpu.VMEM((4, 4, T // 2, WIDTH), BF16),
    got_a=pltpu.VMEM((3, 4, T // 2, WIDTH), BF16),
    got_b=pltpu.VMEM((3, 4, T // 2, WIDTH), BF16),
    sum_a=pltpu.VMEM((4, T // 2, WIDTH), BF16),
    sum_b=pltpu.VMEM((4, T // 2, WIDTH), BF16),
    end_a=pltpu.VMEM((3, T // 2, WIDTH), BF16),
    end_b=pltpu.VMEM((3, T // 2, WIDTH), BF16),
    gained=pltpu.VMEM((TP, T, WIDTH), BF16),
    grads=pltpu.VMEM((2 * T, HID), BF16),
    squares=pltpu.VMEM((2, T, 128), F32),
    out_grad=pltpu.VMEM((T, WIDTH), F32),
    along=pltpu.VMEM((T, WIDTH), F32),
    b_state=pltpu.VMEM((128, WIDTH), BF16),
    b_sib=pltpu.VMEM((128, 256), BF16),
    b_chips=pltpu.VMEM((8, 128, 256), BF16),
    b_result=pltpu.VMEM((128, 256), BF16),
    behind=pltpu.VMEM((128, WIDTH), BF16),
    packed=pltpu.VMEM((DP, T, PACK - WIDTH), BF16),
    read4=pltpu.VMEM((HEADS * T, 128), BF16),
    weight4=pltpu.VMEM((HEADS * T, T), BF16),
    grad4=pltpu.VMEM((HEADS * T, 128), BF16),
    dscore4=pltpu.VMEM((HEADS * T, T), BF16),
    across=pltpu.VMEM((HEADS, T, 128), F32),
    dinject=pltpu.VMEM((T, 128), F32),
    dvalue=pltpu.VMEM((T, 128), F32),
    in_sem=pltpu.SemaphoreType.DMA((11 + TP,)),
    g_send=pltpu.SemaphoreType.DMA((NSEM_HALF,)),
    g_recv=pltpu.SemaphoreType.DMA((NSEM_HALF,)),
    a_send=pltpu.SemaphoreType.DMA((1,)),
    a_recv=pltpu.SemaphoreType.DMA((1,)),
    h_send=pltpu.SemaphoreType.DMA((NSEM,)),
    h_recv=pltpu.SemaphoreType.DMA((NSEM,)),
    i_send=pltpu.SemaphoreType.DMA((NSEM,)),
    i_recv=pltpu.SemaphoreType.DMA((NSEM,)),
    s_send=pltpu.SemaphoreType.DMA((9,)),
    s_recv=pltpu.SemaphoreType.DMA((9,)),
    d_send=pltpu.SemaphoreType.DMA((DP - 1,)),
    d_recv=pltpu.SemaphoreType.DMA((DP - 1,)),
    b_send=pltpu.SemaphoreType.DMA((9,)),
    b_recv=pltpu.SemaphoreType.DMA((9,)),
    c_send=pltpu.SemaphoreType.DMA((DP - 1,)),
    c_recv=pltpu.SemaphoreType.DMA((DP - 1,)),
    t_send=pltpu.SemaphoreType.DMA((2, TP)),
    t_recv=pltpu.SemaphoreType.DMA((2, TP)),
    p1_send=pltpu.SemaphoreType.DMA((12,)),
    p1_recv=pltpu.SemaphoreType.DMA((12,)),
    p2_send=pltpu.SemaphoreType.DMA((12,)),
    p2_recv=pltpu.SemaphoreType.DMA((12,)),
)


def chunk(k, size=256):
    return pl.ds(pl.multiple_of(k * size, size), size)


def columns(p):
    return chunk(p, WIDTH)


def normalise(ref, rows, gain):
    total = jnp.zeros((T, 1), F32)
    for k in range(8):
        part = ref[rows, k * 512 : (k + 1) * 512].astype(F32)
        total = total + jnp.sum(part * part, axis=1, keepdims=True)
    scale = lax.rsqrt(total / D + EPS)
    for k in range(8):
        at = slice(k * 512, (k + 1) * 512)
        ref[rows, at] = (ref[rows, at].astype(F32) * scale * gain[:, at]).astype(BF16)


def whole_kernel(
    resid, teacher, gain_mix, gain_mlp, w_c, w_b, w_x, w_dt, bias, rate, skip, w_out, w_gate, w_up, out, *scratch
):
    s = SimpleNamespace(**dict(zip(SCRATCH, scratch)))
    me, y, z, c = place()
    m = me % 8
    t = lax.axis_index("tensor")
    other = (1 - y) * 8 + m
    half = HID // 2
    keep = pl.ds(pl.multiple_of(y * half, 128), half)
    rest = pl.ds(pl.multiple_of((1 - y) * half, 128), half)
    mine = pl.ds(pl.multiple_of(y * T, T), T)
    pairs = (
        (w_gate.at[:, keep], s.held.at[me, :, 0:half]),
        (w_up.at[:, keep], s.held.at[me, :, half:HID]),
        (w_gate.at[:, rest], s.give.at[:, 0:half]),
        (w_up.at[:, rest], s.give.at[:, half:HID]),
        (resid, s.nin),
        (w_c, s.v_wc),
        (w_b, s.v_wb),
        (w_x, s.v_wx),
        (w_dt, s.v_wdt),
        (teacher, s.lhs.at[mine, :]),
        (resid.at[:, columns(t)], s.v_resid),
    ) + tuple((w_out.at[:, p * WIDTH : (p + 1) * WIDTH], s.v_out.at[p]) for p in range(TP))
    loads = [pltpu.make_async_copy(a, b, s.in_sem.at[k]) for k, (a, b) in enumerate(pairs)]
    for copy in loads:
        copy.start()
    sem = pltpu.get_barrier_semaphore()
    for k in range(1, DP):
        pl.semaphore_signal(sem, inc=1, device_id={"dp": (me + k) % DP}, device_id_type=MESH)
    for k in range(1, TP):
        for dp in (me, other):
            pl.semaphore_signal(
                sem, inc=1, device_id={"dp": dp, "tensor": (t + k) % TP}, device_id_type=MESH
            )
    loads[4].wait()
    normalise(s.nin, slice(None), gain_mix)
    pl.semaphore_wait(sem, DP - 1 + 2 * (TP - 1))
    for copy in loads[0:4]:
        copy.wait()
    gather = Gather(
        HALVES,
        lambda j, start, size: s.held.at[j, pl.ds(start, size), :],
        ROWS,
        112,
        64,
        s.g_send,
        s.g_recv,
        lambda start, size: s.give.at[pl.ds(start, size), :],
    )
    gather.begin(RO1, LO2, YO1)
    theirs = pl.ds(pl.multiple_of((1 - y) * T, T), T)

    def teacher_move(rows):
        return pltpu.make_async_remote_copy(
            src_ref=teacher,
            dst_ref=s.lhs.at[rows, :],
            send_sem=s.a_send.at[0],
            recv_sem=s.a_recv.at[0],
            device_id={"dp": other, "tensor": (t + 4) % TP},
            device_id_type=MESH,
        )

    teacher_move(mine).start()

    bias_row, rate_row, skip_row = spread(bias), spread(rate), spread(skip)
    params = jnp.concatenate([bias_row, rate_row, skip_row, jnp.zeros((5, 128), F32)], axis=0)
    for copy in loads[5:9]:
        copy.wait()
    rows = s.nin[...]
    s.proj[:, 0:512] = jnp.dot(rows, s.v_wc[...], preferred_element_type=F32)
    s.proj[:, 512:640] = jnp.dot(rows, s.v_wb[...], preferred_element_type=F32)
    s.proj[:, 640:768] = jnp.dot(rows, s.v_wx[...], preferred_element_type=F32)
    s.proj[:, 768:896] = jnp.zeros((T, 128), F32)
    s.proj[:, 768 : 768 + HEADS] = mm_t(rows, s.v_wdt[...])
    s.read[...] = s.proj[:, 0:512].astype(BF16)
    inject, values = s.proj[:, 512:640], s.proj[:, 640:768]
    raw = s.proj[:, 768:896]
    gather.leg(RO2).start()
    gather.leg(LO1).start()
    step, decay, step_t, decay_t = steps_of(raw, params)
    s.decays[me] = jnp.broadcast_to(decay[T - 1 : T, :], (8, 128))

    def ends_move(k):
        ref = s.decays.at[me]
        return pltpu.make_async_remote_copy(
            src_ref=ref,
            dst_ref=ref,
            send_sem=s.d_send.at[k - 1],
            recv_sem=s.d_recv.at[k - 1],
            device_id={"dp": (me + k) % DP},
            device_id_type=MESH,
        )

    def ends_landed(k):
        ref = s.decays.at[(me - k + DP) % DP]
        return pltpu.make_async_remote_copy(
            src_ref=ref,
            dst_ref=ref,
            send_sem=s.d_send.at[k - 1],
            recv_sem=s.d_recv.at[k - 1],
            device_id={"dp": (me + k) % DP},
            device_id_type=MESH,
        )

    for k in range(1, DP):
        ends_move(k).start()
    causal = iota(0) >= iota(1)
    inject_t = jnp.transpose(inject)
    for h in range(HEADS):
        s.read4[head(h), :] = s.read[:, head(h)]
    score = mm_t(s.read4[...], inject)
    pulls = []
    for h in range(HEADS):
        row, col, step_row = decay_t[h : h + 1, :], decay[:, h : h + 1], step_t[h : h + 1, :]
        s.fade[h] = jnp.exp(jnp.where(causal, col - row, -1e30))
        s.plain[h] = s.fade[h] * score[head(h), :]
        s.weight4[head(h), :] = (s.plain[h] * step_row).astype(BF16)
        pulls.append(inject_t * (jnp.exp(row[:, T - 1 : T] - row) * step_row))
    carried = mm(jnp.concatenate(pulls, axis=0), values)
    for h in range(HEADS):
        s.state[:, head(h)] = carried[head(h), :].astype(BF16)
    q = me // 2
    states = States(s.state, s.sib, s.chips, s.result, s.enter, s.s_send, s.s_recv)
    states.share().start()
    through = mm(s.weight4[...], values)
    for h in range(HEADS):
        s.through[:, head(h)] = through[head(h), :] + skip_row[:, h : h + 1] * values
    for k, value in enumerate((step, decay, step_t, decay_t)):
        s.steps[k] = value
    ends_landed(jnp.where(c == 0, DP - 1, 1)).wait_recv()
    chip_ends = [s.decays[2 * q + i, 0:1, :] for i in range(2)]
    states.join(chip_ends, True)
    gather.leg(YO2).start()
    gather.leg(RO3).start()
    gather.leg(LO3).start()

    loads[9].wait()
    normalise(s.lhs, mine, gain_mlp)
    gather.arrive(RO1, RA)
    gather.arrive(LO2, LB)
    gather.arrive(YO1, RX1, LX1)

    for k in range(2, DP - 1):
        ends_landed(k).wait_recv()
    ends_landed(jnp.where(c == 0, 1, DP - 1)).wait_recv()
    state_weights(s.decays, q, s.weights)
    states.solve(chip_ends, s.weights[0], True)
    states.hand(True).wait_recv()
    for h in range(HEADS):
        grown = jnp.exp(decay[:, h : h + 1]) * mm(s.read[:, head(h)], s.enter[:, head(h)])
        s.mixer_out[:, head(h)] = (s.through[:, head(h)] + grown).astype(BF16)

    def move(phase, kt, src, dst):
        return pltpu.make_async_remote_copy(
            src_ref=src,
            dst_ref=dst,
            send_sem=s.t_send.at[phase, kt],
            recv_sem=s.t_recv.at[phase, kt],
            device_id={"tensor": (t + kt) % TP},
            device_id_type=MESH,
        )

    def out_move(kt):
        return move(0, kt, s.p_send.at[kt], s.p_recv.at[kt])

    def gained_move(kt):
        return move(1, kt, s.gained.at[t], s.gained.at[t])

    def gained_landed(kt):
        at = s.gained.at[(t - kt + TP) % TP]
        return move(1, kt, at, at)

    px, py = t % 4, (t // 4) * 2 + y

    def plane(sems, leg, over_x, k, src, dst):
        xx = (px + k) % 4 if over_x else px
        yy = py if over_x else (py + k) % 4
        return pltpu.make_async_remote_copy(
            src_ref=src,
            dst_ref=dst,
            send_sem=sems[0].at[3 * leg + k - 1],
            recv_sem=sems[1].at[3 * leg + k - 1],
            device_id={"dp": (yy % 2) * 8 + m, "tensor": (yy // 2) * 4 + xx},
            device_id_type=MESH,
        )

    def stream_leg(leg, k, landing=False):
        d = (4 - k) if landing else 0
        ref = (
            s.str_a.at[py, (px + d) % 4],
            s.str_b.at[px, (py + d) % 4],
            s.str_a.at[(py + d) % 4],
            s.str_b.at[(px + d) % 4],
        )[leg]
        return plane((s.p1_send, s.p1_recv), leg, leg in (0, 3), k, ref, ref)

    def mid_leg(leg, k):
        src, dst = (
            (s.mid_a.at[(px + k) % 4], s.got_a.at[k - 1]),
            (s.mid_b.at[(py + k) % 4], s.got_b.at[k - 1]),
            (s.sum_a.at[(py + k) % 4], s.end_a.at[k - 1]),
            (s.sum_b.at[(px + k) % 4], s.end_b.at[k - 1]),
        )[leg]
        return plane((s.p2_send, s.p2_recv), leg, leg in (0, 3), k, src, dst)

    def stream_block(yy, p):
        row, col = 2 * (p // 4) + yy, p % 4
        return jnp.concatenate([s.str_a[row, col], s.str_b[col, row]], axis=0)

    def out_part(p):
        return jnp.dot(s.mixer_out[...], s.v_out[p], preferred_element_type=F32)

    for copy in loads[10:]:
        copy.wait()

    def out_send(k, _):
        s.p_send[k] = out_part((t + k) % TP).astype(BF16)
        out_move(k).start()
        return 0

    lax.fori_loop(1, TP, out_send, 0)
    stream = out_part(t) + s.v_resid[...].astype(F32)
    gather.arrive(YO2, LX2, RX2)
    gather.arrive(RO2)
    gather.arrive(LO1)
    gather.arrive(RO3)
    gather.arrive(LO3)
    for k in range(1, TP):
        out_move(k).wait_recv()
        stream = stream + s.p_recv[k].astype(F32)
    half_rows = T // 2
    s.str_a[py, px] = stream[0:half_rows].astype(BF16)
    s.str_b[px, py] = stream[half_rows:T].astype(BF16)
    for k in (2, 1, 3):
        stream_leg(0, k).start()
        stream_leg(1, k).start()

    def column_copy(k):
        to = (k // 8 + y) % 2 * 8 + (m + k) % 8
        return pltpu.make_async_remote_copy(
            src_ref=s.v_wx.at[chunk(to), :],
            dst_ref=s.v_wb.at[chunk(me), :],
            send_sem=s.c_send.at[k - 1],
            recv_sem=s.c_recv.at[k - 1],
            device_id={"dp": to},
            device_id_type=MESH,
        )

    def column_landed(k):
        at = (k // 8 + y) % 2 * 8 + (m - k + DP) % 8
        return pltpu.make_async_remote_copy(
            src_ref=s.v_wx.at[chunk(at), :],
            dst_ref=s.v_wb.at[chunk(at), :],
            send_sem=s.c_send.at[k - 1],
            recv_sem=s.c_recv.at[k - 1],
            device_id={"dp": at},
            device_id_type=MESH,
        )

    near, far = range(1, 8), range(8, DP)

    upper_rows, lower_rows = pl.ds(0, 2 * T), pl.ds(2 * T, 2 * T)

    def use(flip, dz, rows=upper_rows):
        base = gather.block(flip, dz, 0)
        s.acc[rows, :] += jnp.dot(
            s.lhs[rows, chunk(base)], s.held[base], preferred_element_type=F32
        ) + jnp.dot(s.lhs[rows, chunk(base + 1)], s.held[base + 1], preferred_element_type=F32)

    def turn(k, _):
        s.v_wx[chunk(k), :] = jnp.transpose(s.nin[:, chunk(k)].astype(F32)).astype(BF16)
        return 0

    lax.fori_loop(0, DP, turn, 0)
    growth_t = jnp.exp(s.steps[3])
    for h in range(HEADS):
        s.read_t[h] = (jnp.transpose(s.read[:, head(h)].astype(F32)) * growth_t[h : h + 1, :]).astype(BF16)
    s.acc[...] = jnp.zeros_like(s.acc)
    teacher_move(theirs).wait_recv()
    normalise(s.lhs, theirs, gain_mlp)
    for k in (2, 1, 3):
        stream_leg(0, k, True).wait_recv()
    for k in (2, 1, 3):
        stream_leg(2, k).start()
    for k in (2, 1, 3):
        stream_leg(1, k, True).wait_recv()
    for k in (2, 1, 3):
        stream_leg(3, k).start()
    gather.arrive(RX1, RXA)
    gather.arrive(RA)
    gather.arrive(LB)
    gather.arrive(LX1)
    gather.side_arrive(OWN, YO1, YO2, RO1, RO2, RO3, LO1, LO2, LO3)

    def teach(i, _):
        use(jnp.where(i == 1, 1, 0), jnp.where(i < 2, 0, jnp.where(i == 2, 3, 1)))
        return 0

    lax.fori_loop(0, 4, teach, 0)
    gather.side_arrive(RA, LB)
    use(0, 2)
    gather.arrive(LX2, LXB)
    gather.arrive(RX2)
    gather.side_arrive(RX1, RX2)
    use(1, -1)
    gather.side_arrive(LX1, LX2)
    use(1, 1)

    for leg in (2, 3):
        for k in (2, 1, 3):
            stream_leg(leg, k, True).wait_recv()
    s.squares[...] = jnp.zeros_like(s.squares)

    def student_rows(p, _):
        for yy in range(2):
            part = stream_block(yy, p).astype(F32)
            s.squares[yy] += jnp.broadcast_to(jnp.sum(part * part, axis=1, keepdims=True), (T, 128))
            s.lhs[pl.ds((2 + yy) * T, T), columns(p)] = (part * gain_mlp[:, columns(p)]).astype(BF16)
        return 0

    lax.fori_loop(0, TP, student_rows, 0)

    def student(i, _):
        use(i % 2, jnp.where(i < 2, 0, jnp.where(i < 4, 3, jnp.where(i < 6, 1, 2))), lower_rows)
        return 0

    lax.fori_loop(0, 7, student, 0)
    for k in far:
        column_copy(k).start()
    gather.arrive(RXA)
    gather.arrive(LXB)

    gather.side_arrive(RXA, LXB)
    use(1, 2, slice(None))
    scales = [lax.rsqrt(s.squares[yy, :, 0:1] / D + EPS) for yy in range(2)]
    scale = jnp.where(y == 0, scales[0], scales[1])
    both = jnp.concatenate(scales, axis=0)

    for n in range(half // 128):
        at, beside = slice(n * 128, (n + 1) * 128), slice(half + n * 128, half + (n + 1) * 128)
        aim_gate = s.acc[upper_rows, at]
        aim = aim_gate * jax.nn.sigmoid(aim_gate) * s.acc[upper_rows, beside]
        gate, up = s.acc[lower_rows, at] * both, s.acc[lower_rows, beside] * both
        sigma = jax.nn.sigmoid(gate)
        silu = gate * sigma
        grad = (2.0 / math.sqrt(FF)) * (silu * up - aim)
        s.grads[:, at] = (grad * up * sigma * (1.0 + gate * (1.0 - sigma))).astype(BF16)
        s.grads[:, beside] = (grad * silu).astype(BF16)

    def back(yh, xx):
        for i in range(2):
            part = mm_t(s.grads[...], s.held[2 * (yh * 4 + xx) + i]).astype(BF16)
            lanes_at = slice(i * 256, (i + 1) * 256)
            for yy in range(2):
                s.mid_a[xx, 2 * yh + yy, :, lanes_at] = part[yy * T : yy * T + half_rows, :]
                s.mid_b[2 * yh + yy, xx, :, lanes_at] = part[yy * T + half_rows : (yy + 1) * T, :]

    def back_far(xx, _):
        back(1 - t // 4, xx)
        return 0

    lax.fori_loop(0, 4, back_far, 0)
    mid_leg(1, 2).start()

    @pl.when(y == 0)
    def _():
        mid_leg(1, 3).start()

    @pl.when(y == 1)
    def _():
        mid_leg(1, 1).start()

    back(t // 4, (px + 2) % 4)
    mid_leg(0, 2).start()
    back(t // 4, (px + 1) % 4)
    mid_leg(0, 1).start()
    back(t // 4, (px + 3) % 4)
    mid_leg(0, 3).start()
    back(t // 4, px)

    @pl.when(y == 0)
    def _():
        mid_leg(1, 1).start()

    @pl.when(y == 1)
    def _():
        mid_leg(1, 3).start()

    for k in near:
        column_copy(k).start()
    s.v_wb[chunk(me), :] = s.v_wx[chunk(me), :]
    s.along[...] = jnp.zeros_like(s.along)

    def stream_part(p, _):
        s.along[...] += mm_t(stream_block(y, p), s.v_out[p])
        return 0

    lax.fori_loop(0, TP, stream_part, 0)

    def fold(own, got, sums):
        for at in range(4):
            total = own[at].astype(F32)
            for k in range(3):
                total = total + got[k, at].astype(F32)
            sums[at] = total.astype(BF16)

    for k in (2, 1, 3):
        mid_leg(0, k).wait_recv()
    fold(s.mid_a.at[px], s.got_a, s.sum_a)
    for k in (2, 1, 3):
        mid_leg(2, k).start()
    for k in (2, 1, 3):
        mid_leg(1, k).wait_recv()
    fold(s.mid_b.at[py], s.got_b, s.sum_b)
    for k in (2, 1, 3):
        mid_leg(3, k).start()
    parts = []
    for leg, own, ends_of in ((2, s.sum_a.at[py], s.end_a), (3, s.sum_b.at[px], s.end_b)):
        total = own[...].astype(F32)
        for k in (2, 1, 3):
            mid_leg(leg, k).wait_recv()
            total = total + ends_of[k - 1].astype(F32)
        parts.append(total)
    mid = jnp.concatenate(parts, axis=0)
    s.gained[t] = (mid * gain_mlp[:, columns(t)]).astype(BF16)
    for k in range(1, TP):
        gained_move(k).start()
    s.out_grad[...] = jnp.zeros_like(s.out_grad)

    def unproject(kt, inner):
        @pl.when(kt > 0)
        def _():
            gained_landed(kt).wait_recv()

        p = (t - kt + TP) % TP
        part = s.gained[p]
        s.out_grad[...] += mm_t(part, s.v_out[p])
        return inner + jnp.sum(part.astype(F32) * stream_block(y, p).astype(F32), axis=1, keepdims=True)

    inner = lax.fori_loop(0, TP, unproject, jnp.zeros((T, 1), F32))
    pull = scale * scale * scale * (inner / D)
    s.out_grad[...] = s.out_grad[...] * scale - s.along[...] * pull

    inject, values = s.proj[:, 512:640], s.proj[:, 640:768]
    raw = s.proj[:, 768:896]
    step, decay, step_t, decay_t = [s.steps[k] for k in range(4)]
    growth = jnp.exp(decay)
    for h in range(HEADS):
        s.b_state[:, head(h)] = mm(s.read_t[h], s.out_grad[:, head(h)]).astype(BF16)
    states_back = States(s.b_state, s.b_sib, s.b_chips, s.b_result, s.behind, s.b_send, s.b_recv)
    states_back.share().start()
    early = Gather(
        LEGS, lambda j, start, size: s.v_wc.at[pl.ds(pl.multiple_of(j * T + start, 16), size), :], T, 48, 48, s.h_send, s.h_recv
    )
    last = Gather(
        LEGS, lambda j, start, size: s.packed.at[j, pl.ds(start, size), :], T, 48, 48, s.i_send, s.i_recv
    )
    lanes = lax.broadcasted_iota(jnp.int32, (1, 128), 1)
    for h in range(HEADS):
        s.grad4[head(h), :] = s.out_grad[:, head(h)].astype(BF16)
    dweight = mm_t(s.grad4[...], values)
    for h in range(HEADS):
        s.dscore4[head(h), :] = (dweight[head(h), :] * s.fade[h] * step_t[h : h + 1, :]).astype(BF16)
        s.across[h] = growth[:, h : h + 1] * mm_t(s.grad4[head(h), :], s.enter[:, head(h)])
    inner_read = mm(s.dscore4[...], inject)
    chip_ends = [s.decays[2 * q + i, 0:1, :] for i in range(2)]
    states_back.join(chip_ends, False)
    for h in range(HEADS):
        s.v_wc[chunk(me, T), head(h)] = (inner_read[head(h), :] + s.across[h]).astype(BF16)
    early.begin(RO, LO, YO)
    step_rows, decay_rows, decay_cols = [], [], []
    skipped = jnp.zeros((T, 128), F32)
    for h in range(HEADS):
        step_row = step_t[h : h + 1, :]
        direct = dweight[head(h), :] * s.plain[h]
        skipped = skipped + skip_row[:, h : h + 1] * s.out_grad[:, head(h)]
        column = jnp.sum(direct, axis=0, keepdims=True)
        step_rows.append(column)
        decay_rows.append(-column * step_row)
        both_ways = direct * step_row + s.across[h] * s.read[:, head(h)].astype(F32)
        decay_cols.append(jnp.sum(both_ways, axis=1, keepdims=True))
    rows_dot = (((0,), (0,)), ((), ()))
    s.dinject[...] = lax.dot_general(s.dscore4[...], s.read4[...], rows_dot, preferred_element_type=F32)
    s.dvalue[...] = skipped + lax.dot_general(
        s.weight4[...], s.grad4[...], rows_dot, preferred_element_type=F32
    )
    states_back.solve(chip_ends, s.weights[1], False)
    early.arrive(YO, RQ, LQ)
    early.arrive(RO, RA, YL)
    early.arrive(LO, LB, YR)
    states_back.hand(True).wait_recv()
    dstep = jnp.zeros((T, 128), F32)
    ddecay = jnp.zeros((T, 128), F32)
    drawn_values = mm(inject, s.behind[...])
    dinject, dvalue = s.dinject[...], s.dvalue[...]
    final = (lax.broadcasted_iota(jnp.int32, (T, 1), 0) == T - 1).astype(F32)
    tails = jnp.exp(decay[T - 1 : T, :] - decay)
    for h in range(HEADS):
        tail_col = tails[:, h : h + 1]
        scaled_col = tail_col * step[:, h : h + 1]
        pulled = mm_t(values, s.behind[:, head(h)])
        dinject = dinject + scaled_col * pulled
        dvalue = dvalue + scaled_col * drawn_values[:, head(h)]
        drawn = tail_col * jnp.sum(inject * pulled, axis=1, keepdims=True)
        moved = drawn * step[:, h : h + 1]
        product = s.behind[:, head(h)].astype(F32) * s.enter[:, head(h)].astype(F32)
        kept = jnp.exp(decay[T - 1 : T, h : h + 1]) * jnp.sum(
            jnp.sum(product, axis=0, keepdims=True), axis=1, keepdims=True
        )
        end = kept + jnp.sum(moved, axis=0, keepdims=True)
        onehot = (lanes == h).astype(F32)
        dstep = dstep + drawn * onehot
        ddecay = ddecay + (decay_cols[h] - moved + final * end) * onehot
    s.packed[me, :, 0:128] = dinject.astype(BF16)
    s.packed[me, :, 128:256] = dvalue.astype(BF16)
    zero = jnp.zeros((128 - HEADS, 128), F32)
    dstep = dstep + jnp.transpose(jnp.concatenate(step_rows + [zero], axis=0))
    ddecay = ddecay + jnp.transpose(jnp.concatenate(decay_rows + [zero], axis=0))
    upper = (iota(0) <= iota(1)).astype(F32)
    later = jnp.dot(upper, ddecay, preferred_element_type=F32, precision=lax.Precision.HIGHEST)
    draw = (dstep - rate_row * later) * jax.nn.sigmoid(raw + bias_row)
    s.packed[me, :, 256:384] = draw.astype(BF16)

    last.begin(RO, LO, YO)
    out[...] = jnp.zeros_like(out)
    for k in range(1, DP):
        column_landed(k).wait_recv()

    def add(lanes_at, base, first, second):
        out[:, lanes_at] += jnp.dot(s.v_wb[chunk(base), :], first, preferred_element_type=F32) + jnp.dot(
            s.v_wb[chunk(base + 1), :], second, preferred_element_type=F32
        )

    def add_c(flip, dz):
        base = early.block(flip, dz, 0)
        add(slice(0, WIDTH), base, s.v_wc[chunk(base, T), :], s.v_wc[chunk(base + 1, T), :])

    def add_rest(flip, dz):
        base = last.block(flip, dz, 0)
        add(slice(WIDTH, PACK), base, s.packed[base], s.packed[base + 1])

    early.arrive(RQ, RQA)
    early.arrive(LQ, LQB)
    early.arrive(RA, YO2)
    early.arrive(LB)
    early.arrive(YL)
    early.arrive(YR)
    early.side_arrive(OWN)
    add_c(0, 0)
    early.side_arrive(YO)
    add_c(1, 0)
    last.arrive(YO, RQ, LQ)
    last.arrive(RO, RA, YL)
    last.arrive(LO, LB, YR)
    early.arrive(RQA)
    early.arrive(LQB)
    early.arrive(YO2)
    early.side_arrive(RO)
    add_c(0, -1)
    early.side_arrive(LO)
    add_c(0, 1)
    last.arrive(RQ, RQA)
    last.arrive(LQ, LQB)
    last.arrive(RA, YO2)
    last.arrive(LB)
    last.arrive(YL)
    last.arrive(YR)
    early.side_arrive(RA, LB)
    add_c(0, 2)
    early.side_arrive(RQ, YL)
    add_c(1, -1)
    early.side_arrive(LQ, YR)
    add_c(1, 1)
    early.side_arrive(RQA, LQB, YO2)
    add_c(1, 2)
    last.arrive(RQA)
    last.arrive(LQB)
    last.arrive(YO2)
    last.side_arrive(OWN)
    add_rest(0, 0)
    last.side_arrive(YO)
    add_rest(1, 0)
    last.side_arrive(RO)
    add_rest(0, -1)
    last.side_arrive(LO)
    add_rest(0, 1)
    last.side_arrive(RA, LB)
    add_rest(0, 2)
    last.side_arrive(RQ, YL)
    add_rest(1, -1)
    last.side_arrive(LQ, YR)
    add_rest(1, 1)
    last.side_arrive(RQA, LQB, YO2)
    add_rest(1, 2)

    gather.finish()
    early.finish()
    last.finish()
    states.finish()
    states_back.finish()
    for k in range(1, DP):
        ends_move(k).wait_send()
        column_copy(k).wait_send()
    teacher_move(mine).wait_send()
    for leg in range(4):
        for k in (1, 2, 3):
            stream_leg(leg, k).wait_send()
            mid_leg(leg, k).wait_send()
    for k in range(1, TP):
        out_move(k).wait_send()
        gained_move(k).wait_send()


def split_kernel(packed, grad_c, grad_b, grad_x, grad_dt):
    grad_c[...] = packed[:, 0:512]
    grad_b[...] = packed[:, 512:640]
    grad_x[...] = packed[:, 640:768]
    grad_dt[...] = jnp.transpose(packed[:, 768:896])[0:HEADS, :]


VM = pl.BlockSpec(memory_space=pltpu.VMEM)
SM = pl.BlockSpec(memory_space=pltpu.SMEM)
ANY = pl.BlockSpec(memory_space=pl.ANY)


def struct(shape, dtype):
    return jax.ShapeDtypeStruct(shape, dtype)


def local(
    resid, teacher_mixed, gain_mix, gain_mlp, w_c, w_b, w_x, w_dt, dt_bias, decay_rate, skip, w_out,
    w_gate, w_up,
):
    gain_mix, gain_mlp = gain_mix.reshape(1, D), gain_mlp.reshape(1, D)
    packed = pl.pallas_call(
        whole_kernel,
        out_shape=struct((ROWS, PACK), F32),
        in_specs=[ANY, ANY, VM, VM, ANY, ANY, ANY, ANY, SM, SM, SM, ANY, ANY, ANY],
        out_specs=VM,
        scratch_shapes=list(SCRATCH.values()),
        compiler_params=pltpu.CompilerParams(
            collective_id=0, has_side_effects=True, vmem_limit_bytes=63 * MIB
        ),
        name="whole",
    )(
        resid, teacher_mixed, gain_mix, gain_mlp, w_c, w_b, w_x, w_dt.T, dt_bias, decay_rate, skip, w_out,
        w_gate, w_up,
    )
    grad_c, grad_b, grad_x, grad_dt = pl.pallas_call(
        split_kernel,
        out_shape=(
            struct((ROWS, 512), F32),
            struct((ROWS, 128), F32),
            struct((ROWS, 128), F32),
            struct((HEADS, ROWS), F32),
        ),
        in_specs=[VM],
        out_specs=(VM,) * 4,
        name="split",
    )(packed)
    return grad_c, grad_b, grad_x, grad_dt.T


def solution(mesh):
    in_specs = (
        P("dp", None),
        P("dp", None),
        P(),
        P(),
        P(None, "tensor"),
        P(None, "tensor"),
        P(None, "tensor"),
        P(None, "tensor"),
        P("tensor"),
        P("tensor"),
        P("tensor"),
        P("tensor", None),
        P("dp", "tensor"),
        P("dp", "tensor"),
    )
    out_specs = (P("dp", "tensor"), P("dp", "tensor"), P("dp", "tensor"), P("dp", "tensor"))
    return jax.shard_map(local, mesh=mesh, in_specs=in_specs, out_specs=out_specs, check_vma=False)
```

```python
import math
from types import SimpleNamespace

import jax
import jax.numpy as jnp
from jax import lax
from jax.experimental import pallas as pl
from jax.experimental.pallas import tpu as pltpu
from jax.sharding import PartitionSpec as P

D = 4096
FF = 14336
EPS = 1e-05
T = 128
HEADS = 4
DP = 16
TP = 8
HID = 1792
ROWS = 256
WIDTH = 512
PACK = 896
F32 = jnp.float32
BF16 = jnp.bfloat16
MESH = pl.DeviceIdType.MESH
MIB = 1024 * 1024

RIGHT, LEFT, ACROSS, SIDE = range(4)
FULL, PART, REST, HALF_A, HALF_B, REST_A, REST_B, HALF_A1, HALF_A2, HALF_B1, HALF_B2 = range(11)
RO, LO, YO, RQ, LQ, RA, LB, YL, YR, RQA, LQB, YO2, RO1, RO2, RO3, LO1, LO2, LO3, YO1, RX1, RX2, LX1, LX2, RXA, LXB, OWN = range(26)

LEGS = {
    RO: (RIGHT, 0, 0, FULL, 0, -1),
    LO: (LEFT, 0, 0, FULL, 0, 1),
    YO: (ACROSS, 0, 0, FULL, 1, 0),
    RQ: (RIGHT, 1, 0, REST, 1, -1),
    LQ: (LEFT, 1, 0, REST, 1, 1),
    RA: (RIGHT, 0, -1, HALF_A, 0, 2),
    LB: (LEFT, 0, 1, HALF_B, 0, 2),
    YL: (ACROSS, 0, -1, PART, 1, -1),
    YR: (ACROSS, 0, 1, PART, 1, 1),
    RQA: (RIGHT, 1, -1, REST_A, 1, 2),
    LQB: (LEFT, 1, 1, REST_B, 1, 2),
    YO2: (ACROSS, 0, 2, PART, 1, 2),
}
HALVES = {
    RO1: (RIGHT, 0, 0, HALF_A, 0, -1),
    RO2: (RIGHT, 0, 0, HALF_B1, 0, -1),
    RO3: (RIGHT, 0, 0, HALF_B2, 0, -1),
    LO2: (LEFT, 0, 0, HALF_B, 0, 1),
    LO1: (LEFT, 0, 0, HALF_A1, 0, 1),
    LO3: (LEFT, 0, 0, HALF_A2, 0, 1),
    YO1: (ACROSS, 0, 0, HALF_A, 1, 0),
    YO2: (ACROSS, 0, 0, HALF_B, 1, 0),
    RX1: (RIGHT, 1, 0, HALF_A, 1, -1),
    RX2: (RIGHT, 1, 0, HALF_B, 1, -1),
    LX1: (LEFT, 1, 0, HALF_A, 1, 1),
    LX2: (LEFT, 1, 0, HALF_B, 1, 1),
    RA: (RIGHT, 0, -1, HALF_A, 0, 2),
    LB: (LEFT, 0, 1, HALF_B, 0, 2),
    RXA: (RIGHT, 1, -1, HALF_A, 1, 2),
    LXB: (LEFT, 1, 1, HALF_B, 1, 2),
}
NSEM = 2 * len(LEGS) + 1
NSEM_HALF = 2 * len(HALVES) + 1


def place():
    me = lax.axis_index("dp")
    return me, me // 8, (me % 8) // 2, me % 2


class Gather:
    def __init__(self, legs, piece, rows, p, qa, send, recv, give=None):
        self.legs, self.order = legs, list(legs)
        self.piece, self.send, self.recv, self.give = piece, send, recv, give
        self.me, self.y, self.z, self.c = place()
        half = rows // 2
        self.rows = {
            FULL: (0, rows),
            PART: (0, p),
            REST: (p, rows - p),
            HALF_A: (0, half),
            HALF_B: (half, rows - half),
            HALF_A1: (0, half // 2),
            HALF_A2: (half // 2, half - half // 2),
            HALF_B1: (half, half // 2),
            HALF_B2: (half + half // 2, half - half // 2),
            REST_A: (p, qa),
            REST_B: (p + qa, rows - p - qa),
        }

    def block(self, flip, dz, core):
        y = self.y + flip - 2 * flip * self.y
        return y * 8 + ((self.z + dz + 4) % 4) * 2 + core

    def target(self, name):
        if name == RIGHT:
            return self.block(0, 1, self.c)
        if name == LEFT:
            return self.block(0, -1, self.c)
        if name == ACROSS:
            return self.block(1, 0, self.c)
        return self.block(0, 0, 1 - self.c)

    def copy(self, src, ref, sem, to):
        return pltpu.make_async_remote_copy(
            src_ref=src,
            dst_ref=ref,
            send_sem=self.send.at[sem],
            recv_sem=self.recv.at[sem],
            device_id={"dp": to},
            device_id_type=MESH,
        )

    def leg(self, name):
        to, flip, dz, rows, _, _ = self.legs[name]
        ref = self.piece(self.block(flip, dz, self.c), *self.rows[rows])
        src = ref
        if to == ACROSS and self.give is not None:
            src = self.give(*self.rows[rows])
        return self.copy(src, ref, self.order.index(name), self.target(to))

    def landed(self, name):
        to, _, _, rows, flip, dz = self.legs[name]
        ref = self.piece(self.block(flip, dz, self.c), *self.rows[rows])
        return self.copy(ref, ref, self.order.index(name), self.target(to))

    def side(self, name, core):
        if name == OWN:
            flip, dz, rows, sem = 0, 0, FULL, len(self.order)
        else:
            _, _, _, rows, flip, dz = self.legs[name]
            sem = len(self.order) + 1 + self.order.index(name)
        ref = self.piece(self.block(flip, dz, core), *self.rows[rows])
        return self.copy(ref, ref, sem, self.target(SIDE))

    def begin(self, *names):
        for name in names:
            self.leg(name).start()
        self.side(OWN, self.c).start()

    def arrive(self, name, *then):
        self.landed(name).wait_recv()
        for other in then:
            self.leg(other).start()
        self.side(name, self.c).start()

    def side_arrive(self, *names):
        for name in names:
            self.side(name, 1 - self.c).wait_recv()

    def finish(self):
        for name in self.order:
            self.leg(name).wait_send()
        for name in [OWN] + self.order:
            self.side(name, self.c).wait_send()


def iota(axis):
    return lax.broadcasted_iota(jnp.int32, (T, T), axis)


def mm(a, b):
    return jnp.dot(a.astype(BF16), b.astype(BF16), preferred_element_type=F32)


def mm_t(a, b):
    return lax.dot_general(
        a.astype(BF16), b.astype(BF16), (((1,), (1,)), ((), ())), preferred_element_type=F32
    )


def softplus(v):
    return jnp.maximum(v, 0.0) + jnp.log1p(jnp.exp(-jnp.abs(v)))


def steps_of(raw, params):
    step = softplus(raw + params[0:1, :])
    lower = (iota(0) >= iota(1)).astype(F32)
    decay = jnp.dot(
        lower, -step * params[1:2, :], preferred_element_type=F32, precision=lax.Precision.HIGHEST
    )
    return step, decay, jnp.transpose(step), jnp.transpose(decay)


def head(k):
    return slice(k * 128, (k + 1) * 128)


class States:
    def __init__(self, own, sib, chips, result, out, send, recv, cross=None):
        self.cross = cross
        self.own, self.sib, self.chips, self.result, self.out = own, sib, chips, result, out
        self.send, self.recv = send, recv
        self.me, self.y, self.z, self.c = place()
        self.q = self.me // 2
        self.mine = pl.ds(pl.multiple_of(self.c * 256, 256), 256)
        self.rest = pl.ds(pl.multiple_of((1 - self.c) * 256, 256), 256)

    def copy(self, src, dst, sem, to):
        return pltpu.make_async_remote_copy(
            src_ref=src,
            dst_ref=dst,
            send_sem=self.send.at[sem],
            recv_sem=self.recv.at[sem],
            device_id={"dp": to},
            device_id_type=MESH,
        )

    def share(self):
        return self.copy(self.own.at[:, self.rest], self.sib, 0, self.q * 2 + 1 - self.c)

    def peer(self, k, landing=False):
        at = self.chips.at[(self.q + 8 - k) % 8 if landing else self.q]
        return self.copy(at, at, k, ((self.q + k) % 8) * 2 + self.c)

    def row_peer(self, k, landing=False):
        at = self.chips.at[self.y * 4 + (self.z + (4 - k if landing else 0)) % 4]
        return self.copy(at, at, k, self.y * 8 + ((self.z + k) % 4) * 2 + self.c)

    def over(self):
        return self.copy(self.cross.at[0], self.cross.at[1], 4, (1 - self.y) * 8 + self.me % 8)

    def hand(self, landing=False):
        lanes = self.rest if landing else self.mine
        return self.copy(self.result, self.out.at[:, lanes], 8, self.q * 2 + 1 - self.c)

    def wide(self, row):
        pick = [jnp.where(self.c == 0, row[:, i : i + 1], row[:, 2 + i : 3 + i]) for i in range(2)]
        lane = lax.broadcasted_iota(jnp.int32, (1, 256), 1)
        return jnp.where(lane < 128, pick[0], pick[1])

    def pair(self):
        mine, theirs = self.own[:, self.mine].astype(F32), self.sib[...].astype(F32)
        return jnp.where(self.c == 0, mine, theirs), jnp.where(self.c == 0, theirs, mine)

    def join(self, ends, forward):
        self.share().wait_recv()
        first, second = self.pair()
        if forward:
            total = self.wide(jnp.exp(ends[1])) * first + second
        else:
            total = first + self.wide(jnp.exp(ends[0])) * second
        self.chips[self.q] = total.astype(BF16)
        if forward:
            for k in (2, 1, 3):
                self.row_peer(k).start()
        else:
            for k in (4, 1, 7, 2, 6, 3, 5):
                self.peer(k).start()

    def solve(self, ends, weights, forward):
        total = jnp.zeros((128, 256), F32)
        if forward:
            for k in range(1, 4):
                self.row_peer(k, True).wait_recv()
            whole = jnp.zeros((128, 256), F32)
            for j in range(4):
                part = self.chips[self.y * 4 + j].astype(F32)
                total = total + self.wide(weights[j : j + 1, :]) * part
                whole = whole + self.wide(weights[4 + j : 5 + j, :]) * part
            self.cross[0] = whole.astype(BF16)
            self.over().start()
            self.over().wait_recv()
            before = self.wide(weights[8:9, :]) * self.cross[1].astype(F32)
            total = total + jnp.where(self.y == 1, before, 0.0)
        else:
            for k in range(1, 8):
                self.peer(k, True).wait_recv()
            for j in range(8):
                total = total + self.wide(weights[j : j + 1, :]) * self.chips[j].astype(F32)
        first, second = self.pair()
        if forward:
            near, far = total, self.wide(jnp.exp(ends[0])) * total + first
        else:
            near, far = second + self.wide(jnp.exp(ends[1])) * total, total
        self.result[...] = jnp.where(self.c == 0, far, near).astype(BF16)
        self.hand().start()
        self.out[:, self.mine] = jnp.where(self.c == 0, near, far).astype(BF16)

    def finish(self):
        self.share().wait_send()
        if self.cross is not None:
            for k in range(1, 4):
                self.row_peer(k).wait_send()
            self.over().wait_send()
        else:
            for k in range(1, 8):
                self.peer(k).wait_send()
        self.hand().wait_send()


def state_weights(decays, y, z, put):
    run_in, run_all = jnp.zeros((1, 128), F32), jnp.zeros((1, 128), F32)
    for j in reversed(range(4)):
        reached = (j < z).astype(F32)
        put[0, j : j + 1, :] = reached * jnp.exp(run_in)
        put[0, 4 + j : 5 + j, :] = jnp.exp(run_all)
        end = decays[(y * 4 + j) * 2, 0:1, :] + decays[(y * 4 + j) * 2 + 1, 0:1, :]
        run_in = run_in + reached * end
        run_all = run_all + end
    put[0, 8:9, :] = jnp.exp(run_in)
    run = jnp.zeros((1, 128), F32)
    for j in range(8):
        reached = (j > y * 4 + z).astype(F32)
        put[1, j : j + 1, :] = reached * jnp.exp(run)
        run = run + reached * (decays[2 * j, 0:1, :] + decays[2 * j + 1, 0:1, :])


def spread(scalars):
    lane = lax.broadcasted_iota(jnp.int32, (1, 128), 1)
    row = jnp.zeros((1, 128), F32)
    for h in range(HEADS):
        row = jnp.where(lane == h, scalars[h], row)
    return row


SCRATCH = dict(
    held=pltpu.VMEM((DP, ROWS, HID), BF16),
    give=pltpu.VMEM((ROWS, HID), BF16),
    v_wc=pltpu.VMEM((D, 512), BF16),
    v_wb=pltpu.VMEM((D, 128), BF16),
    v_wx=pltpu.VMEM((D, 128), BF16),
    v_wdt=pltpu.VMEM((HEADS, D), BF16),
    v_out=pltpu.VMEM((TP, 512, WIDTH), BF16),
    v_resid=pltpu.VMEM((T, WIDTH), BF16),
    nin=pltpu.VMEM((T, D), BF16),
    lhs=pltpu.VMEM((4 * T, D), BF16),
    acc=pltpu.VMEM((4 * T, HID), F32),
    proj=pltpu.VMEM((T, PACK), F32),
    read=pltpu.VMEM((T, WIDTH), BF16),
    state=pltpu.VMEM((128, WIDTH), BF16),
    sib=pltpu.VMEM((128, 256), BF16),
    chips=pltpu.VMEM((8, 128, 256), BF16),
    result=pltpu.VMEM((128, 256), BF16),
    decays=pltpu.VMEM((DP, 8, 128), F32),
    cross=pltpu.VMEM((2, 128, 256), BF16),
    weights=pltpu.VMEM((2, 16, 128), F32),
    steps=pltpu.VMEM((4, T, 128), F32),
    read_t=pltpu.VMEM((HEADS, 128, T), BF16),
    enter=pltpu.VMEM((128, WIDTH), BF16),
    through=pltpu.VMEM((T, WIDTH), F32),
    mixer_out=pltpu.VMEM((T, WIDTH), BF16),
    fade=pltpu.VMEM((HEADS, T, T), F32),
    plain=pltpu.VMEM((HEADS, T, T), F32),
    p_send=pltpu.VMEM((TP, T, WIDTH), BF16),
    p_recv=pltpu.VMEM((TP, T, WIDTH), BF16),
    str_a=pltpu.VMEM((4, 4, T // 2, WIDTH), BF16),
    str_b=pltpu.VMEM((4, 4, T // 2, WIDTH), BF16),
    mid_a=pltpu.VMEM((4, 4, T // 2, WIDTH), BF16),
    mid_b=pltpu.VMEM((4, 4, T // 2, WIDTH), BF16),
    got_a=pltpu.VMEM((3, 4, T // 2, WIDTH), BF16),
    got_b=pltpu.VMEM((3, 4, T // 2, WIDTH), BF16),
    sum_a=pltpu.VMEM((4, T // 2, WIDTH), BF16),
    sum_b=pltpu.VMEM((4, T // 2, WIDTH), BF16),
    end_a=pltpu.VMEM((3, T // 2, WIDTH), BF16),
    end_b=pltpu.VMEM((3, T // 2, WIDTH), BF16),
    gained=pltpu.VMEM((TP, T, WIDTH), BF16),
    grads=pltpu.VMEM((2 * T, HID), BF16),
    squares=pltpu.VMEM((2, T, 128), F32),
    out_grad=pltpu.VMEM((T, WIDTH), F32),
    along=pltpu.VMEM((T, WIDTH), F32),
    b_state=pltpu.VMEM((128, WIDTH), BF16),
    b_sib=pltpu.VMEM((128, 256), BF16),
    b_chips=pltpu.VMEM((8, 128, 256), BF16),
    b_result=pltpu.VMEM((128, 256), BF16),
    behind=pltpu.VMEM((128, WIDTH), BF16),
    packed=pltpu.VMEM((DP, T, PACK - WIDTH), BF16),
    read4=pltpu.VMEM((HEADS * T, 128), BF16),
    weight4=pltpu.VMEM((HEADS * T, T), BF16),
    grad4=pltpu.VMEM((HEADS * T, 128), BF16),
    dscore4=pltpu.VMEM((HEADS * T, T), BF16),
    across=pltpu.VMEM((HEADS, T, 128), F32),
    dinject=pltpu.VMEM((T, 128), F32),
    dvalue=pltpu.VMEM((T, 128), F32),
    in_sem=pltpu.SemaphoreType.DMA((11 + TP,)),
    g_send=pltpu.SemaphoreType.DMA((NSEM_HALF,)),
    g_recv=pltpu.SemaphoreType.DMA((NSEM_HALF,)),
    a_send=pltpu.SemaphoreType.DMA((1,)),
    a_recv=pltpu.SemaphoreType.DMA((1,)),
    h_send=pltpu.SemaphoreType.DMA((NSEM,)),
    h_recv=pltpu.SemaphoreType.DMA((NSEM,)),
    i_send=pltpu.SemaphoreType.DMA((NSEM,)),
    i_recv=pltpu.SemaphoreType.DMA((NSEM,)),
    s_send=pltpu.SemaphoreType.DMA((9,)),
    s_recv=pltpu.SemaphoreType.DMA((9,)),
    d_send=pltpu.SemaphoreType.DMA((DP - 1,)),
    d_recv=pltpu.SemaphoreType.DMA((DP - 1,)),
    b_send=pltpu.SemaphoreType.DMA((9,)),
    b_recv=pltpu.SemaphoreType.DMA((9,)),
    c_send=pltpu.SemaphoreType.DMA((DP - 1,)),
    c_recv=pltpu.SemaphoreType.DMA((DP - 1,)),
    t_send=pltpu.SemaphoreType.DMA((2, TP)),
    t_recv=pltpu.SemaphoreType.DMA((2, TP)),
    p1_send=pltpu.SemaphoreType.DMA((12,)),
    p1_recv=pltpu.SemaphoreType.DMA((12,)),
    p2_send=pltpu.SemaphoreType.DMA((12,)),
    p2_recv=pltpu.SemaphoreType.DMA((12,)),
)


def chunk(k, size=256):
    return pl.ds(pl.multiple_of(k * size, size), size)


def columns(p):
    return chunk(p, WIDTH)


def normalise(ref, rows, gain):
    total = jnp.zeros((T, 1), F32)
    for k in range(8):
        part = ref[rows, k * 512 : (k + 1) * 512].astype(F32)
        total = total + jnp.sum(part * part, axis=1, keepdims=True)
    scale = lax.rsqrt(total / D + EPS)
    for k in range(8):
        at = slice(k * 512, (k + 1) * 512)
        ref[rows, at] = (ref[rows, at].astype(F32) * scale * gain[:, at]).astype(BF16)


def whole_kernel(
    resid, teacher, gain_mix, gain_mlp, w_c, w_b, w_x, w_dt, bias, rate, skip, w_out, w_gate, w_up, out, *scratch
):
    s = SimpleNamespace(**dict(zip(SCRATCH, scratch)))
    me, y, z, c = place()
    m = me % 8
    t = lax.axis_index("tensor")
    other = (1 - y) * 8 + m
    half = HID // 2
    keep = pl.ds(pl.multiple_of(y * half, 128), half)
    rest = pl.ds(pl.multiple_of((1 - y) * half, 128), half)
    mine = pl.ds(pl.multiple_of(y * T, T), T)
    pairs = (
        (w_gate.at[:, keep], s.held.at[me, :, 0:half]),
        (w_up.at[:, keep], s.held.at[me, :, half:HID]),
        (w_gate.at[:, rest], s.give.at[:, 0:half]),
        (w_up.at[:, rest], s.give.at[:, half:HID]),
        (resid, s.nin),
        (w_c, s.v_wc),
        (w_b, s.v_wb),
        (w_x, s.v_wx),
        (w_dt, s.v_wdt),
        (teacher, s.lhs.at[mine, :]),
        (resid.at[:, columns(t)], s.v_resid),
    ) + tuple((w_out.at[:, p * WIDTH : (p + 1) * WIDTH], s.v_out.at[p]) for p in range(TP))
    loads = [pltpu.make_async_copy(a, b, s.in_sem.at[k]) for k, (a, b) in enumerate(pairs)]
    for copy in loads[0:5]:
        copy.start()
    sem = pltpu.get_barrier_semaphore()
    for k in range(1, DP):
        pl.semaphore_signal(sem, inc=1, device_id={"dp": (me + k) % DP}, device_id_type=MESH)
    for k in range(1, TP):
        for dp in (me, other):
            pl.semaphore_signal(
                sem, inc=1, device_id={"dp": dp, "tensor": (t + k) % TP}, device_id_type=MESH
            )
    pl.semaphore_wait(sem, DP - 1 + 2 * (TP - 1))
    for copy in loads[0:4]:
        copy.wait()
    gather = Gather(
        HALVES,
        lambda j, start, size: s.held.at[j, pl.ds(start, size), :],
        ROWS,
        112,
        64,
        s.g_send,
        s.g_recv,
        lambda start, size: s.give.at[pl.ds(start, size), :],
    )
    gather.begin(RO1, LO2, YO1)
    theirs = pl.ds(pl.multiple_of((1 - y) * T, T), T)

    def teacher_move(rows):
        return pltpu.make_async_remote_copy(
            src_ref=teacher,
            dst_ref=s.lhs.at[rows, :],
            send_sem=s.a_send.at[0],
            recv_sem=s.a_recv.at[0],
            device_id={"dp": other, "tensor": (t + 4) % TP},
            device_id_type=MESH,
        )

    teacher_move(mine).start()
    for copy in loads[5:]:
        copy.start()
    loads[4].wait()
    normalise(s.nin, slice(None), gain_mix)

    bias_row, rate_row, skip_row = spread(bias), spread(rate), spread(skip)
    params = jnp.concatenate([bias_row, rate_row, skip_row, jnp.zeros((5, 128), F32)], axis=0)
    for copy in loads[5:9]:
        copy.wait()
    rows = s.nin[...]
    s.proj[:, 0:512] = jnp.dot(rows, s.v_wc[...], preferred_element_type=F32)
    s.proj[:, 512:640] = jnp.dot(rows, s.v_wb[...], preferred_element_type=F32)
    s.proj[:, 640:768] = jnp.dot(rows, s.v_wx[...], preferred_element_type=F32)
    s.proj[:, 768:896] = jnp.zeros((T, 128), F32)
    s.proj[:, 768 : 768 + HEADS] = mm_t(rows, s.v_wdt[...])
    s.read[...] = s.proj[:, 0:512].astype(BF16)
    inject, values = s.proj[:, 512:640], s.proj[:, 640:768]
    raw = s.proj[:, 768:896]
    gather.leg(RO2).start()
    gather.leg(LO1).start()
    step, decay, step_t, decay_t = steps_of(raw, params)
    s.decays[me] = jnp.broadcast_to(decay[T - 1 : T, :], (8, 128))

    def ends_move(k):
        ref = s.decays.at[me]
        return pltpu.make_async_remote_copy(
            src_ref=ref,
            dst_ref=ref,
            send_sem=s.d_send.at[k - 1],
            recv_sem=s.d_recv.at[k - 1],
            device_id={"dp": (me + k) % DP},
            device_id_type=MESH,
        )

    def ends_landed(k):
        ref = s.decays.at[(me - k + DP) % DP]
        return pltpu.make_async_remote_copy(
            src_ref=ref,
            dst_ref=ref,
            send_sem=s.d_send.at[k - 1],
            recv_sem=s.d_recv.at[k - 1],
            device_id={"dp": (me + k) % DP},
            device_id_type=MESH,
        )

    for k in range(1, DP):
        ends_move(k).start()
    causal = iota(0) >= iota(1)
    inject_t = jnp.transpose(inject)
    for h in range(HEADS):
        s.read4[head(h), :] = s.read[:, head(h)]
    score = mm_t(s.read4[...], inject)
    pulls = []
    for h in range(HEADS):
        row, col, step_row = decay_t[h : h + 1, :], decay[:, h : h + 1], step_t[h : h + 1, :]
        s.fade[h] = jnp.exp(jnp.where(causal, col - row, -1e30))
        s.plain[h] = s.fade[h] * score[head(h), :]
        s.weight4[head(h), :] = (s.plain[h] * step_row).astype(BF16)
        pulls.append(inject_t * (jnp.exp(row[:, T - 1 : T] - row) * step_row))
    carried = mm(jnp.concatenate(pulls, axis=0), values)
    for h in range(HEADS):
        s.state[:, head(h)] = carried[head(h), :].astype(BF16)
    q = me // 2
    states = States(s.state, s.sib, s.chips, s.result, s.enter, s.s_send, s.s_recv, s.cross)
    states.share().start()
    through = mm(s.weight4[...], values)
    for h in range(HEADS):
        s.through[:, head(h)] = through[head(h), :] + skip_row[:, h : h + 1] * values
    for k, value in enumerate((step, decay, step_t, decay_t)):
        s.steps[k] = value
    ends_landed(jnp.where(c == 0, DP - 1, 1)).wait_recv()
    chip_ends = [s.decays[2 * q + i, 0:1, :] for i in range(2)]
    states.join(chip_ends, True)
    gather.leg(YO2).start()
    gather.leg(RO3).start()
    gather.leg(LO3).start()

    loads[9].wait()
    normalise(s.lhs, mine, gain_mlp)
    gather.arrive(RO1, RA)
    gather.arrive(LO2, LB)
    gather.arrive(YO1, RX1)

    for k in range(2, DP - 1):
        ends_landed(k).wait_recv()
    ends_landed(jnp.where(c == 0, 1, DP - 1)).wait_recv()
    state_weights(s.decays, y, z, s.weights)
    states.solve(chip_ends, s.weights[0], True)
    states.hand(True).wait_recv()
    for h in range(HEADS):
        grown = jnp.exp(decay[:, h : h + 1]) * mm(s.read[:, head(h)], s.enter[:, head(h)])
        s.mixer_out[:, head(h)] = (s.through[:, head(h)] + grown).astype(BF16)

    def move(phase, kt, src, dst):
        return pltpu.make_async_remote_copy(
            src_ref=src,
            dst_ref=dst,
            send_sem=s.t_send.at[phase, kt],
            recv_sem=s.t_recv.at[phase, kt],
            device_id={"tensor": (t + kt) % TP},
            device_id_type=MESH,
        )

    def out_move(kt):
        return move(0, kt, s.p_send.at[kt], s.p_recv.at[kt])

    def gained_move(kt):
        return move(1, kt, s.gained.at[t], s.gained.at[t])

    def gained_landed(kt):
        at = s.gained.at[(t - kt + TP) % TP]
        return move(1, kt, at, at)

    px, py = t % 4, (t // 4) * 2 + y

    def plane(sems, leg, over_x, k, src, dst):
        xx = (px + k) % 4 if over_x else px
        yy = py if over_x else (py + k) % 4
        return pltpu.make_async_remote_copy(
            src_ref=src,
            dst_ref=dst,
            send_sem=sems[0].at[3 * leg + k - 1],
            recv_sem=sems[1].at[3 * leg + k - 1],
            device_id={"dp": (yy % 2) * 8 + m, "tensor": (yy // 2) * 4 + xx},
            device_id_type=MESH,
        )

    def stream_leg(leg, k, landing=False):
        d = (4 - k) if landing else 0
        ref = (
            s.str_a.at[py, (px + d) % 4],
            s.str_b.at[px, (py + d) % 4],
            s.str_a.at[(py + d) % 4],
            s.str_b.at[(px + d) % 4],
        )[leg]
        return plane((s.p1_send, s.p1_recv), leg, leg in (0, 3), k, ref, ref)

    def mid_leg(leg, k):
        src, dst = (
            (s.mid_a.at[(px + k) % 4], s.got_a.at[k - 1]),
            (s.mid_b.at[(py + k) % 4], s.got_b.at[k - 1]),
            (s.sum_a.at[(py + k) % 4], s.end_a.at[k - 1]),
            (s.sum_b.at[(px + k) % 4], s.end_b.at[k - 1]),
        )[leg]
        return plane((s.p2_send, s.p2_recv), leg, leg in (0, 3), k, src, dst)

    def stream_block(yy, p):
        row, col = 2 * (p // 4) + yy, p % 4
        return jnp.concatenate([s.str_a[row, col], s.str_b[col, row]], axis=0)

    def out_part(p):
        return jnp.dot(s.mixer_out[...], s.v_out[p], preferred_element_type=F32)

    for copy in loads[10:]:
        copy.wait()

    def out_send(k, _):
        s.p_send[k] = out_part((t + k) % TP).astype(BF16)
        out_move(k).start()
        return 0

    lax.fori_loop(1, TP, out_send, 0)
    stream = out_part(t) + s.v_resid[...].astype(F32)
    gather.arrive(YO2, LX2, RX2, LX1)
    gather.arrive(RO2)
    gather.arrive(LO1)
    gather.arrive(RO3)
    gather.arrive(LO3)
    for k in range(1, TP):
        out_move(k).wait_recv()
        stream = stream + s.p_recv[k].astype(F32)
    half_rows = T // 2
    s.str_a[py, px] = stream[0:half_rows].astype(BF16)
    s.str_b[px, py] = stream[half_rows:T].astype(BF16)
    for k in (2, 1, 3):
        stream_leg(0, k).start()
        stream_leg(1, k).start()

    def column_copy(k):
        to = (k // 8 + y) % 2 * 8 + (m + k) % 8
        return pltpu.make_async_remote_copy(
            src_ref=s.v_wx.at[chunk(to), :],
            dst_ref=s.v_wb.at[chunk(me), :],
            send_sem=s.c_send.at[k - 1],
            recv_sem=s.c_recv.at[k - 1],
            device_id={"dp": to},
            device_id_type=MESH,
        )

    def column_landed(k):
        at = (k // 8 + y) % 2 * 8 + (m - k + DP) % 8
        return pltpu.make_async_remote_copy(
            src_ref=s.v_wx.at[chunk(at), :],
            dst_ref=s.v_wb.at[chunk(at), :],
            send_sem=s.c_send.at[k - 1],
            recv_sem=s.c_recv.at[k - 1],
            device_id={"dp": at},
            device_id_type=MESH,
        )

    near, far = range(1, 8), range(8, DP)

    upper_rows, lower_rows = pl.ds(0, 2 * T), pl.ds(2 * T, 2 * T)

    def use(flip, dz, rows=upper_rows):
        base = gather.block(flip, dz, 0)
        s.acc[rows, :] += jnp.dot(
            s.lhs[rows, chunk(base)], s.held[base], preferred_element_type=F32
        ) + jnp.dot(s.lhs[rows, chunk(base + 1)], s.held[base + 1], preferred_element_type=F32)

    def turn(k, _):
        s.v_wx[chunk(k), :] = jnp.transpose(s.nin[:, chunk(k)].astype(F32)).astype(BF16)
        return 0

    lax.fori_loop(0, DP, turn, 0)
    growth_t = jnp.exp(s.steps[3])
    for h in range(HEADS):
        s.read_t[h] = (jnp.transpose(s.read[:, head(h)].astype(F32)) * growth_t[h : h + 1, :]).astype(BF16)
    s.acc[...] = jnp.zeros_like(s.acc)
    gather.arrive(RX1, RXA)
    gather.arrive(LX2, LXB)
    teacher_move(theirs).wait_recv()
    normalise(s.lhs, theirs, gain_mlp)
    for k in (2, 1, 3):
        stream_leg(0, k, True).wait_recv()
    for k in (2, 1, 3):
        stream_leg(2, k).start()
    for k in (2, 1, 3):
        stream_leg(1, k, True).wait_recv()
    for k in (2, 1, 3):
        stream_leg(3, k).start()
    gather.arrive(RA)
    gather.arrive(LB)
    gather.side_arrive(OWN, YO1, YO2, RO1, RO2, RO3, LO1, LO2, LO3)

    def teach(i, _):
        use(jnp.where(i == 1, 1, 0), jnp.where(i < 2, 0, jnp.where(i == 2, 3, 1)))
        return 0

    lax.fori_loop(0, 4, teach, 0)
    gather.side_arrive(RA, LB)
    use(0, 2)
    gather.arrive(LX1)
    gather.arrive(RX2)
    gather.side_arrive(RX1, RX2)
    use(1, -1)
    gather.side_arrive(LX1, LX2)
    use(1, 1)

    for leg in (2, 3):
        for k in (2, 1, 3):
            stream_leg(leg, k, True).wait_recv()
    s.squares[...] = jnp.zeros_like(s.squares)

    def student_rows(p, _):
        for yy in range(2):
            part = stream_block(yy, p).astype(F32)
            s.squares[yy] += jnp.broadcast_to(jnp.sum(part * part, axis=1, keepdims=True), (T, 128))
            s.lhs[pl.ds((2 + yy) * T, T), columns(p)] = (part * gain_mlp[:, columns(p)]).astype(BF16)
        return 0

    lax.fori_loop(0, TP, student_rows, 0)

    def student(i, _):
        use(i % 2, jnp.where(i < 2, 0, jnp.where(i < 4, 3, jnp.where(i < 6, 1, 2))), lower_rows)
        return 0

    lax.fori_loop(0, 4, student, 0)
    gather.arrive(RXA)
    gather.arrive(LXB)
    lax.fori_loop(4, 7, student, 0)

    for k in far:
        column_copy(k).start()
    gather.side_arrive(RXA, LXB)
    use(1, 2, slice(None))
    scales = [lax.rsqrt(s.squares[yy, :, 0:1] / D + EPS) for yy in range(2)]
    scale = jnp.where(y == 0, scales[0], scales[1])
    both = jnp.concatenate(scales, axis=0)

    for n in range(half // 128):
        at, beside = slice(n * 128, (n + 1) * 128), slice(half + n * 128, half + (n + 1) * 128)
        aim_gate = s.acc[upper_rows, at]
        aim = aim_gate * jax.nn.sigmoid(aim_gate) * s.acc[upper_rows, beside]
        gate, up = s.acc[lower_rows, at] * both, s.acc[lower_rows, beside] * both
        sigma = jax.nn.sigmoid(gate)
        silu = gate * sigma
        grad = (2.0 / math.sqrt(FF)) * (silu * up - aim)
        s.grads[:, at] = (grad * up * sigma * (1.0 + gate * (1.0 - sigma))).astype(BF16)
        s.grads[:, beside] = (grad * silu).astype(BF16)

    def back(yh, xx):
        for i in range(2):
            part = mm_t(s.grads[...], s.held[2 * (yh * 4 + xx) + i]).astype(BF16)
            lanes_at = slice(i * 256, (i + 1) * 256)
            for yy in range(2):
                s.mid_a[xx, 2 * yh + yy, :, lanes_at] = part[yy * T : yy * T + half_rows, :]
                s.mid_b[2 * yh + yy, xx, :, lanes_at] = part[yy * T + half_rows : (yy + 1) * T, :]

    def back_far(xx, _):
        back(1 - t // 4, xx)
        return 0

    lax.fori_loop(0, 4, back_far, 0)
    mid_leg(1, 2).start()

    @pl.when(y == 0)
    def _():
        mid_leg(1, 3).start()

    @pl.when(y == 1)
    def _():
        mid_leg(1, 1).start()

    back(t // 4, (px + 2) % 4)
    mid_leg(0, 2).start()
    back(t // 4, (px + 1) % 4)
    mid_leg(0, 1).start()
    back(t // 4, (px + 3) % 4)
    mid_leg(0, 3).start()
    back(t // 4, px)

    @pl.when(y == 0)
    def _():
        mid_leg(1, 1).start()

    @pl.when(y == 1)
    def _():
        mid_leg(1, 3).start()

    for k in near:
        column_copy(k).start()
    s.v_wb[chunk(me), :] = s.v_wx[chunk(me), :]
    s.along[...] = jnp.zeros_like(s.along)

    def stream_part(p, _):
        s.along[...] += mm_t(stream_block(y, p), s.v_out[p])
        return 0

    lax.fori_loop(0, TP, stream_part, 0)

    def fold(own, got, sums):
        for at in range(4):
            total = own[at].astype(F32)
            for k in range(3):
                total = total + got[k, at].astype(F32)
            sums[at] = total.astype(BF16)

    for k in (2, 1, 3):
        mid_leg(0, k).wait_recv()
    fold(s.mid_a.at[px], s.got_a, s.sum_a)
    for k in (2, 1, 3):
        mid_leg(2, k).start()
    for k in (2, 1, 3):
        mid_leg(1, k).wait_recv()
    fold(s.mid_b.at[py], s.got_b, s.sum_b)
    for k in (2, 1, 3):
        mid_leg(3, k).start()
    parts = []
    for leg, own, ends_of in ((2, s.sum_a.at[py], s.end_a), (3, s.sum_b.at[px], s.end_b)):
        total = own[...].astype(F32)
        for k in (2, 1, 3):
            mid_leg(leg, k).wait_recv()
            total = total + ends_of[k - 1].astype(F32)
        parts.append(total)
    mid = jnp.concatenate(parts, axis=0)
    s.gained[t] = (mid * gain_mlp[:, columns(t)]).astype(BF16)
    for k in range(1, TP):
        gained_move(k).start()
    s.out_grad[...] = jnp.zeros_like(s.out_grad)

    def unproject(kt, inner):
        @pl.when(kt > 0)
        def _():
            gained_landed(kt).wait_recv()

        p = (t - kt + TP) % TP
        part = s.gained[p]
        s.out_grad[...] += mm_t(part, s.v_out[p])
        return inner + jnp.sum(part.astype(F32) * stream_block(y, p).astype(F32), axis=1, keepdims=True)

    inner = lax.fori_loop(0, TP, unproject, jnp.zeros((T, 1), F32))
    pull = scale * scale * scale * (inner / D)
    s.out_grad[...] = s.out_grad[...] * scale - s.along[...] * pull

    inject, values = s.proj[:, 512:640], s.proj[:, 640:768]
    raw = s.proj[:, 768:896]
    step, decay, step_t, decay_t = [s.steps[k] for k in range(4)]
    growth = jnp.exp(decay)
    for h in range(HEADS):
        s.b_state[:, head(h)] = mm(s.read_t[h], s.out_grad[:, head(h)]).astype(BF16)
    states_back = States(s.b_state, s.b_sib, s.b_chips, s.b_result, s.behind, s.b_send, s.b_recv)
    states_back.share().start()
    early = Gather(
        LEGS, lambda j, start, size: s.v_wc.at[pl.ds(pl.multiple_of(j * T + start, 16), size), :], T, 48, 48, s.h_send, s.h_recv
    )
    last = Gather(
        LEGS, lambda j, start, size: s.packed.at[j, pl.ds(start, size), :], T, 48, 48, s.i_send, s.i_recv
    )
    lanes = lax.broadcasted_iota(jnp.int32, (1, 128), 1)
    for h in range(HEADS):
        s.grad4[head(h), :] = s.out_grad[:, head(h)].astype(BF16)
    dweight = mm_t(s.grad4[...], values)
    for h in range(HEADS):
        s.dscore4[head(h), :] = (dweight[head(h), :] * s.fade[h] * step_t[h : h + 1, :]).astype(BF16)
        s.across[h] = growth[:, h : h + 1] * mm_t(s.grad4[head(h), :], s.enter[:, head(h)])
    inner_read = mm(s.dscore4[...], inject)
    chip_ends = [s.decays[2 * q + i, 0:1, :] for i in range(2)]
    states_back.join(chip_ends, False)
    for h in range(HEADS):
        s.v_wc[chunk(me, T), head(h)] = (inner_read[head(h), :] + s.across[h]).astype(BF16)
    early.begin(RO, LO, YO)
    step_rows, decay_rows, decay_cols = [], [], []
    skipped = jnp.zeros((T, 128), F32)
    for h in range(HEADS):
        step_row = step_t[h : h + 1, :]
        direct = dweight[head(h), :] * s.plain[h]
        skipped = skipped + skip_row[:, h : h + 1] * s.out_grad[:, head(h)]
        column = jnp.sum(direct, axis=0, keepdims=True)
        step_rows.append(column)
        decay_rows.append(-column * step_row)
        both_ways = direct * step_row + s.across[h] * s.read[:, head(h)].astype(F32)
        decay_cols.append(jnp.sum(both_ways, axis=1, keepdims=True))
    rows_dot = (((0,), (0,)), ((), ()))
    s.dinject[...] = lax.dot_general(s.dscore4[...], s.read4[...], rows_dot, preferred_element_type=F32)
    s.dvalue[...] = skipped + lax.dot_general(
        s.weight4[...], s.grad4[...], rows_dot, preferred_element_type=F32
    )
    states_back.solve(chip_ends, s.weights[1], False)
    early.arrive(YO, RQ, LQ)
    early.arrive(RO, RA, YL)
    early.arrive(LO, LB, YR)
    states_back.hand(True).wait_recv()
    dstep = jnp.zeros((T, 128), F32)
    ddecay = jnp.zeros((T, 128), F32)
    drawn_values = mm(inject, s.behind[...])
    dinject, dvalue = s.dinject[...], s.dvalue[...]
    final = (lax.broadcasted_iota(jnp.int32, (T, 1), 0) == T - 1).astype(F32)
    tails = jnp.exp(decay[T - 1 : T, :] - decay)
    for h in range(HEADS):
        tail_col = tails[:, h : h + 1]
        scaled_col = tail_col * step[:, h : h + 1]
        pulled = mm_t(values, s.behind[:, head(h)])
        dinject = dinject + scaled_col * pulled
        dvalue = dvalue + scaled_col * drawn_values[:, head(h)]
        drawn = tail_col * jnp.sum(inject * pulled, axis=1, keepdims=True)
        moved = drawn * step[:, h : h + 1]
        product = s.behind[:, head(h)].astype(F32) * s.enter[:, head(h)].astype(F32)
        kept = jnp.exp(decay[T - 1 : T, h : h + 1]) * jnp.sum(
            jnp.sum(product, axis=0, keepdims=True), axis=1, keepdims=True
        )
        end = kept + jnp.sum(moved, axis=0, keepdims=True)
        onehot = (lanes == h).astype(F32)
        dstep = dstep + drawn * onehot
        ddecay = ddecay + (decay_cols[h] - moved + final * end) * onehot
    s.packed[me, :, 0:128] = dinject.astype(BF16)
    s.packed[me, :, 128:256] = dvalue.astype(BF16)
    zero = jnp.zeros((128 - HEADS, 128), F32)
    dstep = dstep + jnp.transpose(jnp.concatenate(step_rows + [zero], axis=0))
    ddecay = ddecay + jnp.transpose(jnp.concatenate(decay_rows + [zero], axis=0))
    upper = (iota(0) <= iota(1)).astype(F32)
    later = jnp.dot(upper, ddecay, preferred_element_type=F32, precision=lax.Precision.HIGHEST)
    draw = (dstep - rate_row * later) * jax.nn.sigmoid(raw + bias_row)
    s.packed[me, :, 256:384] = draw.astype(BF16)

    last.begin(RO, LO, YO)
    out[...] = jnp.zeros_like(out)
    for k in range(1, DP):
        column_landed(k).wait_recv()

    def add(lanes_at, base, first, second):
        out[:, lanes_at] += jnp.dot(s.v_wb[chunk(base), :], first, preferred_element_type=F32) + jnp.dot(
            s.v_wb[chunk(base + 1), :], second, preferred_element_type=F32
        )

    def add_c(flip, dz):
        base = early.block(flip, dz, 0)
        add(slice(0, WIDTH), base, s.v_wc[chunk(base, T), :], s.v_wc[chunk(base + 1, T), :])

    def add_rest(flip, dz):
        base = last.block(flip, dz, 0)
        add(slice(WIDTH, PACK), base, s.packed[base], s.packed[base + 1])

    early.arrive(RQ, RQA)
    early.arrive(LQ, LQB)
    early.arrive(RA, YO2)
    early.arrive(LB)
    early.arrive(YL)
    early.arrive(YR)
    early.side_arrive(OWN)
    add_c(0, 0)
    early.side_arrive(YO)
    add_c(1, 0)
    last.arrive(YO, RQ, LQ)
    last.arrive(RO, RA, YL)
    last.arrive(LO, LB, YR)
    early.arrive(RQA)
    early.arrive(LQB)
    early.arrive(YO2)
    early.side_arrive(RO)
    add_c(0, -1)
    early.side_arrive(LO)
    add_c(0, 1)
    last.arrive(RQ, RQA)
    last.arrive(LQ, LQB)
    last.arrive(RA, YO2)
    last.arrive(LB)
    last.arrive(YL)
    last.arrive(YR)
    early.side_arrive(RA, LB)
    add_c(0, 2)
    early.side_arrive(RQ, YL)
    add_c(1, -1)
    early.side_arrive(LQ, YR)
    add_c(1, 1)
    early.side_arrive(RQA, LQB, YO2)
    add_c(1, 2)
    last.arrive(RQA)
    last.arrive(LQB)
    last.arrive(YO2)
    last.side_arrive(OWN)
    add_rest(0, 0)
    last.side_arrive(YO)
    add_rest(1, 0)
    last.side_arrive(RO)
    add_rest(0, -1)
    last.side_arrive(LO)
    add_rest(0, 1)
    last.side_arrive(RA, LB)
    add_rest(0, 2)
    last.side_arrive(RQ, YL)
    add_rest(1, -1)
    last.side_arrive(LQ, YR)
    add_rest(1, 1)
    last.side_arrive(RQA, LQB, YO2)
    add_rest(1, 2)

    gather.finish()
    early.finish()
    last.finish()
    states.finish()
    states_back.finish()
    for k in range(1, DP):
        ends_move(k).wait_send()
        column_copy(k).wait_send()
    teacher_move(mine).wait_send()
    for leg in range(4):
        for k in (1, 2, 3):
            stream_leg(leg, k).wait_send()
            mid_leg(leg, k).wait_send()
    for k in range(1, TP):
        out_move(k).wait_send()
        gained_move(k).wait_send()


def split_kernel(packed, grad_c, grad_b, grad_x, grad_dt):
    grad_c[...] = packed[:, 0:512]
    grad_b[...] = packed[:, 512:640]
    grad_x[...] = packed[:, 640:768]
    grad_dt[...] = jnp.transpose(packed[:, 768:896])[0:HEADS, :]


VM = pl.BlockSpec(memory_space=pltpu.VMEM)
SM = pl.BlockSpec(memory_space=pltpu.SMEM)
ANY = pl.BlockSpec(memory_space=pl.ANY)


def struct(shape, dtype):
    return jax.ShapeDtypeStruct(shape, dtype)


def local(
    resid, teacher_mixed, gain_mix, gain_mlp, w_c, w_b, w_x, w_dt, dt_bias, decay_rate, skip, w_out,
    w_gate, w_up,
):
    gain_mix, gain_mlp = gain_mix.reshape(1, D), gain_mlp.reshape(1, D)
    packed = pl.pallas_call(
        whole_kernel,
        out_shape=struct((ROWS, PACK), F32),
        in_specs=[ANY, ANY, VM, VM, ANY, ANY, ANY, ANY, SM, SM, SM, ANY, ANY, ANY],
        out_specs=VM,
        scratch_shapes=list(SCRATCH.values()),
        compiler_params=pltpu.CompilerParams(
            collective_id=0, has_side_effects=True, vmem_limit_bytes=63 * MIB
        ),
        name="whole",
    )(
        resid, teacher_mixed, gain_mix, gain_mlp, w_c, w_b, w_x, w_dt.T, dt_bias, decay_rate, skip, w_out,
        w_gate, w_up,
    )
    grad_c, grad_b, grad_x, grad_dt = pl.pallas_call(
        split_kernel,
        out_shape=(
            struct((ROWS, 512), F32),
            struct((ROWS, 128), F32),
            struct((ROWS, 128), F32),
            struct((HEADS, ROWS), F32),
        ),
        in_specs=[VM],
        out_specs=(VM,) * 4,
        name="split",
    )(packed)
    return grad_c, grad_b, grad_x, grad_dt.T


def solution(mesh):
    in_specs = (
        P("dp", None),
        P("dp", None),
        P(),
        P(),
        P(None, "tensor"),
        P(None, "tensor"),
        P(None, "tensor"),
        P(None, "tensor"),
        P("tensor"),
        P("tensor"),
        P("tensor"),
        P("tensor", None),
        P("dp", "tensor"),
        P("dp", "tensor"),
    )
    out_specs = (P("dp", "tensor"), P("dp", "tensor"), P("dp", "tensor"), P("dp", "tensor"))
    return jax.shard_map(local, mesh=mesh, in_specs=in_specs, out_specs=out_specs, check_vma=False)
```

```python
import math
from types import SimpleNamespace

import jax
import jax.numpy as jnp
from jax import lax
from jax.experimental import pallas as pl
from jax.experimental.pallas import tpu as pltpu
from jax.sharding import PartitionSpec as P

D = 4096
FF = 14336
EPS = 1e-05
T = 128
HEADS = 4
DP = 16
TP = 8
HID = 1792
ROWS = 256
WIDTH = 512
PACK = 896
F32 = jnp.float32
BF16 = jnp.bfloat16
MESH = pl.DeviceIdType.MESH
MIB = 1024 * 1024

RIGHT, LEFT, ACROSS, SIDE = range(4)
FULL, PART, REST, HALF_A, HALF_B, REST_A, REST_B, HALF_A1, HALF_A2, HALF_B1, HALF_B2 = range(11)
RO, LO, YO, RQ, LQ, RA, LB, YL, YR, RQA, LQB, YO2, RO1, RO2, RO3, LO1, LO2, LO3, YO1, RX1, RX2, LX1, LX2, RXA, LXB, OWN = range(26)

LEGS = {
    RO: (RIGHT, 0, 0, FULL, 0, -1),
    LO: (LEFT, 0, 0, FULL, 0, 1),
    YO: (ACROSS, 0, 0, FULL, 1, 0),
    RQ: (RIGHT, 1, 0, REST, 1, -1),
    LQ: (LEFT, 1, 0, REST, 1, 1),
    RA: (RIGHT, 0, -1, HALF_A, 0, 2),
    LB: (LEFT, 0, 1, HALF_B, 0, 2),
    YL: (ACROSS, 0, -1, PART, 1, -1),
    YR: (ACROSS, 0, 1, PART, 1, 1),
    RQA: (RIGHT, 1, -1, REST_A, 1, 2),
    LQB: (LEFT, 1, 1, REST_B, 1, 2),
    YO2: (ACROSS, 0, 2, PART, 1, 2),
}
HALVES = {
    RO1: (RIGHT, 0, 0, HALF_A, 0, -1),
    RO2: (RIGHT, 0, 0, HALF_B1, 0, -1),
    RO3: (RIGHT, 0, 0, HALF_B2, 0, -1),
    LO2: (LEFT, 0, 0, HALF_B, 0, 1),
    LO1: (LEFT, 0, 0, HALF_A1, 0, 1),
    LO3: (LEFT, 0, 0, HALF_A2, 0, 1),
    YO1: (ACROSS, 0, 0, HALF_A, 1, 0),
    YO2: (ACROSS, 0, 0, HALF_B, 1, 0),
    RX1: (RIGHT, 1, 0, HALF_A, 1, -1),
    RX2: (RIGHT, 1, 0, HALF_B, 1, -1),
    LX1: (LEFT, 1, 0, HALF_A, 1, 1),
    LX2: (LEFT, 1, 0, HALF_B, 1, 1),
    RA: (RIGHT, 0, -1, HALF_A, 0, 2),
    LB: (LEFT, 0, 1, HALF_B, 0, 2),
    RXA: (RIGHT, 1, -1, HALF_A, 1, 2),
    LXB: (LEFT, 1, 1, HALF_B, 1, 2),
}
NSEM = 2 * len(LEGS) + 1
NSEM_HALF = 2 * len(HALVES) + 1


def place():
    me = lax.axis_index("dp")
    return me, me // 8, (me % 8) // 2, me % 2


class Gather:
    def __init__(self, legs, piece, rows, p, qa, send, recv, give=None):
        self.legs, self.order = legs, list(legs)
        self.piece, self.send, self.recv, self.give = piece, send, recv, give
        self.me, self.y, self.z, self.c = place()
        half = rows // 2
        self.rows = {
            FULL: (0, rows),
            PART: (0, p),
            REST: (p, rows - p),
            HALF_A: (0, half),
            HALF_B: (half, rows - half),
            HALF_A1: (0, half // 2),
            HALF_A2: (half // 2, half - half // 2),
            HALF_B1: (half, half // 2),
            HALF_B2: (half + half // 2, half - half // 2),
            REST_A: (p, qa),
            REST_B: (p + qa, rows - p - qa),
        }

    def block(self, flip, dz, core):
        y = self.y + flip - 2 * flip * self.y
        return y * 8 + ((self.z + dz + 4) % 4) * 2 + core

    def target(self, name):
        if name == RIGHT:
            return self.block(0, 1, self.c)
        if name == LEFT:
            return self.block(0, -1, self.c)
        if name == ACROSS:
            return self.block(1, 0, self.c)
        return self.block(0, 0, 1 - self.c)

    def copy(self, src, ref, sem, to):
        return pltpu.make_async_remote_copy(
            src_ref=src,
            dst_ref=ref,
            send_sem=self.send.at[sem],
            recv_sem=self.recv.at[sem],
            device_id={"dp": to},
            device_id_type=MESH,
        )

    def leg(self, name):
        to, flip, dz, rows, _, _ = self.legs[name]
        ref = self.piece(self.block(flip, dz, self.c), *self.rows[rows])
        src = ref
        if to == ACROSS and self.give is not None:
            src = self.give(*self.rows[rows])
        return self.copy(src, ref, self.order.index(name), self.target(to))

    def landed(self, name):
        to, _, _, rows, flip, dz = self.legs[name]
        ref = self.piece(self.block(flip, dz, self.c), *self.rows[rows])
        return self.copy(ref, ref, self.order.index(name), self.target(to))

    def side(self, name, core):
        if name == OWN:
            flip, dz, rows, sem = 0, 0, FULL, len(self.order)
        else:
            _, _, _, rows, flip, dz = self.legs[name]
            sem = len(self.order) + 1 + self.order.index(name)
        ref = self.piece(self.block(flip, dz, core), *self.rows[rows])
        return self.copy(ref, ref, sem, self.target(SIDE))

    def begin(self, *names):
        for name in names:
            self.leg(name).start()
        self.side(OWN, self.c).start()

    def arrive(self, name, *then):
        self.landed(name).wait_recv()
        for other in then:
            self.leg(other).start()
        self.side(name, self.c).start()

    def side_arrive(self, *names):
        for name in names:
            self.side(name, 1 - self.c).wait_recv()

    def finish(self):
        for name in self.order:
            self.leg(name).wait_send()
        for name in [OWN] + self.order:
            self.side(name, self.c).wait_send()


def iota(axis):
    return lax.broadcasted_iota(jnp.int32, (T, T), axis)


def mm(a, b):
    return jnp.dot(a.astype(BF16), b.astype(BF16), preferred_element_type=F32)


def mm_t(a, b):
    return lax.dot_general(
        a.astype(BF16), b.astype(BF16), (((1,), (1,)), ((), ())), preferred_element_type=F32
    )


def softplus(v):
    return jnp.maximum(v, 0.0) + jnp.log1p(jnp.exp(-jnp.abs(v)))


def steps_of(raw, params):
    step = softplus(raw + params[0:1, :])
    lower = (iota(0) >= iota(1)).astype(F32)
    decay = jnp.dot(
        lower, -step * params[1:2, :], preferred_element_type=F32, precision=lax.Precision.HIGHEST
    )
    return step, decay, jnp.transpose(step), jnp.transpose(decay)


def head(k):
    return slice(k * 128, (k + 1) * 128)


class States:
    def __init__(self, own, sib, chips, result, out, send, recv, cross=None):
        self.cross = cross
        self.own, self.sib, self.chips, self.result, self.out = own, sib, chips, result, out
        self.send, self.recv = send, recv
        self.me, self.y, self.z, self.c = place()
        self.q = self.me // 2
        self.mine = pl.ds(pl.multiple_of(self.c * 256, 256), 256)
        self.rest = pl.ds(pl.multiple_of((1 - self.c) * 256, 256), 256)

    def copy(self, src, dst, sem, to):
        return pltpu.make_async_remote_copy(
            src_ref=src,
            dst_ref=dst,
            send_sem=self.send.at[sem],
            recv_sem=self.recv.at[sem],
            device_id={"dp": to},
            device_id_type=MESH,
        )

    def share(self):
        return self.copy(self.own.at[:, self.rest], self.sib, 0, self.q * 2 + 1 - self.c)

    def peer(self, k, landing=False):
        at = self.chips.at[(self.q + 8 - k) % 8 if landing else self.q]
        return self.copy(at, at, k, ((self.q + k) % 8) * 2 + self.c)

    def row_peer(self, k, landing=False):
        at = self.chips.at[self.y * 4 + (self.z + (4 - k if landing else 0)) % 4]
        return self.copy(at, at, k, self.y * 8 + ((self.z + k) % 4) * 2 + self.c)

    def over(self):
        return self.copy(self.cross.at[0], self.cross.at[1], 4, (1 - self.y) * 8 + self.me % 8)

    def hand(self, landing=False):
        lanes = self.rest if landing else self.mine
        return self.copy(self.result, self.out.at[:, lanes], 8, self.q * 2 + 1 - self.c)

    def wide(self, row):
        pick = [jnp.where(self.c == 0, row[:, i : i + 1], row[:, 2 + i : 3 + i]) for i in range(2)]
        lane = lax.broadcasted_iota(jnp.int32, (1, 256), 1)
        return jnp.where(lane < 128, pick[0], pick[1])

    def pair(self):
        mine, theirs = self.own[:, self.mine].astype(F32), self.sib[...].astype(F32)
        return jnp.where(self.c == 0, mine, theirs), jnp.where(self.c == 0, theirs, mine)

    def join(self, ends, forward):
        self.share().wait_recv()
        first, second = self.pair()
        if forward:
            total = self.wide(jnp.exp(ends[1])) * first + second
        else:
            total = first + self.wide(jnp.exp(ends[0])) * second
        self.chips[self.q] = total.astype(BF16)
        if forward:
            for k in (2, 1, 3):
                self.row_peer(k).start()
        else:
            for k in (4, 1, 7, 2, 6, 3, 5):
                self.peer(k).start()

    def solve(self, ends, weights, forward):
        total = jnp.zeros((128, 256), F32)
        if forward:
            for k in range(1, 4):
                self.row_peer(k, True).wait_recv()
            whole = jnp.zeros((128, 256), F32)
            for j in range(4):
                part = self.chips[self.y * 4 + j].astype(F32)
                total = total + self.wide(weights[j : j + 1, :]) * part
                whole = whole + self.wide(weights[4 + j : 5 + j, :]) * part
            self.cross[0] = whole.astype(BF16)
            self.over().start()
            self.over().wait_recv()
            before = self.wide(weights[8:9, :]) * self.cross[1].astype(F32)
            total = total + jnp.where(self.y == 1, before, 0.0)
        else:
            for k in range(1, 8):
                self.peer(k, True).wait_recv()
            for j in range(8):
                total = total + self.wide(weights[j : j + 1, :]) * self.chips[j].astype(F32)
        first, second = self.pair()
        if forward:
            near, far = total, self.wide(jnp.exp(ends[0])) * total + first
        else:
            near, far = second + self.wide(jnp.exp(ends[1])) * total, total
        self.result[...] = jnp.where(self.c == 0, far, near).astype(BF16)
        self.hand().start()
        self.out[:, self.mine] = jnp.where(self.c == 0, near, far).astype(BF16)

    def finish(self):
        self.share().wait_send()
        if self.cross is not None:
            for k in range(1, 4):
                self.row_peer(k).wait_send()
            self.over().wait_send()
        else:
            for k in range(1, 8):
                self.peer(k).wait_send()
        self.hand().wait_send()


def state_weights(decays, y, z, put):
    run_in, run_all = jnp.zeros((1, 128), F32), jnp.zeros((1, 128), F32)
    for j in reversed(range(4)):
        reached = (j < z).astype(F32)
        put[0, j : j + 1, :] = reached * jnp.exp(run_in)
        put[0, 4 + j : 5 + j, :] = jnp.exp(run_all)
        end = decays[(y * 4 + j) * 2, 0:1, :] + decays[(y * 4 + j) * 2 + 1, 0:1, :]
        run_in = run_in + reached * end
        run_all = run_all + end
    put[0, 8:9, :] = jnp.exp(run_in)
    run = jnp.zeros((1, 128), F32)
    for j in range(8):
        reached = (j > y * 4 + z).astype(F32)
        put[1, j : j + 1, :] = reached * jnp.exp(run)
        run = run + reached * (decays[2 * j, 0:1, :] + decays[2 * j + 1, 0:1, :])


def spread(scalars):
    lane = lax.broadcasted_iota(jnp.int32, (1, 128), 1)
    row = jnp.zeros((1, 128), F32)
    for h in range(HEADS):
        row = jnp.where(lane == h, scalars[h], row)
    return row


SCRATCH = dict(
    held=pltpu.VMEM((DP, ROWS, HID), BF16),
    give=pltpu.VMEM((ROWS, HID), BF16),
    v_wc=pltpu.VMEM((D, 512), BF16),
    v_wb=pltpu.VMEM((D, 128), BF16),
    v_wx=pltpu.VMEM((D, 128), BF16),
    v_wdt=pltpu.VMEM((HEADS, D), BF16),
    v_out=pltpu.VMEM((TP, 512, WIDTH), BF16),
    v_resid=pltpu.VMEM((T, WIDTH), BF16),
    nin=pltpu.VMEM((T, D), BF16),
    lhs=pltpu.VMEM((4 * T, D), BF16),
    acc=pltpu.VMEM((4 * T, HID), F32),
    proj=pltpu.VMEM((T, PACK), F32),
    read=pltpu.VMEM((T, WIDTH), BF16),
    state=pltpu.VMEM((128, WIDTH), BF16),
    sib=pltpu.VMEM((128, 256), BF16),
    chips=pltpu.VMEM((8, 128, 256), BF16),
    result=pltpu.VMEM((128, 256), BF16),
    decays=pltpu.VMEM((DP, 8, 128), F32),
    cross=pltpu.VMEM((2, 128, 256), BF16),
    weights=pltpu.VMEM((2, 16, 128), F32),
    steps=pltpu.VMEM((4, T, 128), F32),
    read_t=pltpu.VMEM((HEADS, 128, T), BF16),
    enter=pltpu.VMEM((128, WIDTH), BF16),
    through=pltpu.VMEM((T, WIDTH), F32),
    mixer_out=pltpu.VMEM((T, WIDTH), BF16),
    fade=pltpu.VMEM((HEADS, T, T), F32),
    plain=pltpu.VMEM((HEADS, T, T), F32),
    p_send=pltpu.VMEM((TP, T, WIDTH), BF16),
    p_recv=pltpu.VMEM((TP, T, WIDTH), BF16),
    str_a=pltpu.VMEM((4, 4, T // 2, WIDTH), BF16),
    str_b=pltpu.VMEM((4, 4, T // 2, WIDTH), BF16),
    mid_a=pltpu.VMEM((4, 4, T // 2, WIDTH), BF16),
    mid_b=pltpu.VMEM((4, 4, T // 2, WIDTH), BF16),
    got_a=pltpu.VMEM((3, 4, T // 2, WIDTH), BF16),
    got_b=pltpu.VMEM((3, 4, T // 2, WIDTH), BF16),
    sum_a=pltpu.VMEM((4, T // 2, WIDTH), BF16),
    sum_b=pltpu.VMEM((4, T // 2, WIDTH), BF16),
    end_a=pltpu.VMEM((3, T // 2, WIDTH), BF16),
    end_b=pltpu.VMEM((3, T // 2, WIDTH), BF16),
    gained=pltpu.VMEM((TP, T, WIDTH), BF16),
    grads=pltpu.VMEM((2 * T, HID), BF16),
    squares=pltpu.VMEM((2, T, 128), F32),
    out_grad=pltpu.VMEM((T, WIDTH), F32),
    along=pltpu.VMEM((T, WIDTH), F32),
    b_state=pltpu.VMEM((128, WIDTH), BF16),
    b_sib=pltpu.VMEM((128, 256), BF16),
    b_chips=pltpu.VMEM((8, 128, 256), BF16),
    b_result=pltpu.VMEM((128, 256), BF16),
    behind=pltpu.VMEM((128, WIDTH), BF16),
    packed=pltpu.VMEM((DP, T, PACK - WIDTH), BF16),
    read4=pltpu.VMEM((HEADS * T, 128), BF16),
    weight4=pltpu.VMEM((HEADS * T, T), BF16),
    grad4=pltpu.VMEM((HEADS * T, 128), BF16),
    dscore4=pltpu.VMEM((HEADS * T, T), BF16),
    across=pltpu.VMEM((HEADS, T, 128), F32),
    dinject=pltpu.VMEM((T, 128), F32),
    dvalue=pltpu.VMEM((T, 128), F32),
    in_sem=pltpu.SemaphoreType.DMA((11 + TP,)),
    g_send=pltpu.SemaphoreType.DMA((NSEM_HALF,)),
    g_recv=pltpu.SemaphoreType.DMA((NSEM_HALF,)),
    a_send=pltpu.SemaphoreType.DMA((1,)),
    a_recv=pltpu.SemaphoreType.DMA((1,)),
    h_send=pltpu.SemaphoreType.DMA((NSEM,)),
    h_recv=pltpu.SemaphoreType.DMA((NSEM,)),
    i_send=pltpu.SemaphoreType.DMA((NSEM,)),
    i_recv=pltpu.SemaphoreType.DMA((NSEM,)),
    s_send=pltpu.SemaphoreType.DMA((9,)),
    s_recv=pltpu.SemaphoreType.DMA((9,)),
    d_send=pltpu.SemaphoreType.DMA((DP - 1,)),
    d_recv=pltpu.SemaphoreType.DMA((DP - 1,)),
    b_send=pltpu.SemaphoreType.DMA((9,)),
    b_recv=pltpu.SemaphoreType.DMA((9,)),
    c_send=pltpu.SemaphoreType.DMA((DP - 1,)),
    c_recv=pltpu.SemaphoreType.DMA((DP - 1,)),
    t_send=pltpu.SemaphoreType.DMA((2, TP)),
    t_recv=pltpu.SemaphoreType.DMA((2, TP)),
    p1_send=pltpu.SemaphoreType.DMA((12,)),
    p1_recv=pltpu.SemaphoreType.DMA((12,)),
    p2_send=pltpu.SemaphoreType.DMA((12,)),
    p2_recv=pltpu.SemaphoreType.DMA((12,)),
)


def chunk(k, size=256):
    return pl.ds(pl.multiple_of(k * size, size), size)


def columns(p):
    return chunk(p, WIDTH)


def normalise(ref, rows, gain):
    total = jnp.zeros((T, 1), F32)
    for k in range(8):
        part = ref[rows, k * 512 : (k + 1) * 512].astype(F32)
        total = total + jnp.sum(part * part, axis=1, keepdims=True)
    scale = lax.rsqrt(total / D + EPS)
    for k in range(8):
        at = slice(k * 512, (k + 1) * 512)
        ref[rows, at] = (ref[rows, at].astype(F32) * scale * gain[:, at]).astype(BF16)


def whole_kernel(
    resid, teacher, gain_mix, gain_mlp, w_c, w_b, w_x, w_dt, bias, rate, skip, w_out, w_gate, w_up, out, *scratch
):
    s = SimpleNamespace(**dict(zip(SCRATCH, scratch)))
    me, y, z, c = place()
    m = me % 8
    t = lax.axis_index("tensor")
    other = (1 - y) * 8 + m
    half = HID // 2
    keep = pl.ds(pl.multiple_of(y * half, 128), half)
    rest = pl.ds(pl.multiple_of((1 - y) * half, 128), half)
    mine = pl.ds(pl.multiple_of(y * T, T), T)
    pairs = (
        (w_gate.at[:, keep], s.held.at[me, :, 0:half]),
        (w_up.at[:, keep], s.held.at[me, :, half:HID]),
        (w_gate.at[:, rest], s.give.at[:, 0:half]),
        (w_up.at[:, rest], s.give.at[:, half:HID]),
        (resid, s.nin),
        (w_c, s.v_wc),
        (w_b, s.v_wb),
        (w_x, s.v_wx),
        (w_dt, s.v_wdt),
        (teacher, s.lhs.at[mine, :]),
        (resid.at[:, columns(t)], s.v_resid),
    ) + tuple((w_out.at[:, p * WIDTH : (p + 1) * WIDTH], s.v_out.at[p]) for p in range(TP))
    loads = [pltpu.make_async_copy(a, b, s.in_sem.at[k]) for k, (a, b) in enumerate(pairs)]
    for copy in loads[0:5]:
        copy.start()
    sem = pltpu.get_barrier_semaphore()
    for k in range(1, DP):
        pl.semaphore_signal(sem, inc=1, device_id={"dp": (me + k) % DP}, device_id_type=MESH)
    for k in range(1, TP):
        for dp in (me, other):
            pl.semaphore_signal(
                sem, inc=1, device_id={"dp": dp, "tensor": (t + k) % TP}, device_id_type=MESH
            )
    pl.semaphore_wait(sem, DP - 1 + 2 * (TP - 1))
    for copy in loads[0:4]:
        copy.wait()
    gather = Gather(
        HALVES,
        lambda j, start, size: s.held.at[j, pl.ds(start, size), :],
        ROWS,
        112,
        64,
        s.g_send,
        s.g_recv,
        lambda start, size: s.give.at[pl.ds(start, size), :],
    )
    gather.begin(RO1, LO2, YO1)
    theirs = pl.ds(pl.multiple_of((1 - y) * T, T), T)

    def teacher_move(rows):
        return pltpu.make_async_remote_copy(
            src_ref=teacher,
            dst_ref=s.lhs.at[rows, :],
            send_sem=s.a_send.at[0],
            recv_sem=s.a_recv.at[0],
            device_id={"dp": other, "tensor": (t + 4) % TP},
            device_id_type=MESH,
        )

    teacher_move(mine).start()
    for copy in loads[5:]:
        copy.start()
    loads[4].wait()
    normalise(s.nin, slice(None), gain_mix)

    bias_row, rate_row, skip_row = spread(bias), spread(rate), spread(skip)
    params = jnp.concatenate([bias_row, rate_row, skip_row, jnp.zeros((5, 128), F32)], axis=0)
    for copy in loads[5:9]:
        copy.wait()
    rows = s.nin[...]
    s.proj[:, 0:512] = jnp.dot(rows, s.v_wc[...], preferred_element_type=F32)
    s.proj[:, 512:640] = jnp.dot(rows, s.v_wb[...], preferred_element_type=F32)
    s.proj[:, 640:768] = jnp.dot(rows, s.v_wx[...], preferred_element_type=F32)
    s.proj[:, 768:896] = jnp.zeros((T, 128), F32)
    s.proj[:, 768 : 768 + HEADS] = mm_t(rows, s.v_wdt[...])
    s.read[...] = s.proj[:, 0:512].astype(BF16)
    inject, values = s.proj[:, 512:640], s.proj[:, 640:768]
    raw = s.proj[:, 768:896]
    gather.leg(RO2).start()
    gather.leg(LO1).start()
    step, decay, step_t, decay_t = steps_of(raw, params)
    s.decays[me] = jnp.broadcast_to(decay[T - 1 : T, :], (8, 128))

    def ends_move(k):
        ref = s.decays.at[me]
        return pltpu.make_async_remote_copy(
            src_ref=ref,
            dst_ref=ref,
            send_sem=s.d_send.at[k - 1],
            recv_sem=s.d_recv.at[k - 1],
            device_id={"dp": (me + k) % DP},
            device_id_type=MESH,
        )

    def ends_landed(k):
        ref = s.decays.at[(me - k + DP) % DP]
        return pltpu.make_async_remote_copy(
            src_ref=ref,
            dst_ref=ref,
            send_sem=s.d_send.at[k - 1],
            recv_sem=s.d_recv.at[k - 1],
            device_id={"dp": (me + k) % DP},
            device_id_type=MESH,
        )

    for k in range(1, DP):
        ends_move(k).start()
    causal = iota(0) >= iota(1)
    inject_t = jnp.transpose(inject)
    for h in range(HEADS):
        s.read4[head(h), :] = s.read[:, head(h)]
    score = mm_t(s.read4[...], inject)
    pulls = []
    for h in range(HEADS):
        row, col, step_row = decay_t[h : h + 1, :], decay[:, h : h + 1], step_t[h : h + 1, :]
        s.fade[h] = jnp.exp(jnp.where(causal, col - row, -1e30))
        s.plain[h] = s.fade[h] * score[head(h), :]
        s.weight4[head(h), :] = (s.plain[h] * step_row).astype(BF16)
        pulls.append(inject_t * (jnp.exp(row[:, T - 1 : T] - row) * step_row))
    carried = mm(jnp.concatenate(pulls, axis=0), values)
    for h in range(HEADS):
        s.state[:, head(h)] = carried[head(h), :].astype(BF16)
    q = me // 2
    states = States(s.state, s.sib, s.chips, s.result, s.enter, s.s_send, s.s_recv, s.cross)
    states.share().start()
    through = mm(s.weight4[...], values)
    for h in range(HEADS):
        s.through[:, head(h)] = through[head(h), :] + skip_row[:, h : h + 1] * values
    for k, value in enumerate((step, decay, step_t, decay_t)):
        s.steps[k] = value
    ends_landed(jnp.where(c == 0, DP - 1, 1)).wait_recv()
    chip_ends = [s.decays[2 * q + i, 0:1, :] for i in range(2)]
    states.join(chip_ends, True)
    gather.leg(YO2).start()
    gather.leg(RO3).start()
    gather.leg(LO3).start()

    loads[9].wait()
    normalise(s.lhs, mine, gain_mlp)
    gather.arrive(RO1, RA)
    gather.arrive(LO2, LB)
    gather.arrive(YO1, RX1)

    for k in range(2, DP - 1):
        ends_landed(k).wait_recv()
    ends_landed(jnp.where(c == 0, 1, DP - 1)).wait_recv()
    state_weights(s.decays, y, z, s.weights)
    states.solve(chip_ends, s.weights[0], True)
    states.hand(True).wait_recv()
    for h in range(HEADS):
        grown = jnp.exp(decay[:, h : h + 1]) * mm(s.read[:, head(h)], s.enter[:, head(h)])
        s.mixer_out[:, head(h)] = (s.through[:, head(h)] + grown).astype(BF16)

    def move(phase, kt, src, dst):
        return pltpu.make_async_remote_copy(
            src_ref=src,
            dst_ref=dst,
            send_sem=s.t_send.at[phase, kt],
            recv_sem=s.t_recv.at[phase, kt],
            device_id={"tensor": (t + kt) % TP},
            device_id_type=MESH,
        )

    def out_move(kt):
        return move(0, kt, s.p_send.at[kt], s.p_recv.at[kt])

    def gained_move(kt):
        return move(1, kt, s.gained.at[t], s.gained.at[t])

    def gained_landed(kt):
        at = s.gained.at[(t - kt + TP) % TP]
        return move(1, kt, at, at)

    px, py = t % 4, (t // 4) * 2 + y

    def plane(sems, leg, over_x, k, src, dst):
        xx = (px + k) % 4 if over_x else px
        yy = py if over_x else (py + k) % 4
        return pltpu.make_async_remote_copy(
            src_ref=src,
            dst_ref=dst,
            send_sem=sems[0].at[3 * leg + k - 1],
            recv_sem=sems[1].at[3 * leg + k - 1],
            device_id={"dp": (yy % 2) * 8 + m, "tensor": (yy // 2) * 4 + xx},
            device_id_type=MESH,
        )

    def stream_leg(leg, k, landing=False):
        d = (4 - k) if landing else 0
        ref = (
            s.str_a.at[py, (px + d) % 4],
            s.str_b.at[px, (py + d) % 4],
            s.str_a.at[(py + d) % 4],
            s.str_b.at[(px + d) % 4],
        )[leg]
        return plane((s.p1_send, s.p1_recv), leg, leg in (0, 3), k, ref, ref)

    def mid_leg(leg, k):
        src, dst = (
            (s.mid_a.at[(px + k) % 4], s.got_a.at[k - 1]),
            (s.mid_b.at[(py + k) % 4], s.got_b.at[k - 1]),
            (s.sum_a.at[(py + k) % 4], s.end_a.at[k - 1]),
            (s.sum_b.at[(px + k) % 4], s.end_b.at[k - 1]),
        )[leg]
        return plane((s.p2_send, s.p2_recv), leg, leg in (0, 3), k, src, dst)

    def stream_block(yy, p):
        row, col = 2 * (p // 4) + yy, p % 4
        return jnp.concatenate([s.str_a[row, col], s.str_b[col, row]], axis=0)

    def out_part(p):
        return jnp.dot(s.mixer_out[...], s.v_out[p], preferred_element_type=F32)

    for copy in loads[10:]:
        copy.wait()

    def out_send(k, _):
        s.p_send[k] = out_part((t + k) % TP).astype(BF16)
        out_move(k).start()
        return 0

    lax.fori_loop(1, TP, out_send, 0)
    stream = out_part(t) + s.v_resid[...].astype(F32)
    gather.arrive(YO2, LX2, RX2, LX1)
    gather.arrive(RO2)
    gather.arrive(LO1)
    gather.arrive(RO3)
    gather.arrive(LO3)
    for k in range(1, TP):
        out_move(k).wait_recv()
        stream = stream + s.p_recv[k].astype(F32)
    half_rows = T // 2
    s.str_a[py, px] = stream[0:half_rows].astype(BF16)
    s.str_b[px, py] = stream[half_rows:T].astype(BF16)
    for k in (2, 1, 3):
        stream_leg(0, k).start()
        stream_leg(1, k).start()

    def column_copy(k):
        to = (k // 8 + y) % 2 * 8 + (m + k) % 8
        return pltpu.make_async_remote_copy(
            src_ref=s.v_wx.at[chunk(to), :],
            dst_ref=s.v_wb.at[chunk(me), :],
            send_sem=s.c_send.at[k - 1],
            recv_sem=s.c_recv.at[k - 1],
            device_id={"dp": to},
            device_id_type=MESH,
        )

    def column_landed(k):
        at = (k // 8 + y) % 2 * 8 + (m - k + DP) % 8
        return pltpu.make_async_remote_copy(
            src_ref=s.v_wx.at[chunk(at), :],
            dst_ref=s.v_wb.at[chunk(at), :],
            send_sem=s.c_send.at[k - 1],
            recv_sem=s.c_recv.at[k - 1],
            device_id={"dp": at},
            device_id_type=MESH,
        )

    near, far = range(1, 8), range(8, DP)

    upper_rows, lower_rows = pl.ds(0, 2 * T), pl.ds(2 * T, 2 * T)

    def use(flip, dz, rows=upper_rows):
        base = gather.block(flip, dz, 0)
        s.acc[rows, :] += jnp.dot(
            s.lhs[rows, chunk(base)], s.held[base], preferred_element_type=F32
        ) + jnp.dot(s.lhs[rows, chunk(base + 1)], s.held[base + 1], preferred_element_type=F32)

    def turn(k, _):
        s.v_wx[chunk(k), :] = jnp.transpose(s.nin[:, chunk(k)].astype(F32)).astype(BF16)
        return 0

    lax.fori_loop(0, DP, turn, 0)
    growth_t = jnp.exp(s.steps[3])
    for h in range(HEADS):
        s.read_t[h] = (jnp.transpose(s.read[:, head(h)].astype(F32)) * growth_t[h : h + 1, :]).astype(BF16)
    s.acc[...] = jnp.zeros_like(s.acc)
    gather.arrive(RX1, RXA)
    gather.arrive(LX2, LXB)
    teacher_move(theirs).wait_recv()
    normalise(s.lhs, theirs, gain_mlp)
    for k in (2, 1, 3):
        stream_leg(0, k, True).wait_recv()
    for k in (2, 1, 3):
        stream_leg(2, k).start()
    for k in (2, 1, 3):
        stream_leg(1, k, True).wait_recv()
    for k in (2, 1, 3):
        stream_leg(3, k).start()
    gather.arrive(RA)
    gather.arrive(LB)
    gather.side_arrive(OWN, YO1, YO2, RO1, RO2, RO3, LO1, LO2, LO3)

    def teach(i, _):
        use(jnp.where(i == 1, 1, 0), jnp.where(i < 2, 0, jnp.where(i == 2, 3, 1)))
        return 0

    lax.fori_loop(0, 4, teach, 0)
    gather.side_arrive(RA, LB)
    use(0, 2)
    gather.arrive(LX1)
    gather.arrive(RX2)
    gather.side_arrive(RX1, RX2)
    use(1, -1)
    gather.side_arrive(LX1, LX2)
    use(1, 1)

    for leg in (2, 3):
        for k in (2, 1, 3):
            stream_leg(leg, k, True).wait_recv()
    s.squares[...] = jnp.zeros_like(s.squares)

    def student_rows(p, _):
        for yy in range(2):
            part = stream_block(yy, p).astype(F32)
            s.squares[yy] += jnp.broadcast_to(jnp.sum(part * part, axis=1, keepdims=True), (T, 128))
            s.lhs[pl.ds((2 + yy) * T, T), columns(p)] = (part * gain_mlp[:, columns(p)]).astype(BF16)
        return 0

    lax.fori_loop(0, TP, student_rows, 0)

    def student(i, _):
        use(i % 2, jnp.where(i < 2, 0, jnp.where(i < 4, 3, jnp.where(i < 6, 1, 2))), lower_rows)
        return 0

    lax.fori_loop(0, 4, student, 0)
    gather.arrive(RXA)
    gather.arrive(LXB)
    lax.fori_loop(4, 7, student, 0)

    for k in far:
        column_copy(k).start()
    def use_one(block):
        s.acc[...] += jnp.dot(s.lhs[:, chunk(block)], s.held[block], preferred_element_type=F32)

    use_one(gather.block(1, 2, c))
    gather.side_arrive(RXA, LXB)
    use_one(gather.block(1, 2, 1 - c))
    scales = [lax.rsqrt(s.squares[yy, :, 0:1] / D + EPS) for yy in range(2)]
    scale = jnp.where(y == 0, scales[0], scales[1])
    both = jnp.concatenate(scales, axis=0)

    for n in range(half // 128):
        at, beside = slice(n * 128, (n + 1) * 128), slice(half + n * 128, half + (n + 1) * 128)
        aim_gate = s.acc[upper_rows, at]
        aim = aim_gate * jax.nn.sigmoid(aim_gate) * s.acc[upper_rows, beside]
        gate, up = s.acc[lower_rows, at] * both, s.acc[lower_rows, beside] * both
        sigma = jax.nn.sigmoid(gate)
        silu = gate * sigma
        grad = (2.0 / math.sqrt(FF)) * (silu * up - aim)
        s.grads[:, at] = (grad * up * sigma * (1.0 + gate * (1.0 - sigma))).astype(BF16)
        s.grads[:, beside] = (grad * silu).astype(BF16)

    def back(yh, xx):
        for i in range(2):
            part = mm_t(s.grads[...], s.held[2 * (yh * 4 + xx) + i]).astype(BF16)
            lanes_at = slice(i * 256, (i + 1) * 256)
            for yy in range(2):
                s.mid_a[xx, 2 * yh + yy, :, lanes_at] = part[yy * T : yy * T + half_rows, :]
                s.mid_b[2 * yh + yy, xx, :, lanes_at] = part[yy * T + half_rows : (yy + 1) * T, :]

    def back_far(xx, _):
        back(1 - t // 4, xx)
        return 0

    lax.fori_loop(0, 4, back_far, 0)
    mid_leg(1, 2).start()

    @pl.when(y == 0)
    def _():
        mid_leg(1, 3).start()

    @pl.when(y == 1)
    def _():
        mid_leg(1, 1).start()

    back(t // 4, (px + 2) % 4)
    mid_leg(0, 2).start()
    back(t // 4, (px + 1) % 4)
    mid_leg(0, 1).start()
    back(t // 4, (px + 3) % 4)
    mid_leg(0, 3).start()
    back(t // 4, px)

    @pl.when(y == 0)
    def _():
        mid_leg(1, 1).start()

    @pl.when(y == 1)
    def _():
        mid_leg(1, 3).start()

    for k in near:
        column_copy(k).start()
    s.v_wb[chunk(me), :] = s.v_wx[chunk(me), :]
    s.along[...] = jnp.zeros_like(s.along)

    def stream_part(p, _):
        s.along[...] += mm_t(stream_block(y, p), s.v_out[p])
        return 0

    lax.fori_loop(0, TP, stream_part, 0)

    def fold(own, got, sums):
        for at in range(4):
            total = own[at].astype(F32)
            for k in range(3):
                total = total + got[k, at].astype(F32)
            sums[at] = total.astype(BF16)

    for k in (2, 1, 3):
        mid_leg(0, k).wait_recv()
    fold(s.mid_a.at[px], s.got_a, s.sum_a)
    for k in (2, 1, 3):
        mid_leg(2, k).start()
    for k in (2, 1, 3):
        mid_leg(1, k).wait_recv()
    fold(s.mid_b.at[py], s.got_b, s.sum_b)
    for k in (2, 1, 3):
        mid_leg(3, k).start()
    parts = []
    for leg, own, ends_of in ((2, s.sum_a.at[py], s.end_a), (3, s.sum_b.at[px], s.end_b)):
        total = own[...].astype(F32)
        for k in (2, 1, 3):
            mid_leg(leg, k).wait_recv()
            total = total + ends_of[k - 1].astype(F32)
        parts.append(total)
    mid = jnp.concatenate(parts, axis=0)
    s.gained[t] = (mid * gain_mlp[:, columns(t)]).astype(BF16)
    for k in range(1, TP):
        gained_move(k).start()
    s.out_grad[...] = jnp.zeros_like(s.out_grad)

    def unproject(kt, inner):
        @pl.when(kt > 0)
        def _():
            gained_landed(kt).wait_recv()

        p = (t - kt + TP) % TP
        part = s.gained[p]
        s.out_grad[...] += mm_t(part, s.v_out[p])
        return inner + jnp.sum(part.astype(F32) * stream_block(y, p).astype(F32), axis=1, keepdims=True)

    inner = lax.fori_loop(0, TP, unproject, jnp.zeros((T, 1), F32))
    pull = scale * scale * scale * (inner / D)
    s.out_grad[...] = s.out_grad[...] * scale - s.along[...] * pull

    inject, values = s.proj[:, 512:640], s.proj[:, 640:768]
    raw = s.proj[:, 768:896]
    step, decay, step_t, decay_t = [s.steps[k] for k in range(4)]
    growth = jnp.exp(decay)
    for h in range(HEADS):
        s.b_state[:, head(h)] = mm(s.read_t[h], s.out_grad[:, head(h)]).astype(BF16)
    states_back = States(s.b_state, s.b_sib, s.b_chips, s.b_result, s.behind, s.b_send, s.b_recv)
    states_back.share().start()
    early = Gather(
        LEGS, lambda j, start, size: s.v_wc.at[pl.ds(pl.multiple_of(j * T + start, 16), size), :], T, 48, 48, s.h_send, s.h_recv
    )
    last = Gather(
        LEGS, lambda j, start, size: s.packed.at[j, pl.ds(start, size), :], T, 48, 48, s.i_send, s.i_recv
    )
    lanes = lax.broadcasted_iota(jnp.int32, (1, 128), 1)
    for h in range(HEADS):
        s.grad4[head(h), :] = s.out_grad[:, head(h)].astype(BF16)
    dweight = mm_t(s.grad4[...], values)
    for h in range(HEADS):
        s.dscore4[head(h), :] = (dweight[head(h), :] * s.fade[h] * step_t[h : h + 1, :]).astype(BF16)
        s.across[h] = growth[:, h : h + 1] * mm_t(s.grad4[head(h), :], s.enter[:, head(h)])
    inner_read = mm(s.dscore4[...], inject)
    chip_ends = [s.decays[2 * q + i, 0:1, :] for i in range(2)]
    states_back.join(chip_ends, False)
    for h in range(HEADS):
        s.v_wc[chunk(me, T), head(h)] = (inner_read[head(h), :] + s.across[h]).astype(BF16)
    early.begin(RO, LO, YO)
    step_rows, decay_rows, decay_cols = [], [], []
    skipped = jnp.zeros((T, 128), F32)
    for h in range(HEADS):
        step_row = step_t[h : h + 1, :]
        direct = dweight[head(h), :] * s.plain[h]
        skipped = skipped + skip_row[:, h : h + 1] * s.out_grad[:, head(h)]
        column = jnp.sum(direct, axis=0, keepdims=True)
        step_rows.append(column)
        decay_rows.append(-column * step_row)
        both_ways = direct * step_row + s.across[h] * s.read[:, head(h)].astype(F32)
        decay_cols.append(jnp.sum(both_ways, axis=1, keepdims=True))
    rows_dot = (((0,), (0,)), ((), ()))
    s.dinject[...] = lax.dot_general(s.dscore4[...], s.read4[...], rows_dot, preferred_element_type=F32)
    s.dvalue[...] = skipped + lax.dot_general(
        s.weight4[...], s.grad4[...], rows_dot, preferred_element_type=F32
    )
    states_back.solve(chip_ends, s.weights[1], False)
    early.arrive(YO, RQ, LQ)
    early.arrive(RO, RA, YL)
    early.arrive(LO, LB, YR)
    states_back.hand(True).wait_recv()
    dstep = jnp.zeros((T, 128), F32)
    ddecay = jnp.zeros((T, 128), F32)
    drawn_values = mm(inject, s.behind[...])
    dinject, dvalue = s.dinject[...], s.dvalue[...]
    final = (lax.broadcasted_iota(jnp.int32, (T, 1), 0) == T - 1).astype(F32)
    tails = jnp.exp(decay[T - 1 : T, :] - decay)
    for h in range(HEADS):
        tail_col = tails[:, h : h + 1]
        scaled_col = tail_col * step[:, h : h + 1]
        pulled = mm_t(values, s.behind[:, head(h)])
        dinject = dinject + scaled_col * pulled
        dvalue = dvalue + scaled_col * drawn_values[:, head(h)]
        drawn = tail_col * jnp.sum(inject * pulled, axis=1, keepdims=True)
        moved = drawn * step[:, h : h + 1]
        product = s.behind[:, head(h)].astype(F32) * s.enter[:, head(h)].astype(F32)
        kept = jnp.exp(decay[T - 1 : T, h : h + 1]) * jnp.sum(
            jnp.sum(product, axis=0, keepdims=True), axis=1, keepdims=True
        )
        end = kept + jnp.sum(moved, axis=0, keepdims=True)
        onehot = (lanes == h).astype(F32)
        dstep = dstep + drawn * onehot
        ddecay = ddecay + (decay_cols[h] - moved + final * end) * onehot
    s.packed[me, :, 0:128] = dinject.astype(BF16)
    s.packed[me, :, 128:256] = dvalue.astype(BF16)
    zero = jnp.zeros((128 - HEADS, 128), F32)
    dstep = dstep + jnp.transpose(jnp.concatenate(step_rows + [zero], axis=0))
    ddecay = ddecay + jnp.transpose(jnp.concatenate(decay_rows + [zero], axis=0))
    upper = (iota(0) <= iota(1)).astype(F32)
    later = jnp.dot(upper, ddecay, preferred_element_type=F32, precision=lax.Precision.HIGHEST)
    draw = (dstep - rate_row * later) * jax.nn.sigmoid(raw + bias_row)
    s.packed[me, :, 256:384] = draw.astype(BF16)

    last.begin(RO, LO, YO)
    out[...] = jnp.zeros_like(out)
    for k in range(1, DP):
        column_landed(k).wait_recv()

    def add(lanes_at, base, first, second):
        out[:, lanes_at] += jnp.dot(s.v_wb[chunk(base), :], first, preferred_element_type=F32) + jnp.dot(
            s.v_wb[chunk(base + 1), :], second, preferred_element_type=F32
        )

    def add_c(flip, dz):
        base = early.block(flip, dz, 0)
        add(slice(0, WIDTH), base, s.v_wc[chunk(base, T), :], s.v_wc[chunk(base + 1, T), :])

    def add_rest(flip, dz):
        base = last.block(flip, dz, 0)
        add(slice(WIDTH, PACK), base, s.packed[base], s.packed[base + 1])

    early.arrive(RQ, RQA)
    early.arrive(LQ, LQB)
    early.arrive(RA, YO2)
    early.arrive(LB)
    early.arrive(YL)
    early.arrive(YR)
    early.side_arrive(OWN)
    add_c(0, 0)
    early.side_arrive(YO)
    add_c(1, 0)
    last.arrive(YO, RQ, LQ)
    last.arrive(RO, RA, YL)
    last.arrive(LO, LB, YR)
    early.arrive(RQA)
    early.arrive(LQB)
    early.arrive(YO2)
    early.side_arrive(RO)
    add_c(0, -1)
    early.side_arrive(LO)
    add_c(0, 1)
    last.arrive(RQ, RQA)
    last.arrive(LQ, LQB)
    last.arrive(RA, YO2)
    last.arrive(LB)
    last.arrive(YL)
    last.arrive(YR)
    early.side_arrive(RA, LB)
    add_c(0, 2)
    early.side_arrive(RQ, YL)
    add_c(1, -1)
    early.side_arrive(LQ, YR)
    add_c(1, 1)
    early.side_arrive(RQA, LQB, YO2)
    add_c(1, 2)
    last.arrive(RQA)
    last.arrive(LQB)
    last.arrive(YO2)
    last.side_arrive(OWN)
    add_rest(0, 0)
    last.side_arrive(YO)
    add_rest(1, 0)
    last.side_arrive(RO)
    add_rest(0, -1)
    last.side_arrive(LO)
    add_rest(0, 1)
    last.side_arrive(RA, LB)
    add_rest(0, 2)
    last.side_arrive(RQ, YL)
    add_rest(1, -1)
    last.side_arrive(LQ, YR)
    add_rest(1, 1)
    last.side_arrive(RQA, LQB, YO2)
    add_rest(1, 2)

    gather.finish()
    early.finish()
    last.finish()
    states.finish()
    states_back.finish()
    for k in range(1, DP):
        ends_move(k).wait_send()
        column_copy(k).wait_send()
    teacher_move(mine).wait_send()
    for leg in range(4):
        for k in (1, 2, 3):
            stream_leg(leg, k).wait_send()
            mid_leg(leg, k).wait_send()
    for k in range(1, TP):
        out_move(k).wait_send()
        gained_move(k).wait_send()


def split_kernel(packed, grad_c, grad_b, grad_x, grad_dt):
    grad_c[...] = packed[:, 0:512]
    grad_b[...] = packed[:, 512:640]
    grad_x[...] = packed[:, 640:768]
    grad_dt[...] = jnp.transpose(packed[:, 768:896])[0:HEADS, :]


VM = pl.BlockSpec(memory_space=pltpu.VMEM)
SM = pl.BlockSpec(memory_space=pltpu.SMEM)
ANY = pl.BlockSpec(memory_space=pl.ANY)


def struct(shape, dtype):
    return jax.ShapeDtypeStruct(shape, dtype)


def local(
    resid, teacher_mixed, gain_mix, gain_mlp, w_c, w_b, w_x, w_dt, dt_bias, decay_rate, skip, w_out,
    w_gate, w_up,
):
    gain_mix, gain_mlp = gain_mix.reshape(1, D), gain_mlp.reshape(1, D)
    packed = pl.pallas_call(
        whole_kernel,
        out_shape=struct((ROWS, PACK), F32),
        in_specs=[ANY, ANY, VM, VM, ANY, ANY, ANY, ANY, SM, SM, SM, ANY, ANY, ANY],
        out_specs=VM,
        scratch_shapes=list(SCRATCH.values()),
        compiler_params=pltpu.CompilerParams(
            collective_id=0, has_side_effects=True, vmem_limit_bytes=63 * MIB
        ),
        name="whole",
    )(
        resid, teacher_mixed, gain_mix, gain_mlp, w_c, w_b, w_x, w_dt.T, dt_bias, decay_rate, skip, w_out,
        w_gate, w_up,
    )
    grad_c, grad_b, grad_x, grad_dt = pl.pallas_call(
        split_kernel,
        out_shape=(
            struct((ROWS, 512), F32),
            struct((ROWS, 128), F32),
            struct((ROWS, 128), F32),
            struct((HEADS, ROWS), F32),
        ),
        in_specs=[VM],
        out_specs=(VM,) * 4,
        name="split",
    )(packed)
    return grad_c, grad_b, grad_x, grad_dt.T


def solution(mesh):
    in_specs = (
        P("dp", None),
        P("dp", None),
        P(),
        P(),
        P(None, "tensor"),
        P(None, "tensor"),
        P(None, "tensor"),
        P(None, "tensor"),
        P("tensor"),
        P("tensor"),
        P("tensor"),
        P("tensor", None),
        P("dp", "tensor"),
        P("dp", "tensor"),
    )
    out_specs = (P("dp", "tensor"), P("dp", "tensor"), P("dp", "tensor"), P("dp", "tensor"))
    return jax.shard_map(local, mesh=mesh, in_specs=in_specs, out_specs=out_specs, check_vma=False)
```
